32 devices in a mesh: dp: 4 (over y, x), table: 8 (over z, core).
Axes of the slice: x: 2, y: 2, z: 4, core: 2. Of those that a mesh axis runs over, the one named last changes fastest.
Arguments:
- shard_of: int32 [256, 200, 3], P(('dp', 'table')), may hold values from 0 to 7, all different within a row; in each aligned block of 1600 rows (0 to 1599, 1600 to 3199, ..., all dimensions but the last counted through in order) at most 1200 rows name the same one
- offsets: int32 [256, 200, 3], P(('dp', 'table')), may hold values from 0 to 2047
- table: bfloat16 [3, 16384, 256], P(None, 'table'), may hold values from -4 to 4
- weight_one: bfloat16 [768, 256], replicated, may hold values from -0.21875 to 0.21875
- gain_one: float32 [256], replicated, may hold values from 0.5 to 1.5
- weight_two: bfloat16 [768, 256], replicated, may hold values from -0.21875 to 0.21875
- gain_two: float32 [256], replicated, may hold values from 0.5 to 1.5
- grad_out: bfloat16 [256, 200, 256], P(('dp', 'table')), may hold values from -6 to 6
Outputs:
- block_out: bfloat16 [256, 200, 256], P(('dp', 'table'))
- grad_weight_one: float32 [768, 256], replicated
- grad_weight_two: float32 [768, 256], replicated
- grad_gain_one: float32 [256], replicated
- grad_gain_two: float32 [256], replicated
- table_grad: float32 [3, 16384, 256], P(None, 'table', 'dp')
The draws below stay inside these ranges and needn't reach their ends.
Inputs may be any that keep to these rules, and one draw needn't show every extreme that they name: `shard_of`: the three lookups of one item go to three different shards; at most 1200 lookups of the items of one device go to one shard, and exactly 1200 for some shard of some device.
All inputs are finite; a program needn't handle non-finite values.
Results may differ from the reference program's by a relative error of at most 0.017.
Values may be sent and summed in bfloat16 or wider, within the bound.
No kernel may reach another device: no remote copies, remote signals or barrier semaphores. Data moves between devices by JAX's collectives and lax.ppermute only.
A program may use at most 128 MiB of HBM per device.

```python
import math
import jax
import jax.numpy as jnp
import numpy as np
from jax import lax

D = 256
LEN = 200
ROWS_DEV = 2048
SESS_DEV = 8
ITEMS_DEV = 1600
CAP = 1200
SESS = 256
HROWS = 16384
N_TABLE = 8


def touch_ends(values, key, low, high):
    longest = values.shape.index(max(values.shape))
    spots = []
    for shift in (0, 1):
        where = [jax.random.randint(jax.random.fold_in(key, axis), (), 0, length) for axis, length in enumerate(values.shape)]
        where[longest] = (where[longest] + shift) % values.shape[longest]
        spots.append(tuple(where))
    return values.at[spots[0]].set(low).at[spots[1]].set(high)


def block_levels(stream_key, shape, pieces, least, largest):
    factor_of, own = 1.0, jax.random.fold_in(stream_key, 6)
    for axis_at, blocks in pieces:
        steps = jnp.exp(jax.random.uniform(jax.random.fold_in(own, axis_at), (blocks,), jnp.float32, least / len(pieces), largest / len(pieces)))
        factor_of = factor_of * jnp.repeat(steps, shape[axis_at] // blocks).reshape([-1 if axis == axis_at else 1 for axis in range(len(shape))])
    return factor_of


def deal_out(rng, own, number, rows, number_of, top, most, skew):
    ranking = jax.random.permutation(rng, number_of)
    crowded, common = load_shares(number_of, rows * top, most, skew, True), load_shares(number_of, rows * top, most, skew, False)
    places = jnp.arange(number_of)

    def named(sizes, offset_by):
        used = int((sizes > 0).sum())
        fixed = max(1, used // 4)
        moved = fixed + (places - fixed + offset_by * (used - fixed)) % max(1, number_of - fixed)
        return jnp.zeros((number_of,), jnp.int32).at[ranking[jnp.where(places < fixed, places, moved)]].set(jnp.asarray(sizes, jnp.int32))

    sizes = jnp.where(number % 4 == 0, named(crowded, number // 4), named(common, number - number // 4 - 1))
    mixed = jax.random.permutation(jax.random.fold_in(own, 3), number_of)
    donor, sink = mixed[0:number_of // 2 * 2:2], mixed[1:number_of // 2 * 2:2]
    room = jnp.minimum(sizes[donor] - 1, most - sizes[sink]) // 2
    room = jnp.where((donor == ranking[0]) | (sink == ranking[0]) | (sizes[sink] == 0), 0, jnp.maximum(room, 0))
    moved = jax.random.randint(jax.random.fold_in(own, 4), (number_of // 2,), 0, 1 << 20) % (room + 1)
    sizes = sizes.at[donor].add(-moved).at[sink].add(moved)
    items = jnp.searchsorted(jnp.cumsum(sizes), jnp.arange(rows * top), side="right").astype(jnp.int32)
    listing = items.reshape(top, rows).T
    listing = listing[jax.random.permutation(jax.random.fold_in(own, 1), rows)]
    offset_by = jax.random.randint(jax.random.fold_in(own, 2), (rows, 1), 0, top)
    return jnp.take_along_axis(listing, (jnp.arange(top)[None, :] + offset_by) % top, axis=1)


def load_shares(count, total, reach, skew, full):
    portions = [(1 << 20) // math.isqrt(standing ** skew) + 1 for standing in range(1, count + 1)]
    largest = reach if full else min(reach, max(-(-total // count), total * portions[0] // sum(portions)))
    least = 1 if total - largest >= count - 1 else 0
    holding, surplus = [largest] + [least] * (count - 1), total - largest - least * (count - 1)
    while surplus > 0:
        movable = [i for i in range(1, count) if holding[i] < largest] or [i for i in range(1, count) if holding[i] < reach]
        mass, remaining = sum([portions[i] for i in movable]), surplus
        for i in movable:
            extra = min(reach - holding[i], max(1, remaining * portions[i] // mass), surplus)
            holding[i] = holding[i] + extra
            surplus = surplus - extra
    return np.array(holding)


def normal_values(rng, shape, spread, bound, shards=(), held_as=jnp.bfloat16):
    level = block_levels(rng, shape, shards, -0.22, 0.18) if shards else 1.0
    drawn = jax.random.normal(rng, shape, jnp.float32) * spread * level
    return jnp.minimum(jnp.maximum(drawn, -bound), bound).astype(held_as)


def setup_inputs(seed: int = 0) -> dict:
    key_of = jax.random.split(jax.random.key(seed), 9)
    shard_of_keys = jax.random.split(jax.random.fold_in(key_of[0], 1), SESS * LEN // ITEMS_DEV)
    shard_of_turns = jax.random.permutation(jax.random.fold_in(key_of[0], 3), SESS * LEN // ITEMS_DEV)
    shard_of = jax.vmap(lambda own, number: deal_out(jax.random.fold_in(key_of[0], 2), own, number, ITEMS_DEV, N_TABLE, 3, CAP, 2))(shard_of_keys, shard_of_turns).reshape((SESS, LEN, 3))
    offsets = touch_ends(jax.random.randint(key_of[1], (SESS, LEN, 3), 0, ROWS_DEV), jax.random.fold_in(key_of[1], 1), 0, ROWS_DEV - 1).astype(jnp.int32)
    table = normal_values(key_of[2], (3, HROWS, D), 0.6, 4.0, ((1, 8),))
    weight_one = normal_values(key_of[3], (3 * D, D), (3 * D) ** -0.5, 0.21875)
    gain_one = jnp.clip(1.0 + 0.1 * jax.random.normal(key_of[4], (D,), jnp.float32), 0.5, 1.5)
    weight_two = normal_values(key_of[5], (3 * D, D), (3 * D) ** -0.5, 0.21875)
    gain_two = jnp.clip(1.0 + 0.1 * jax.random.normal(key_of[6], (D,), jnp.float32), 0.5, 1.5)
    grad_out = normal_values(key_of[7], (SESS, LEN, D), 1.0, 6.0, ((0, 32),))
    return {"shard_of": shard_of, "offsets": offsets, "table": table, "weight_one": weight_one, "gain_one": gain_one, "weight_two": weight_two, "gain_two": gain_two, "grad_out": grad_out}


GELU_C = 0.7978845608028654
GELU_K = 0.044715

def shifted(values, spacing):
    return jnp.pad(values, ((0, 0), (spacing, 0), (0, 0)))[:, :values.shape[1], :]

def unshifted(values, spacing):
    return jnp.pad(values, ((0, 0), (0, spacing), (0, 0)))[:, spacing:, :]

def stack_taps(values, spacing):
    return jnp.concatenate([values, shifted(values, spacing), shifted(values, 2 * spacing)], axis=-1)

def gelu_parts(inputs):
    inner = GELU_C * (inputs + GELU_K * inputs * inputs * inputs)
    tangent = jnp.tanh(inner)
    output = 0.5 * inputs * (1.0 + tangent)
    slope = 0.5 * (1.0 + tangent) + 0.5 * inputs * (1.0 - tangent * tangent) * GELU_C * (1.0 + 3.0 * GELU_K * inputs * inputs)
    return (output, slope)

def layer_forward(values, weight, gain, spacing):
    sessions, length, width = values.shape
    stacked = stack_taps(values, spacing).reshape(sessions * length, 3 * width)
    before_norm = jnp.dot(stacked, weight, preferred_element_type=jnp.float32)
    centred = before_norm - lax.optimization_barrier(jnp.mean(before_norm, axis=-1, keepdims=True))
    inv_std = lax.rsqrt(lax.optimization_barrier(jnp.mean(centred * centred, axis=-1, keepdims=True)) + 1e-05)
    normal = centred * inv_std
    output, slope = gelu_parts(normal * gain)
    return (output, (stacked, normal, inv_std, slope))

def layer_backward(grad_output, weight, gain, saved, spacing, sessions, length):
    stacked, normal, inv_std, slope = saved
    width = weight.shape[1]
    grad_scaled = grad_output * slope
    grad_gain = lax.optimization_barrier(jnp.sum(grad_scaled * normal, axis=0))
    grad_normal = grad_scaled * gain
    grad_before = inv_std * (grad_normal - lax.optimization_barrier(jnp.mean(grad_normal, axis=-1, keepdims=True)) - normal * lax.optimization_barrier(jnp.mean(grad_normal * normal, axis=-1, keepdims=True)))
    grad_before = grad_before.astype(jnp.bfloat16)
    grad_weight = lax.dot_general(stacked, grad_before, (((0,), (0,)), ((), ())), preferred_element_type=jnp.float32)
    grad_taps = lax.dot_general(grad_before, weight, (((1,), (1,)), ((), ())), preferred_element_type=jnp.float32).reshape(sessions, length, 3 * width)
    grad_input = grad_taps[..., :width] + unshifted(grad_taps[..., width:2 * width], spacing) + unshifted(grad_taps[..., 2 * width:], 2 * spacing)
    return (grad_input, grad_weight, grad_gain)

def block_pass(embedded, weight_one, gain_one, weight_two, gain_two, grad_out):
    sessions, length, width = embedded.shape
    item_count = sessions * length
    act_one, saved_one = layer_forward(embedded, weight_one, gain_one, 1)
    hidden = act_one.astype(jnp.bfloat16).reshape(sessions, length, width)
    act_two, saved_two = layer_forward(hidden, weight_two, gain_two, 2)
    block_out = (embedded.reshape(item_count, width).astype(jnp.float32) + act_two).astype(jnp.bfloat16)
    grad_top = grad_out.reshape(item_count, width).astype(jnp.float32)
    grad_hidden, second_weights, second_gains = layer_backward(grad_top, weight_two, gain_two, saved_two, 2, sessions, length)
    grad_inner, first_weights, first_gains = layer_backward(grad_hidden.reshape(item_count, width), weight_one, gain_one, saved_one, 1, sessions, length)
    grad_embed = (grad_top + grad_inner.reshape(item_count, width)).astype(jnp.bfloat16)
    return (block_out, grad_embed, first_weights, second_weights, first_gains, second_gains)

def reference(shard_of, offsets, table, weight_one, gain_one, weight_two, gain_two, grad_out):
    global_rows = (shard_of * ROWS_DEV + offsets).astype(jnp.int32)
    block_count = SESS // SESS_DEV
    rows_blocks = global_rows.reshape(block_count, SESS_DEV, LEN, 3)
    grad_blocks = grad_out.reshape(block_count, SESS_DEV, LEN, D)
    picker = jnp.arange(3, dtype=jnp.int32)[None, None, :]

    def one_block(carry, inputs):
        rows_here, grad_here = inputs
        looked = table[picker, rows_here]
        embedded = lax.optimization_barrier(jnp.sum(looked.astype(jnp.float32), axis=2)).astype(jnp.bfloat16)
        block_out, grad_embed, first_weights, second_weights, first_gains, second_gains = block_pass(embedded, weight_one, gain_one, weight_two, gain_two, grad_here)
        new_carry = (carry[0] + first_weights, carry[1] + second_weights, carry[2] + first_gains, carry[3] + second_gains)
        return (new_carry, (block_out.reshape(SESS_DEV, LEN, D), grad_embed.reshape(SESS_DEV, LEN, D)))
    start = (jnp.zeros((3 * D, D), jnp.float32), jnp.zeros((3 * D, D), jnp.float32), jnp.zeros((D,), jnp.float32), jnp.zeros((D,), jnp.float32))
    totals, (outputs, grads) = lax.scan(one_block, start, (rows_blocks, grad_blocks))
    scale = 1.0 / math.sqrt(SESS * LEN)
    flat_rows = global_rows.reshape(SESS * LEN, 3)
    flat_grads = grads.reshape(SESS * LEN, D).astype(jnp.float32)
    table_grad = jnp.zeros((3, HROWS, D), jnp.float32)
    for column in range(3):
        table_grad = table_grad.at[column, flat_rows[:, column]].add(flat_grads)
    return (outputs.reshape(SESS, LEN, D), totals[0] * scale, totals[1] * scale, totals[2] * scale, totals[3] * scale, table_grad)
```

```python
import math

import jax
import jax.numpy as jnp
from jax import lax
from jax.experimental import pallas as pl
from jax.experimental.pallas import tpu as pltpu
from jax.sharding import PartitionSpec as P

GELU_C = 0.7978845608028654
GELU_K = 0.044715
LANES = 128
MIB = 2**20
CHAINS = 4
UNROLL = 4


def shifted(values, spacing):
    return jnp.pad(values, ((0, 0), (spacing, 0), (0, 0)))[:, : values.shape[1], :]


def unshifted(values, spacing):
    return jnp.pad(values, ((0, 0), (0, spacing), (0, 0)))[:, spacing:, :]


def stack_taps(values, spacing):
    return jnp.concatenate(
        [values, shifted(values, spacing), shifted(values, 2 * spacing)], axis=-1
    )


def gelu_parts(inputs):
    inner = GELU_C * (inputs + GELU_K * inputs * inputs * inputs)
    tangent = jnp.tanh(inner)
    output = 0.5 * inputs * (1.0 + tangent)
    slope = 0.5 * (1.0 + tangent) + 0.5 * inputs * (1.0 - tangent * tangent) * GELU_C * (
        1.0 + 3.0 * GELU_K * inputs * inputs
    )
    return (output, slope)


def layer_forward(values, weight, gain, spacing):
    sessions, length, width = values.shape
    stacked = stack_taps(values, spacing).reshape(sessions * length, 3 * width)
    before_norm = jnp.dot(stacked, weight, preferred_element_type=jnp.float32)
    centred = before_norm - jnp.mean(before_norm, axis=-1, keepdims=True)
    inv_std = lax.rsqrt(jnp.mean(centred * centred, axis=-1, keepdims=True) + 1e-05)
    normal = centred * inv_std
    output, slope = gelu_parts(normal * gain)
    return (output, (stacked, normal, inv_std, slope))


def layer_backward(grad_output, weight, gain, saved, spacing, sessions, length):
    stacked, normal, inv_std, slope = saved
    width = weight.shape[1]
    grad_scaled = grad_output * slope
    grad_gain = jnp.sum(grad_scaled * normal, axis=0)
    grad_normal = grad_scaled * gain
    grad_before = inv_std * (
        grad_normal
        - jnp.mean(grad_normal, axis=-1, keepdims=True)
        - normal * jnp.mean(grad_normal * normal, axis=-1, keepdims=True)
    )
    grad_before = grad_before.astype(jnp.bfloat16)
    grad_weight = lax.dot_general(
        stacked, grad_before, (((0,), (0,)), ((), ())), preferred_element_type=jnp.float32
    )
    grad_taps = lax.dot_general(
        grad_before, weight, (((1,), (1,)), ((), ())), preferred_element_type=jnp.float32
    ).reshape(sessions, length, 3 * width)
    grad_input = (
        grad_taps[..., :width]
        + unshifted(grad_taps[..., width : 2 * width], spacing)
        + unshifted(grad_taps[..., 2 * width :], 2 * spacing)
    )
    return (grad_input, grad_weight, grad_gain)


def to_owners(grad_rows, slot_place, shards, slot_count, width):
    outgoing = (
        jnp.zeros((shards * slot_count, width), jnp.bfloat16)
        .at[slot_place]
        .set(grad_rows)
        .reshape(shards, slot_count, width)
    )
    return lax.all_to_all(outgoing, "table", split_axis=0, concat_axis=0, tiled=True)


def padded_plan(shard_of, offsets, table, weight_one, gain_one, weight_two, gain_two, grad_out):
    sessions, length, _ = shard_of.shape
    width = table.shape[2]
    rows_dev = table.shape[1]
    item_count = sessions * length
    shards = lax.axis_size("table")
    groups = lax.axis_size("dp")
    quarter = width // groups
    slot_count = 8 * ((6 * item_count + 8 * shards - 1) // (8 * shards))
    target = shard_of.reshape(-1)
    table_pick = jnp.tile(jnp.arange(3, dtype=jnp.int32), item_count)
    row_codes = table_pick * rows_dev + offsets.reshape(-1)
    onehot = (jnp.arange(shards, dtype=jnp.int32)[:, None] == target[None, :]).astype(jnp.int32)
    before = jnp.cumsum(onehot, axis=1) - onehot
    slot_rank = jnp.sum(before * onehot, axis=0)
    slot_place = target * slot_count + slot_rank
    requests = (
        jnp.full((shards * slot_count,), -1, jnp.int32)
        .at[slot_place]
        .set(row_codes)
        .reshape(shards, slot_count)
    )
    table_flat = table.reshape(3 * rows_dev, width)
    asked_rows = lax.all_to_all(requests, "table", split_axis=0, concat_axis=0, tiled=True)
    found_rows = jnp.take(table_flat, jnp.maximum(asked_rows, 0), axis=0)
    found_rows = jnp.where((asked_rows >= 0)[..., None], found_rows, jnp.zeros((), jnp.bfloat16))
    sent_back = lax.all_to_all(found_rows, "table", split_axis=0, concat_axis=0, tiled=True)
    picked = jnp.take(sent_back.reshape(shards * slot_count, width), slot_place, axis=0).reshape(
        item_count, 3, width
    )
    embedded = (
        jnp.sum(picked.astype(jnp.float32), axis=1)
        .astype(jnp.bfloat16)
        .reshape(sessions, length, width)
    )
    act_one, saved_one = layer_forward(embedded, weight_one, gain_one, 1)
    hidden = act_one.astype(jnp.bfloat16).reshape(sessions, length, width)
    act_two, saved_two = layer_forward(hidden, weight_two, gain_two, 2)
    block_out = (
        (embedded.reshape(item_count, width).astype(jnp.float32) + act_two)
        .astype(jnp.bfloat16)
        .reshape(sessions, length, width)
    )
    grad_top = grad_out.reshape(item_count, width).astype(jnp.float32)
    scale = 1.0 / math.sqrt(item_count * groups * shards)
    grad_hidden, second_weights, second_gains = layer_backward(
        grad_top, weight_two, gain_two, saved_two, 2, sessions, length
    )
    grad_inner, first_weights, first_gains = layer_backward(
        grad_hidden.reshape(item_count, width), weight_one, gain_one, saved_one, 1, sessions, length
    )
    grad_embed = (grad_top + grad_inner.reshape(item_count, width)).astype(jnp.bfloat16)
    repeated = jnp.repeat(grad_embed, 3, axis=0)
    arrived = to_owners(repeated, slot_place, shards, slot_count, width)
    dense_grad = (
        jnp.zeros((3 * rows_dev, width), jnp.float32)
        .at[jnp.maximum(asked_rows, 0).reshape(-1)]
        .add(arrived.reshape(-1, width).astype(jnp.float32))
    )
    table_grad = lax.psum_scatter(
        dense_grad.astype(jnp.bfloat16), "dp", scatter_dimension=1, tiled=True
    ).astype(jnp.float32)
    table_grad = table_grad.reshape(3, rows_dev, quarter)
    totals = lax.psum((first_weights, second_weights, first_gains, second_gains), ("dp", "table"))
    return (
        block_out,
        totals[0] * scale,
        totals[1] * scale,
        totals[2] * scale,
        totals[3] * scale,
        table_grad,
    )


VMEM = pl.BlockSpec(memory_space=pltpu.VMEM)


def columns_fit(items_shape, table_shape, groups, shards):
    sessions, length, _ = items_shape
    _, rows_dev, width = table_shape
    run = 2 * length
    return (
        2 * width == groups * LANES
        and groups % 2 == 0
        and shards % 2 == 0
        and shards >= 4
        and sessions % 4 == 0
        and run % 16 == 0
        and (groups * sessions * length // 2) % (CHAINS * UNROLL) == 0
        and rows_dev % 32 == 0
        and CHAINS * shards * rows_dev * LANES * 4 <= 40 * MIB
    )


def low_lanes(rows):
    return lax.broadcasted_iota(jnp.int32, (rows, LANES), 1) < LANES // 2


def swap_halves(values):
    return pltpu.roll(values, LANES // 2, 1)


def own_columns(me, table):
    tables, rows_dev, _ = table.shape
    half = rows_dev // 2

    def kernel(me_ref, table_ref, *out_refs):
        odd = me_ref[0] % 2 == 1
        low = low_lanes(half)
        for t, out_ref in enumerate(out_refs):
            top = table_ref[t, :half, :].astype(jnp.float32)
            bottom = table_ref[t, half:, :].astype(jnp.float32)
            in_low = jnp.where(odd, swap_halves(top), top)
            in_high = jnp.where(odd, bottom, swap_halves(bottom))
            out_ref[...] = jnp.where(low, in_low, in_high).astype(jnp.bfloat16)

    return pl.pallas_call(
        kernel,
        grid_spec=pltpu.PrefetchScalarGridSpec(
            num_scalar_prefetch=1,
            grid=(1,),
            in_specs=[pl.BlockSpec((tables, rows_dev, LANES), lambda i, m: (0, 0, m[0] // 2))],
            out_specs=[pl.BlockSpec((half, LANES), lambda i, m: (0, 0))] * tables,
        ),
        out_shape=[jax.ShapeDtypeStruct((half, LANES), jnp.bfloat16)] * tables,
        compiler_params=pltpu.CompilerParams(vmem_limit_bytes=24 * MIB),
        name="own_columns",
    )(me, table)


def look_up(codes, slots, total, last):
    count = codes[0].shape[0]
    half = slots[0].shape[0]

    def kernel(low_ref, high_ref, *refs):
        slot_refs, refs = refs[: len(slots)], refs[len(slots) :]
        total_ref = None if total is None else refs[0]
        out_ref, rows, found = refs[-3:]
        for s, slot_ref in enumerate(slot_refs):
            values = slot_ref[...].astype(jnp.float32)
            rows[pl.ds(2 * s * half, half), :] = values
            rows[pl.ds((2 * s + 1) * half, half), :] = swap_halves(values)
        low = low_lanes(1)

        def some(step, carry):
            for j in range(16):
                i = step * 16 + j
                for_low = rows[pl.ds(low_ref[i], 1), :]
                for_high = rows[pl.ds(high_ref[i], 1), :]
                found[pl.ds(i, 1), :] = jnp.where(low, for_low, for_high)
            return carry

        lax.fori_loop(0, count // 16, some, 0)
        result = found[...]
        if total_ref is not None:
            result = result + total_ref[...]
        out_ref[...] = result.astype(out_ref.dtype)

    operands = list(slots) + ([] if total is None else [total])
    return pl.pallas_call(
        kernel,
        grid_spec=pltpu.PrefetchScalarGridSpec(
            num_scalar_prefetch=2,
            grid=(),
            in_specs=[VMEM] * len(operands),
            out_specs=VMEM,
            scratch_shapes=[
                pltpu.VMEM((2 * len(slots) * half, LANES), jnp.float32),
                pltpu.VMEM((count, LANES), jnp.float32),
            ],
        ),
        out_shape=jax.ShapeDtypeStruct((count, LANES), jnp.bfloat16 if last else jnp.float32),
        compiler_params=pltpu.CompilerParams(vmem_limit_bytes=32 * MIB),
        cost_estimate=pl.CostEstimate(
            flops=0, bytes_accessed=8 * 3 * count * LANES * 4, transcendentals=0
        ),
        name="look_up",
    )(*codes, *operands)


def add_rows(codes, blocks, shards, half):
    count = codes[0].shape[0]
    per = blocks[0].shape[0]
    planes = shards // 2
    share = count // CHAINS

    def kernel(low_ref, high_ref, *refs):
        block_refs, refs = refs[: len(blocks)], refs[len(blocks) :]
        near_ref, far_ref, values, *sums = refs
        for k, block_ref in enumerate(block_refs):
            values[pl.ds(k * per, per), :] = block_ref[...].astype(jnp.float32)
        for part in sums:
            part[...] = jnp.zeros_like(part)
        low = low_lanes(1)
        high = jnp.logical_not(low)

        def some(step, carry):
            for j in range(UNROLL):
                ready = []
                for k, part in enumerate(sums):
                    i = k * share + step * UNROLL + j
                    value = values[pl.ds(i, 1), :]
                    to_low, to_high = pl.ds(low_ref[i], 1), pl.ds(high_ref[i], 1)
                    ready.append((to_low, part[to_low, :] + value, to_high, part[to_high, :] + value))
                for part, (to_low, in_low, to_high, in_high) in zip(sums, ready):
                    pltpu.store(part.at[to_low, :], in_low, mask=low)
                    pltpu.store(part.at[to_high, :], in_high, mask=high)
            return carry

        lax.fori_loop(0, share // UNROLL, some, 0)
        for s in range(shards):
            straight = sum(part[pl.ds(2 * s * half, half), :] for part in sums)
            crossed = sum(part[pl.ds((2 * s + 1) * half, half), :] for part in sums)
            result = (straight + swap_halves(crossed)).astype(jnp.bfloat16)
            if s < planes:
                near_ref[s] = result
            else:
                far_ref[s - planes] = result

    return pl.pallas_call(
        kernel,
        grid_spec=pltpu.PrefetchScalarGridSpec(
            num_scalar_prefetch=2,
            grid=(),
            in_specs=[VMEM] * len(blocks),
            out_specs=[VMEM] * 2,
            scratch_shapes=[pltpu.VMEM((count, LANES), jnp.float32)]
            + [pltpu.VMEM((2 * shards * half, LANES), jnp.float32)] * CHAINS,
        ),
        out_shape=[jax.ShapeDtypeStruct((planes, half, LANES), jnp.bfloat16)] * 2,
        compiler_params=pltpu.CompilerParams(vmem_limit_bytes=56 * MIB),
        cost_estimate=pl.CostEstimate(
            flops=0, bytes_accessed=12 * 3 * count * LANES * 4, transcendentals=0
        ),
        name="add_rows",
    )(*codes, *blocks)


def both_layers(me, blocks, weight_one, gain_one, weight_two, gain_two, grad_out, length):
    groups = len(blocks)
    items, width = grad_out.shape
    run = 2 * length
    steps = items // (2 * run)
    tall = weight_one.shape[0]
    chunk = -(-(2 * tall + 16) // (32 * groups)) * 32

    def kernel(me_ref, *refs):
        block_refs, refs = refs[:groups], refs[groups:]
        w_one_ref, g_one_ref, w_two_ref, g_two_ref, top_ref, out_ref, *refs = refs
        grad_refs, weight_refs, refs = refs[:groups], refs[groups : 2 * groups], refs[2 * groups :]
        held, packed, sum_one, sum_two, sum_gains, flat = refs
        step = pl.program_id(0)
        me_at = me_ref[0]
        low = low_lanes(run)
        place = lax.broadcasted_iota(jnp.int32, (run, width), 0)
        place = jnp.where(place >= length, place - length, place)

        @pl.when(step == 0)
        def _():
            sum_one[...] = jnp.zeros_like(sum_one)
            sum_two[...] = jnp.zeros_like(sum_two)
            sum_gains[...] = jnp.zeros_like(sum_gains)

        def taps(values, gap):
            one = jnp.where(place >= gap, pltpu.roll(values, gap, 0), 0.0)
            two = jnp.where(place >= 2 * gap, pltpu.roll(values, 2 * gap, 0), 0.0)
            return jnp.concatenate([x.astype(jnp.bfloat16) for x in (values, one, two)], axis=1)

        def untaps(values, gap):
            one = jnp.where(place < length - gap, pltpu.roll(values, run - gap, 0), 0.0)
            two = jnp.where(place < length - 2 * gap, pltpu.roll(values, run - 2 * gap, 0), 0.0)
            return [x.astype(jnp.bfloat16) for x in (values, one, two)]

        def forward(values, weight_ref, gain, gap):
            before = jnp.dot(taps(values, gap), weight_ref[...], preferred_element_type=jnp.float32)
            centred = before - jnp.mean(before, axis=-1, keepdims=True)
            inv_std = lax.rsqrt(jnp.mean(centred * centred, axis=-1, keepdims=True) + 1e-05)
            normal = centred * inv_std
            output, slope = gelu_parts(normal * gain)
            return output, (normal, inv_std, slope)

        def backward(grad, values, weight_ref, gain, saved, gap, total, row):
            normal, inv_std, slope = saved
            scaled = grad * slope
            sum_gains[pl.ds(row, 1), :] += jnp.sum(scaled * normal, axis=0, keepdims=True)
            back = scaled * gain
            before = inv_std * (
                back
                - jnp.mean(back, axis=-1, keepdims=True)
                - normal * jnp.mean(back * normal, axis=-1, keepdims=True)
            )
            parts = untaps(before.astype(jnp.bfloat16).astype(jnp.float32), gap)
            total[...] += lax.dot_general(
                values.astype(jnp.bfloat16),
                jnp.concatenate(parts, axis=1),
                (((0,), (0,)), ((), ())),
                preferred_element_type=jnp.float32,
            )
            return sum(
                lax.dot_general(
                    part,
                    weight_ref[k * width : (k + 1) * width, :],
                    (((1,), (1,)), ((), ())),
                    preferred_element_type=jnp.float32,
                )
                for k, part in enumerate(parts)
            )

        for k in range(groups):
            held[k] = block_refs[k][...].astype(jnp.float32)
        gain_one_at, gain_two_at = g_one_ref[...], g_two_ref[...]
        back_to = []
        for side in range(2):
            columns = []
            for q in range(0, groups, 2):
                left = held[(q - me_at + groups) % groups]
                right = held[(q + 1 - me_at + groups) % groups]
                if side == 0:
                    columns.append(jnp.where(low, left, swap_halves(right)))
                else:
                    columns.append(jnp.where(low, swap_halves(left), right))
            embedded = jnp.concatenate(columns, axis=1)
            rows = pl.ds(side * run, run)
            top = top_ref[rows, :].astype(jnp.float32)
            act_one, saved_one = forward(embedded, w_one_ref, gain_one_at, 1)
            hidden = act_one.astype(jnp.bfloat16).astype(jnp.float32)
            act_two, saved_two = forward(hidden, w_two_ref, gain_two_at, 2)
            out_ref[rows, :] = (embedded + act_two).astype(jnp.bfloat16)
            grad_hidden = backward(top, hidden, w_two_ref, gain_two_at, saved_two, 2, sum_two, 1)
            grad_inner = backward(grad_hidden, embedded, w_one_ref, gain_one_at, saved_one, 1, sum_one, 0)
            back_to.append(top + grad_inner)
        for q in range(groups):
            at = slice((q // 2) * LANES, (q // 2 + 1) * LANES)
            first, second = back_to[0][:, at], back_to[1][:, at]
            if q % 2 == 0:
                pair = jnp.where(low, first, swap_halves(second))
            else:
                pair = jnp.where(low, swap_halves(first), second)
            packed[(q - me_at + groups) % groups] = pair
        for k in range(groups):
            grad_refs[k][...] = packed[k].astype(jnp.bfloat16)

        @pl.when(step == steps - 1)
        def _():
            for n, total in enumerate((sum_one, sum_two)):
                for k in range(tall // width):
                    flat[n * tall + k * width : n * tall + (k + 1) * width, :] = total[
                        :, k * width : (k + 1) * width
                    ].astype(jnp.bfloat16)
            flat[2 * tall : 2 * tall + 16, :] = jnp.concatenate(
                [sum_gains[...], jnp.zeros_like(sum_gains)], axis=0
            ).astype(jnp.bfloat16)
            if groups * chunk > 2 * tall + 16:
                flat[2 * tall + 16 :, :] = jnp.zeros(
                    (groups * chunk - 2 * tall - 16, width), jnp.bfloat16
                )
            for k in range(groups):
                begin = pl.multiple_of(((me_at + k) % groups) * chunk, 32)
                weight_refs[k][...] = flat[pl.ds(begin, chunk), :]

    def whole(shape):
        return pl.BlockSpec(shape, lambda j, m: (0, 0))

    def by_step(rows, columns):
        return pl.BlockSpec((rows, columns), lambda j, m: (j, 0))

    return pl.pallas_call(
        kernel,
        grid_spec=pltpu.PrefetchScalarGridSpec(
            num_scalar_prefetch=1,
            grid=(steps,),
            in_specs=[by_step(run, LANES)] * groups
            + [whole((tall, width)), whole((1, width))] * 2
            + [by_step(2 * run, width)],
            out_specs=[by_step(2 * run, width)]
            + [by_step(run, LANES)] * groups
            + [whole((chunk, width))] * groups,
            scratch_shapes=[
                pltpu.VMEM((groups, run, LANES), jnp.float32),
                pltpu.VMEM((groups, run, LANES), jnp.float32),
                pltpu.VMEM((width, tall), jnp.float32),
                pltpu.VMEM((width, tall), jnp.float32),
                pltpu.VMEM((8, width), jnp.float32),
                pltpu.VMEM((groups * chunk, width), jnp.bfloat16),
            ],
        ),
        out_shape=[jax.ShapeDtypeStruct((items, width), jnp.bfloat16)]
        + [jax.ShapeDtypeStruct((items // 2, LANES), jnp.bfloat16)] * groups
        + [jax.ShapeDtypeStruct((chunk, width), jnp.bfloat16)] * groups,
        compiler_params=pltpu.CompilerParams(vmem_limit_bytes=48 * MIB),
        name="both_layers",
    )(
        me,
        *blocks,
        weight_one,
        gain_one.reshape(1, width),
        weight_two,
        gain_two.reshape(1, width),
        grad_out,
    )


def column_plan(shard_of, offsets, table, weight_one, gain_one, weight_two, gain_two, grad_out):
    sessions, length, _ = shard_of.shape
    tables, rows_dev, width = table.shape
    items = sessions * length
    groups = lax.axis_size("dp")
    shards = lax.axis_size("table")
    planes = shards // 2
    half = rows_dev // 2
    run = 2 * length
    me = lax.axis_index("dp")
    plane, core = lax.axis_index("table") // 2, lax.axis_index("table") % 2
    me_at = me.astype(jnp.int32).reshape(1)

    def dp_shift(values, k):
        return lax.ppermute(values, "dp", [(i, (i + k) % groups) for i in range(groups)])

    def up(values):
        return lax.ppermute(values, "table", [(i, (i + 2) % shards) for i in range(shards)])

    def down(values):
        return lax.ppermute(values, "table", [(i, (i - 2) % shards) for i in range(shards)])

    def across(values):
        return lax.ppermute(values, "table", [(i, i ^ 1) for i in range(shards)])

    slot = (shard_of + core) % 2 * planes + (shard_of // 2 - plane + planes) % planes
    places = jnp.stack(
        [slot * rows_dev + offsets, slot * rows_dev + (offsets + half) % rows_dev], axis=0
    ).astype(jnp.int32)
    places = places.reshape(2, items // (2 * run), 2, run, tables)
    mine = jnp.stack([places[0, :, 0], places[1, :, 1]], axis=0)
    mine = jnp.transpose(mine, (3, 0, 1, 2)).reshape(tables, 2, items // 2)
    all_codes = jnp.concatenate([mine] + [dp_shift(mine, k) for k in range(1, groups)], axis=2)
    codes = [(all_codes[t, 0], all_codes[t, 1]) for t in range(tables)]

    total = None
    for t, own in enumerate(own_columns(me_at, table)):
        near = [None] * planes
        near[0] = rising = falling = own
        for k in range(1, planes // 2 + 1):
            near[planes - k] = rising = up(rising)
            if k <= (planes - 1) // 2:
                near[k] = falling = down(falling)
        far = [across(values) for values in near]
        total = look_up(codes[t], near + far, total, t == tables - 1)

    pieces = total.reshape(groups, items // 2, LANES)
    arrived = [pieces[0]] + [dp_shift(pieces[k], -k) for k in range(1, groups)]
    done = both_layers(
        me_at, arrived, weight_one, gain_one, weight_two, gain_two, grad_out.reshape(items, width), length
    )
    block_out = done[0].reshape(sessions, length, width)
    sent, sums = done[1 : 1 + groups], done[1 + groups :]
    blocks = [sent[0]] + [dp_shift(sent[k], k) for k in range(1, groups)]

    grads = []
    for t in range(tables):
        near, far = add_rows(codes[t], blocks, shards, half)
        got = across(far)

        def both(r):
            return near[r].astype(jnp.float32) + got[r].astype(jnp.float32)

        result = both(0)
        for move, order in (
            (up, list(range(planes // 2, 0, -1))),
            (down, list(range(planes // 2 + 1, planes))),
        ):
            moving = None
            for r in order:
                term = both(r)
                if moving is not None:
                    term = term + moving.astype(jnp.float32)
                moving = move(term.astype(jnp.bfloat16))
            if moving is not None:
                result = result + moving.astype(jnp.float32)
        grads.append(jnp.concatenate([result[:, : LANES // 2], result[:, LANES // 2 :]], axis=0))
    table_grad = jnp.stack(grads, axis=0)

    def add_up(parts):
        return sum(part.astype(jnp.float32) for part in parts)

    chunk = sums[0].shape[0]
    mid = add_up([sums[0]] + [dp_shift(sums[k], k) for k in range(1, groups)]).astype(jnp.bfloat16)
    kept = lax.dynamic_slice_in_dim(mid, core * (chunk // 2), chunk // 2, 0)
    given = lax.dynamic_slice_in_dim(mid, (1 - core) * (chunk // 2), chunk // 2, 0)
    by_plane = [None] * planes
    by_plane[0] = rising = falling = add_up([kept, across(given)]).astype(jnp.bfloat16)
    for k in range(1, planes // 2 + 1):
        by_plane[planes - k] = rising = up(rising)
        if k <= (planes - 1) // 2:
            by_plane[k] = falling = down(falling)
    stacked = jnp.stack(by_plane, axis=0)
    kept = add_up(
        [
            lax.dynamic_index_in_dim(stacked, (a - plane + planes) % planes, 0, keepdims=False)
            for a in range(planes)
        ]
    ).astype(jnp.bfloat16)
    given = across(kept)
    mid = jnp.where(core == 0, jnp.concatenate([kept, given]), jnp.concatenate([given, kept]))
    stacked = jnp.stack([mid] + [dp_shift(mid, k) for k in range(1, groups)], axis=0)
    sums = jnp.concatenate(
        [
            lax.dynamic_index_in_dim(stacked, (me - a + groups) % groups, 0, keepdims=False)
            for a in range(groups)
        ],
        axis=0,
    ).astype(jnp.float32) * (1.0 / math.sqrt(items * groups * shards))
    tall = weight_one.shape[0]
    return (
        block_out,
        sums[:tall],
        sums[tall : 2 * tall],
        sums[2 * tall],
        sums[2 * tall + 1],
        table_grad,
    )


def solution(mesh):
    placed = (
        P(("dp", "table"), None, None),
        P(("dp", "table"), None, None),
        P(None, "table", None),
        P(),
        P(),
        P(),
        P(),
        P(("dp", "table"), None, None),
    )

    def on_device(shard_of, offsets, table, *rest):
        fits = columns_fit(shard_of.shape, table.shape, mesh.shape["dp"], mesh.shape["table"])
        plan = column_plan if fits else padded_plan
        return plan(shard_of, offsets, table, *rest)

    return jax.shard_map(
        on_device,
        mesh=mesh,
        in_specs=placed,
        out_specs=(P(("dp", "table"), None, None), P(), P(), P(), P(), P(None, "table", "dp")),
        check_vma=False,
    )
```

```python
import math

import jax
import jax.numpy as jnp
from jax import lax
from jax.experimental import pallas as pl
from jax.experimental.pallas import tpu as pltpu
from jax.sharding import PartitionSpec as P

GELU_C = 0.7978845608028654
GELU_K = 0.044715
LANES = 128
MIB = 2**20

UNROLL = 4


def shifted(values, spacing):
    return jnp.pad(values, ((0, 0), (spacing, 0), (0, 0)))[:, : values.shape[1], :]


def unshifted(values, spacing):
    return jnp.pad(values, ((0, 0), (0, spacing), (0, 0)))[:, spacing:, :]


def stack_taps(values, spacing):
    return jnp.concatenate(
        [values, shifted(values, spacing), shifted(values, 2 * spacing)], axis=-1
    )


def gelu_parts(inputs):
    inner = GELU_C * (inputs + GELU_K * inputs * inputs * inputs)
    tangent = jnp.tanh(inner)
    output = 0.5 * inputs * (1.0 + tangent)
    slope = 0.5 * (1.0 + tangent) + 0.5 * inputs * (1.0 - tangent * tangent) * GELU_C * (
        1.0 + 3.0 * GELU_K * inputs * inputs
    )
    return (output, slope)


def layer_forward(values, weight, gain, spacing):
    sessions, length, width = values.shape
    stacked = stack_taps(values, spacing).reshape(sessions * length, 3 * width)
    before_norm = jnp.dot(stacked, weight, preferred_element_type=jnp.float32)
    centred = before_norm - jnp.mean(before_norm, axis=-1, keepdims=True)
    inv_std = lax.rsqrt(jnp.mean(centred * centred, axis=-1, keepdims=True) + 1e-05)
    normal = centred * inv_std
    output, slope = gelu_parts(normal * gain)
    return (output, (stacked, normal, inv_std, slope))


def layer_backward(grad_output, weight, gain, saved, spacing, sessions, length):
    stacked, normal, inv_std, slope = saved
    width = weight.shape[1]
    grad_scaled = grad_output * slope
    grad_gain = jnp.sum(grad_scaled * normal, axis=0)
    grad_normal = grad_scaled * gain
    grad_before = inv_std * (
        grad_normal
        - jnp.mean(grad_normal, axis=-1, keepdims=True)
        - normal * jnp.mean(grad_normal * normal, axis=-1, keepdims=True)
    )
    grad_before = grad_before.astype(jnp.bfloat16)
    grad_weight = lax.dot_general(
        stacked, grad_before, (((0,), (0,)), ((), ())), preferred_element_type=jnp.float32
    )
    grad_taps = lax.dot_general(
        grad_before, weight, (((1,), (1,)), ((), ())), preferred_element_type=jnp.float32
    ).reshape(sessions, length, 3 * width)
    grad_input = (
        grad_taps[..., :width]
        + unshifted(grad_taps[..., width : 2 * width], spacing)
        + unshifted(grad_taps[..., 2 * width :], 2 * spacing)
    )
    return (grad_input, grad_weight, grad_gain)


def to_owners(grad_rows, slot_place, shards, slot_count, width):
    outgoing = (
        jnp.zeros((shards * slot_count, width), jnp.bfloat16)
        .at[slot_place]
        .set(grad_rows)
        .reshape(shards, slot_count, width)
    )
    return lax.all_to_all(outgoing, "table", split_axis=0, concat_axis=0, tiled=True)


def padded_plan(shard_of, offsets, table, weight_one, gain_one, weight_two, gain_two, grad_out):
    sessions, length, _ = shard_of.shape
    width = table.shape[2]
    rows_dev = table.shape[1]
    item_count = sessions * length
    shards = lax.axis_size("table")
    groups = lax.axis_size("dp")
    quarter = width // groups
    slot_count = 8 * ((6 * item_count + 8 * shards - 1) // (8 * shards))
    target = shard_of.reshape(-1)
    table_pick = jnp.tile(jnp.arange(3, dtype=jnp.int32), item_count)
    row_codes = table_pick * rows_dev + offsets.reshape(-1)
    onehot = (jnp.arange(shards, dtype=jnp.int32)[:, None] == target[None, :]).astype(jnp.int32)
    before = jnp.cumsum(onehot, axis=1) - onehot
    slot_rank = jnp.sum(before * onehot, axis=0)
    slot_place = target * slot_count + slot_rank
    requests = (
        jnp.full((shards * slot_count,), -1, jnp.int32)
        .at[slot_place]
        .set(row_codes)
        .reshape(shards, slot_count)
    )
    table_flat = table.reshape(3 * rows_dev, width)
    asked_rows = lax.all_to_all(requests, "table", split_axis=0, concat_axis=0, tiled=True)
    found_rows = jnp.take(table_flat, jnp.maximum(asked_rows, 0), axis=0)
    found_rows = jnp.where((asked_rows >= 0)[..., None], found_rows, jnp.zeros((), jnp.bfloat16))
    sent_back = lax.all_to_all(found_rows, "table", split_axis=0, concat_axis=0, tiled=True)
    picked = jnp.take(sent_back.reshape(shards * slot_count, width), slot_place, axis=0).reshape(
        item_count, 3, width
    )
    embedded = (
        jnp.sum(picked.astype(jnp.float32), axis=1)
        .astype(jnp.bfloat16)
        .reshape(sessions, length, width)
    )
    act_one, saved_one = layer_forward(embedded, weight_one, gain_one, 1)
    hidden = act_one.astype(jnp.bfloat16).reshape(sessions, length, width)
    act_two, saved_two = layer_forward(hidden, weight_two, gain_two, 2)
    block_out = (
        (embedded.reshape(item_count, width).astype(jnp.float32) + act_two)
        .astype(jnp.bfloat16)
        .reshape(sessions, length, width)
    )
    grad_top = grad_out.reshape(item_count, width).astype(jnp.float32)
    scale = 1.0 / math.sqrt(item_count * groups * shards)
    grad_hidden, second_weights, second_gains = layer_backward(
        grad_top, weight_two, gain_two, saved_two, 2, sessions, length
    )
    grad_inner, first_weights, first_gains = layer_backward(
        grad_hidden.reshape(item_count, width), weight_one, gain_one, saved_one, 1, sessions, length
    )
    grad_embed = (grad_top + grad_inner.reshape(item_count, width)).astype(jnp.bfloat16)
    repeated = jnp.repeat(grad_embed, 3, axis=0)
    arrived = to_owners(repeated, slot_place, shards, slot_count, width)
    dense_grad = (
        jnp.zeros((3 * rows_dev, width), jnp.float32)
        .at[jnp.maximum(asked_rows, 0).reshape(-1)]
        .add(arrived.reshape(-1, width).astype(jnp.float32))
    )
    table_grad = lax.psum_scatter(
        dense_grad.astype(jnp.bfloat16), "dp", scatter_dimension=1, tiled=True
    ).astype(jnp.float32)
    table_grad = table_grad.reshape(3, rows_dev, quarter)
    totals = lax.psum((first_weights, second_weights, first_gains, second_gains), ("dp", "table"))
    return (
        block_out,
        totals[0] * scale,
        totals[1] * scale,
        totals[2] * scale,
        totals[3] * scale,
        table_grad,
    )


VMEM = pl.BlockSpec(memory_space=pltpu.VMEM)


def columns_fit(items_shape, table_shape, groups, shards):
    sessions, length, _ = items_shape
    _, rows_dev, width = table_shape
    run = 2 * length
    return (
        2 * width == groups * LANES
        and groups % 2 == 0
        and shards >= 4
        and (shards & (shards - 1)) == 0
        and sessions % 4 == 0
        and run % 16 == 0
        and (groups * sessions * length // 2) % (16) == 0
        and rows_dev % 32 == 0
        and table_shape[0] * shards * rows_dev * LANES * 4 <= 32 * MIB
    )


def low_lanes(rows):
    return lax.broadcasted_iota(jnp.int32, (rows, LANES), 1) < LANES // 2


def swap_halves(values):
    return pltpu.roll(values, LANES // 2, 1)


def own_columns(at, table):
    tables, rows_dev, _ = table.shape
    half = rows_dev // 2

    def kernel(at_ref, table_ref, first_ref, last_ref, all_ref):
        odd = at_ref[0] % 2 == 1
        low = low_lanes(half)
        for t in range(tables):
            top = table_ref[t, :half, :].astype(jnp.float32)
            bottom = table_ref[t, half:, :].astype(jnp.float32)
            in_low = jnp.where(odd, swap_halves(top), top)
            in_high = jnp.where(odd, bottom, swap_halves(bottom))
            values = jnp.where(low, in_low, in_high).astype(jnp.bfloat16)
            if t < tables - 1:
                first_ref[t] = values
            else:
                last_ref[0] = values
            all_ref[t] = values

    def whole(count):
        return pl.BlockSpec((count, half, LANES), lambda i, m: (0, 0, 0))

    return pl.pallas_call(
        kernel,
        grid_spec=pltpu.PrefetchScalarGridSpec(
            num_scalar_prefetch=1,
            grid=(1,),
            in_specs=[pl.BlockSpec((tables, rows_dev, LANES), lambda i, m: (0, 0, m[0] // 2))],
            out_specs=[whole(tables - 1), whole(1), whole(tables)],
        ),
        out_shape=[
            jax.ShapeDtypeStruct((count, half, LANES), jnp.bfloat16)
            for count in (tables - 1, 1, tables)
        ],
        compiler_params=pltpu.CompilerParams(vmem_limit_bytes=24 * MIB),
        name="own_columns",
    )(at, table)


def look_up(codes, slots, total, last):
    count = codes[0].shape[0]
    half = slots[0][0].shape[1]

    def kernel(low_ref, high_ref, *refs):
        slot_refs, refs = refs[: len(slots)], refs[len(slots) :]
        total_ref = None if total is None else refs[0]
        out_ref, rows, found = refs[-3:]
        for s, slot_ref in enumerate(slot_refs):
            values = slot_ref[0].astype(jnp.float32)
            rows[pl.ds(2 * s * half, half), :] = values
            rows[pl.ds((2 * s + 1) * half, half), :] = swap_halves(values)
        low = low_lanes(1)

        def some(step, carry):
            for j in range(16):
                i = step * 16 + j
                for_low = rows[pl.ds(low_ref[i], 1), :]
                for_high = rows[pl.ds(high_ref[i], 1), :]
                found[pl.ds(i, 1), :] = jnp.where(low, for_low, for_high)
            return carry

        lax.fori_loop(0, count // 16, some, 0)
        result = found[...]
        if total_ref is not None:
            result = result + total_ref[...]
        out_ref[...] = result.astype(out_ref.dtype)

    def part(at):
        return pl.BlockSpec((1, half, LANES), lambda i, *codes: (at, 0, 0))

    operands = [slot[0] for slot in slots] + ([] if total is None else [total])
    whole = pl.BlockSpec((count, LANES), lambda i, *codes: (0, 0))
    return pl.pallas_call(
        kernel,
        grid_spec=pltpu.PrefetchScalarGridSpec(
            num_scalar_prefetch=2,
            grid=(1,),
            in_specs=[part(slot[1]) for slot in slots] + ([] if total is None else [whole]),
            out_specs=whole,
            scratch_shapes=[
                pltpu.VMEM((2 * len(slots) * half, LANES), jnp.float32),
                pltpu.VMEM((count, LANES), jnp.float32),
            ],
        ),
        out_shape=jax.ShapeDtypeStruct((count, LANES), jnp.bfloat16 if last else jnp.float32),
        compiler_params=pltpu.CompilerParams(vmem_limit_bytes=32 * MIB),
        cost_estimate=pl.CostEstimate(
            flops=0, bytes_accessed=8 * 3 * count * LANES * 4, transcendentals=0
        ),
        name="look_up",
    )(*codes, *operands)


def add_rows(codes, blocks, shards, half):
    tables = len(codes)
    count = codes[0][0].shape[0]
    per = blocks[0].shape[0]
    planes = shards // 2

    def kernel(*refs):
        code_refs, refs = refs[: 2 * tables], refs[2 * tables :]
        block_refs, refs = refs[: len(blocks)], refs[len(blocks) :]
        out_refs, values, sums = refs[: 2 * tables], refs[2 * tables], refs[2 * tables + 1 :]
        for k, block_ref in enumerate(block_refs):
            values[pl.ds(k * per, per), :] = block_ref[...].astype(jnp.float32)
        for part in sums:
            part[...] = jnp.zeros_like(part)
        low = low_lanes(1)
        high = jnp.logical_not(low)

        def some(step, carry):
            for j in range(UNROLL):
                i = step * UNROLL + j
                value = values[pl.ds(i, 1), :]
                ready = []
                for t, part in enumerate(sums):
                    to_low, to_high = pl.ds(code_refs[2 * t][i], 1), pl.ds(code_refs[2 * t + 1][i], 1)
                    ready.append((to_low, part[to_low, :] + value, to_high, part[to_high, :] + value))
                for part, (to_low, in_low, to_high, in_high) in zip(sums, ready):
                    pltpu.store(part.at[to_low, :], in_low, mask=low)
                    pltpu.store(part.at[to_high, :], in_high, mask=high)
            return carry

        lax.fori_loop(0, count // UNROLL, some, 0)
        for t, part in enumerate(sums):
            for s in range(shards):
                straight = part[pl.ds(2 * s * half, half), :]
                crossed = part[pl.ds((2 * s + 1) * half, half), :]
                result = (straight + swap_halves(crossed)).astype(jnp.bfloat16)
                out_refs[2 * t + s // planes][s % planes] = result

    results = pl.pallas_call(
        kernel,
        grid_spec=pltpu.PrefetchScalarGridSpec(
            num_scalar_prefetch=2 * tables,
            grid=(),
            in_specs=[VMEM] * len(blocks),
            out_specs=[VMEM] * (2 * tables),
            scratch_shapes=[pltpu.VMEM((count, LANES), jnp.float32)]
            + [pltpu.VMEM((2 * shards * half, LANES), jnp.float32)] * tables,
        ),
        out_shape=[jax.ShapeDtypeStruct((planes, half, LANES), jnp.bfloat16)] * (2 * tables),
        compiler_params=pltpu.CompilerParams(vmem_limit_bytes=48 * MIB),
        cost_estimate=pl.CostEstimate(
            flops=0, bytes_accessed=100 * MIB, transcendentals=0
        ),
        name="add_rows",
    )(*[part for pair in codes for part in pair], *blocks)
    return list(zip(results[::2], results[1::2]))


def weight_chunk(tall, groups):
    return -(-(2 * tall + 16) // (32 * groups)) * 16


def scaled_sums(at, near, far, tall, scale):
    groups, chunk, width = near.shape

    def kernel(at_ref, near_ref, far_ref, one_ref, two_ref, gain_one_ref, gain_two_ref, flat):
        me, core = at_ref[0], at_ref[1]
        for k in range(groups):
            for part_ref, side in ((near_ref, core), (far_ref, 1 - core)):
                begin = pl.multiple_of((side * groups + (me - k + groups) % groups) * chunk, 16)
                flat[pl.ds(begin, chunk), :] = part_ref[k].astype(jnp.float32) * scale
        one_ref[...] = flat[:tall, :]
        two_ref[...] = flat[tall : 2 * tall, :]
        gain_one_ref[...] = flat[2 * tall : 2 * tall + 1, :]
        gain_two_ref[...] = flat[2 * tall + 1 : 2 * tall + 2, :]

    return pl.pallas_call(
        kernel,
        grid_spec=pltpu.PrefetchScalarGridSpec(
            num_scalar_prefetch=1,
            grid=(),
            in_specs=[VMEM] * 2,
            out_specs=[VMEM] * 4,
            scratch_shapes=[pltpu.VMEM((2 * groups * chunk, width), jnp.float32)],
        ),
        out_shape=[jax.ShapeDtypeStruct((tall, width), jnp.float32)] * 2
        + [jax.ShapeDtypeStruct((1, width), jnp.float32)] * 2,
        compiler_params=pltpu.CompilerParams(vmem_limit_bytes=16 * MIB),
        name="scaled_sums",
    )(at, near, far)


def both_layers(me, blocks, weight_one, gain_one, weight_two, gain_two, grad_out, length):
    groups = len(blocks)
    items, width = grad_out.shape
    run = 2 * length
    steps = items // (2 * run)
    tall = weight_one.shape[0]
    chunk = weight_chunk(tall, groups)

    def kernel(me_ref, *refs):
        block_refs, refs = refs[:groups], refs[groups:]
        w_one_ref, g_one_ref, w_two_ref, g_two_ref, top_ref, out_ref, *refs = refs
        grad_refs, refs = refs[:groups], refs[groups:]
        kept_ref, given_ref, held, packed, sum_one, sum_two, sum_gains, flat = refs
        step = pl.program_id(0)
        me_at, core = me_ref[0], me_ref[1]
        low = low_lanes(run)
        place = lax.broadcasted_iota(jnp.int32, (run, width), 0)
        place = jnp.where(place >= length, place - length, place)

        @pl.when(step == 0)
        def _():
            sum_one[...] = jnp.zeros_like(sum_one)
            sum_two[...] = jnp.zeros_like(sum_two)
            sum_gains[...] = jnp.zeros_like(sum_gains)

        def taps(values, gap):
            one = jnp.where(place >= gap, pltpu.roll(values, gap, 0), 0.0)
            two = jnp.where(place >= 2 * gap, pltpu.roll(values, 2 * gap, 0), 0.0)
            return jnp.concatenate([x.astype(jnp.bfloat16) for x in (values, one, two)], axis=1)

        def untaps(values, gap):
            one = jnp.where(place < length - gap, pltpu.roll(values, run - gap, 0), 0.0)
            two = jnp.where(place < length - 2 * gap, pltpu.roll(values, run - 2 * gap, 0), 0.0)
            return [x.astype(jnp.bfloat16) for x in (values, one, two)]

        def forward(values, weight_ref, gain, gap):
            before = jnp.dot(taps(values, gap), weight_ref[...], preferred_element_type=jnp.float32)
            centred = before - jnp.mean(before, axis=-1, keepdims=True)
            inv_std = lax.rsqrt(jnp.mean(centred * centred, axis=-1, keepdims=True) + 1e-05)
            normal = centred * inv_std
            output, slope = gelu_parts(normal * gain)
            return output, (normal, inv_std, slope)

        def backward(grad, values, weight_ref, gain, saved, gap, total, row):
            normal, inv_std, slope = saved
            scaled = grad * slope
            sum_gains[pl.ds(row, 1), :] += jnp.sum(scaled * normal, axis=0, keepdims=True)
            back = scaled * gain
            before = inv_std * (
                back
                - jnp.mean(back, axis=-1, keepdims=True)
                - normal * jnp.mean(back * normal, axis=-1, keepdims=True)
            )
            parts = untaps(before.astype(jnp.bfloat16).astype(jnp.float32), gap)
            total[...] += lax.dot_general(
                values.astype(jnp.bfloat16),
                jnp.concatenate(parts, axis=1),
                (((0,), (0,)), ((), ())),
                preferred_element_type=jnp.float32,
            )
            return sum(
                lax.dot_general(
                    part,
                    weight_ref[k * width : (k + 1) * width, :],
                    (((1,), (1,)), ((), ())),
                    preferred_element_type=jnp.float32,
                )
                for k, part in enumerate(parts)
            )

        for k in range(groups):
            held[k] = block_refs[k][...].astype(jnp.float32)
        gain_one_at, gain_two_at = g_one_ref[...], g_two_ref[...]
        back_to = []
        for side in range(2):
            columns = []
            for q in range(0, groups, 2):
                left = held[(q - me_at + groups) % groups]
                right = held[(q + 1 - me_at + groups) % groups]
                if side == 0:
                    columns.append(jnp.where(low, left, swap_halves(right)))
                else:
                    columns.append(jnp.where(low, swap_halves(left), right))
            embedded = jnp.concatenate(columns, axis=1)
            rows = pl.ds(side * run, run)
            top = top_ref[rows, :].astype(jnp.float32)
            act_one, saved_one = forward(embedded, w_one_ref, gain_one_at, 1)
            hidden = act_one.astype(jnp.bfloat16).astype(jnp.float32)
            act_two, saved_two = forward(hidden, w_two_ref, gain_two_at, 2)
            out_ref[rows, :] = (embedded + act_two).astype(jnp.bfloat16)
            grad_hidden = backward(top, hidden, w_two_ref, gain_two_at, saved_two, 2, sum_two, 1)
            grad_inner = backward(grad_hidden, embedded, w_one_ref, gain_one_at, saved_one, 1, sum_one, 0)
            back_to.append(top + grad_inner)
        for q in range(groups):
            at = slice((q // 2) * LANES, (q // 2 + 1) * LANES)
            first, second = back_to[0][:, at], back_to[1][:, at]
            if q % 2 == 0:
                pair = jnp.where(low, first, swap_halves(second))
            else:
                pair = jnp.where(low, swap_halves(first), second)
            packed[(q - me_at + groups) % groups] = pair
        for k in range(groups):
            grad_refs[k][...] = packed[k].astype(jnp.bfloat16)

        @pl.when(step == steps - 1)
        def _():
            for n, total in enumerate((sum_one, sum_two)):
                for k in range(tall // width):
                    flat[n * tall + k * width : n * tall + (k + 1) * width, :] = total[
                        :, k * width : (k + 1) * width
                    ].astype(jnp.bfloat16)
            flat[2 * tall : 2 * tall + 16, :] = jnp.concatenate(
                [sum_gains[...], jnp.zeros_like(sum_gains)], axis=0
            ).astype(jnp.bfloat16)
            if 2 * groups * chunk > 2 * tall + 16:
                flat[2 * tall + 16 :, :] = jnp.zeros(
                    (2 * groups * chunk - 2 * tall - 16, width), jnp.bfloat16
                )
            for k in range(groups):
                for part_ref, side in ((kept_ref, core), (given_ref, 1 - core)):
                    begin = pl.multiple_of((side * groups + (me_at + k) % groups) * chunk, 16)
                    part_ref[k] = flat[pl.ds(begin, chunk), :]

    def whole(shape):
        return pl.BlockSpec(shape, lambda j, m: (0, 0))

    def by_step(rows, columns):
        return pl.BlockSpec((rows, columns), lambda j, m: (j, 0))

    return pl.pallas_call(
        kernel,
        grid_spec=pltpu.PrefetchScalarGridSpec(
            num_scalar_prefetch=1,
            grid=(steps,),
            in_specs=[by_step(run, LANES)] * groups
            + [whole((tall, width)), whole((1, width))] * 2
            + [by_step(2 * run, width)],
            out_specs=[by_step(2 * run, width)]
            + [by_step(run, LANES)] * groups
            + [pl.BlockSpec((groups, chunk, width), lambda j, m: (0, 0, 0))] * 2,
            scratch_shapes=[
                pltpu.VMEM((groups, run, LANES), jnp.float32),
                pltpu.VMEM((groups, run, LANES), jnp.float32),
                pltpu.VMEM((width, tall), jnp.float32),
                pltpu.VMEM((width, tall), jnp.float32),
                pltpu.VMEM((8, width), jnp.float32),
                pltpu.VMEM((2 * groups * chunk, width), jnp.bfloat16),
            ],
        ),
        out_shape=[jax.ShapeDtypeStruct((items, width), jnp.bfloat16)]
        + [jax.ShapeDtypeStruct((items // 2, LANES), jnp.bfloat16)] * groups
        + [jax.ShapeDtypeStruct((groups, chunk, width), jnp.bfloat16)] * 2,
        compiler_params=pltpu.CompilerParams(vmem_limit_bytes=48 * MIB),
        name="both_layers",
    )(
        me,
        *blocks,
        weight_one,
        gain_one.reshape(1, width),
        weight_two,
        gain_two.reshape(1, width),
        grad_out,
    )


def after(values, *first):
    return lax.optimization_barrier((values, *first))[0]


def column_plan(shard_of, offsets, table, weight_one, gain_one, weight_two, gain_two, grad_out):
    sessions, length, _ = shard_of.shape
    tables, rows_dev, width = table.shape
    items = sessions * length
    groups = lax.axis_size("dp")
    shards = lax.axis_size("table")
    planes = shards // 2
    half = rows_dev // 2
    run = 2 * length
    me = lax.axis_index("dp")
    plane, core = lax.axis_index("table") // 2, lax.axis_index("table") % 2
    at = jnp.stack([me, core]).astype(jnp.int32)

    def dp_shift(values, k):
        return lax.ppermute(values, "dp", [(i, (i + k) % groups) for i in range(groups)])

    def table_shift(values, k):
        return lax.ppermute(values, "table", [(i, (i + k) % shards) for i in range(shards)])

    def up(values):
        return table_shift(values, 2)

    def down(values):
        return table_shift(values, -2)

    def plane_flip(values, k):
        return lax.ppermute(values, "table", [(i, i ^ (2 * k)) for i in range(shards)])

    def across(values):
        return lax.ppermute(values, "table", [(i, i ^ 1) for i in range(shards)])

    slot = (shard_of + core) % 2 * planes + (shard_of // 2 - plane + planes) % planes
    places = jnp.stack(
        [slot * rows_dev + offsets, slot * rows_dev + (offsets + half) % rows_dev], axis=0
    ).astype(jnp.int32)
    places = places.reshape(2, items // (2 * run), 2, run, tables)
    mine = jnp.stack([places[0, :, 0], places[1, :, 1]], axis=0)
    mine = jnp.transpose(mine, (3, 0, 1, 2)).reshape(tables, 2, items // 2)

    first, last, own = own_columns(at, table)
    mine = after(mine, own)
    all_codes = jnp.concatenate([mine] + [dp_shift(mine, k) for k in range(1, groups)], axis=2)
    codes = [(all_codes[t, 0], all_codes[t, 1]) for t in range(tables)]

    def from_planes(own, first=None):
        near = [None] * planes
        rising = falling = own
        for k in range(1, planes // 2 + 1):
            if first is not None and k == planes // 2:
                rising = after(rising, first)
            near[planes - k] = rising = up(rising)
            if k <= (planes - 1) // 2:
                near[k] = falling = down(falling)
        return near[1:]

    near_first = from_planes(first)
    swapped = across(after(own, all_codes))
    last = after(last, swapped, near_first[0], near_first[-1])
    far_first = [across(values) for values in near_first]

    def slots(t, near, far, place):
        return [(own, t), *((v, place) for v in near), (swapped, t), *((v, place) for v in far)]

    total = look_up(codes[0], slots(0, near_first, far_first, 0), None, False)
    near_last = from_planes(last, total)
    for t in range(1, tables - 1):
        total = look_up(codes[t], slots(t, near_first, far_first, t), total, False)
    near_last[planes // 2 - 1] = after(near_last[planes // 2 - 1], total)
    far_last = [across(values) for values in near_last]
    total = look_up(codes[tables - 1], slots(tables - 1, near_last, far_last, 0), total, True)

    pieces = total.reshape(groups, items // 2, LANES)
    arrived = [pieces[0]] + [dp_shift(pieces[k], -k) for k in range(1, groups)]
    done = both_layers(
        at, arrived, weight_one, gain_one, weight_two, gain_two, grad_out.reshape(items, width), length
    )
    block_out = done[0].reshape(sessions, length, width)
    sent, kept, given = done[1 : 1 + groups], done[1 + groups], done[2 + groups]
    blocks = [sent[0]] + [dp_shift(sent[k], k) for k in range(1, groups)]

    def add_up(parts):
        return sum(part.astype(jnp.float32) for part in parts)

    got = across(given)
    chunks = [kept[k].astype(jnp.float32) + got[k].astype(jnp.float32) for k in range(groups)]
    chunks = [chunks[0]] + [dp_shift(chunk.astype(jnp.bfloat16), k) for k, chunk in enumerate(chunks[1:], 1)]

    def send_on(state):
        sent = []
        for side, move in (("up", up), ("down", down)):
            terms, came = state[side], state["came"].pop(side, None)
            if terms:
                value = terms.pop(0)
                if came is not None:
                    value = value + came.astype(jnp.float32)
                sent.append(value.astype(jnp.bfloat16))
                state["came"][side] = move(sent[-1])
            elif came is not None:
                state["home"] = state["home"] + came.astype(jnp.float32)
        return sent

    states = []
    sums = add_rows(codes, blocks, shards, half)
    chunk = add_up([after(part, sums[0][1]) for part in chunks]).astype(jnp.bfloat16)
    got = None
    for near, far in sums:
        got = across(far) if got is None else across(after(far, got))
        if not states:
            got = after(got, chunk)
        sides = [near[r].astype(jnp.float32) + got[r].astype(jnp.float32) for r in range(planes)]
        states.append(
            {
                "home": sides[0],
                "up": [sides[r] for r in range(planes // 2, 0, -1)],
                "down": [sides[r] for r in range(planes // 2 + 1, planes)],
                "came": {},
            }
        )
        send_on(states[-1])
    sent = [state["came"]["up"] for state in states]
    while any(state["came"] for state in states):
        for state in states:
            send_on(state)
    grads = [
        jnp.concatenate([state["home"][:, : LANES // 2], state["home"][:, LANES // 2 :]], axis=0)
        for state in states
    ]
    table_grad = jnp.stack(grads, axis=0)

    for k in range((planes - 1).bit_length()):
        chunk = add_up([chunk, after(plane_flip(chunk, 2**k), sent[min(k, tables - 1)])]).astype(jnp.bfloat16)
    near = jnp.stack([chunk] + [dp_shift(chunk, k) for k in range(1, groups)], axis=0)
    far = across(near)
    sums = scaled_sums(
        at, near, far, weight_one.shape[0], 1.0 / math.sqrt(items * groups * shards)
    )
    return (block_out, sums[0], sums[1], sums[2].reshape(width), sums[3].reshape(width), table_grad)


def solution(mesh):
    placed = (
        P(("dp", "table"), None, None),
        P(("dp", "table"), None, None),
        P(None, "table", None),
        P(),
        P(),
        P(),
        P(),
        P(("dp", "table"), None, None),
    )

    def on_device(shard_of, offsets, table, *rest):
        fits = columns_fit(shard_of.shape, table.shape, mesh.shape["dp"], mesh.shape["table"])
        plan = column_plan if fits else padded_plan
        return plan(shard_of, offsets, table, *rest)

    return jax.shard_map(
        on_device,
        mesh=mesh,
        in_specs=placed,
        out_specs=(P(("dp", "table"), None, None), P(), P(), P(), P(), P(None, "table", "dp")),
        check_vma=False,
    )
```

```python
import math

import jax
import jax.numpy as jnp
from jax import lax
from jax.experimental import pallas as pl
from jax.experimental.pallas import tpu as pltpu
from jax.sharding import PartitionSpec as P

GELU_C = 0.7978845608028654
GELU_K = 0.044715
LANES = 128
MIB = 2**20

UNROLL = 16
ROWS = 40


def shifted(values, spacing):
    return jnp.pad(values, ((0, 0), (spacing, 0), (0, 0)))[:, : values.shape[1], :]


def unshifted(values, spacing):
    return jnp.pad(values, ((0, 0), (0, spacing), (0, 0)))[:, spacing:, :]


def stack_taps(values, spacing):
    return jnp.concatenate(
        [values, shifted(values, spacing), shifted(values, 2 * spacing)], axis=-1
    )


def gelu_parts(inputs):
    inner = GELU_C * (inputs + GELU_K * inputs * inputs * inputs)
    tangent = jnp.tanh(inner)
    output = 0.5 * inputs * (1.0 + tangent)
    slope = 0.5 * (1.0 + tangent) + 0.5 * inputs * (1.0 - tangent * tangent) * GELU_C * (
        1.0 + 3.0 * GELU_K * inputs * inputs
    )
    return (output, slope)


def layer_forward(values, weight, gain, spacing):
    sessions, length, width = values.shape
    stacked = stack_taps(values, spacing).reshape(sessions * length, 3 * width)
    before_norm = jnp.dot(stacked, weight, preferred_element_type=jnp.float32)
    centred = before_norm - jnp.mean(before_norm, axis=-1, keepdims=True)
    inv_std = lax.rsqrt(jnp.mean(centred * centred, axis=-1, keepdims=True) + 1e-05)
    normal = centred * inv_std
    output, slope = gelu_parts(normal * gain)
    return (output, (stacked, normal, inv_std, slope))


def layer_backward(grad_output, weight, gain, saved, spacing, sessions, length):
    stacked, normal, inv_std, slope = saved
    width = weight.shape[1]
    grad_scaled = grad_output * slope
    grad_gain = jnp.sum(grad_scaled * normal, axis=0)
    grad_normal = grad_scaled * gain
    grad_before = inv_std * (
        grad_normal
        - jnp.mean(grad_normal, axis=-1, keepdims=True)
        - normal * jnp.mean(grad_normal * normal, axis=-1, keepdims=True)
    )
    grad_before = grad_before.astype(jnp.bfloat16)
    grad_weight = lax.dot_general(
        stacked, grad_before, (((0,), (0,)), ((), ())), preferred_element_type=jnp.float32
    )
    grad_taps = lax.dot_general(
        grad_before, weight, (((1,), (1,)), ((), ())), preferred_element_type=jnp.float32
    ).reshape(sessions, length, 3 * width)
    grad_input = (
        grad_taps[..., :width]
        + unshifted(grad_taps[..., width : 2 * width], spacing)
        + unshifted(grad_taps[..., 2 * width :], 2 * spacing)
    )
    return (grad_input, grad_weight, grad_gain)


def to_owners(grad_rows, slot_place, shards, slot_count, width):
    outgoing = (
        jnp.zeros((shards * slot_count, width), jnp.bfloat16)
        .at[slot_place]
        .set(grad_rows)
        .reshape(shards, slot_count, width)
    )
    return lax.all_to_all(outgoing, "table", split_axis=0, concat_axis=0, tiled=True)


def padded_plan(shard_of, offsets, table, weight_one, gain_one, weight_two, gain_two, grad_out):
    sessions, length, _ = shard_of.shape
    width = table.shape[2]
    rows_dev = table.shape[1]
    item_count = sessions * length
    shards = lax.axis_size("table")
    groups = lax.axis_size("dp")
    quarter = width // groups
    slot_count = 8 * ((6 * item_count + 8 * shards - 1) // (8 * shards))
    target = shard_of.reshape(-1)
    table_pick = jnp.tile(jnp.arange(3, dtype=jnp.int32), item_count)
    row_codes = table_pick * rows_dev + offsets.reshape(-1)
    onehot = (jnp.arange(shards, dtype=jnp.int32)[:, None] == target[None, :]).astype(jnp.int32)
    before = jnp.cumsum(onehot, axis=1) - onehot
    slot_rank = jnp.sum(before * onehot, axis=0)
    slot_place = target * slot_count + slot_rank
    requests = (
        jnp.full((shards * slot_count,), -1, jnp.int32)
        .at[slot_place]
        .set(row_codes)
        .reshape(shards, slot_count)
    )
    table_flat = table.reshape(3 * rows_dev, width)
    asked_rows = lax.all_to_all(requests, "table", split_axis=0, concat_axis=0, tiled=True)
    found_rows = jnp.take(table_flat, jnp.maximum(asked_rows, 0), axis=0)
    found_rows = jnp.where((asked_rows >= 0)[..., None], found_rows, jnp.zeros((), jnp.bfloat16))
    sent_back = lax.all_to_all(found_rows, "table", split_axis=0, concat_axis=0, tiled=True)
    picked = jnp.take(sent_back.reshape(shards * slot_count, width), slot_place, axis=0).reshape(
        item_count, 3, width
    )
    embedded = (
        jnp.sum(picked.astype(jnp.float32), axis=1)
        .astype(jnp.bfloat16)
        .reshape(sessions, length, width)
    )
    act_one, saved_one = layer_forward(embedded, weight_one, gain_one, 1)
    hidden = act_one.astype(jnp.bfloat16).reshape(sessions, length, width)
    act_two, saved_two = layer_forward(hidden, weight_two, gain_two, 2)
    block_out = (
        (embedded.reshape(item_count, width).astype(jnp.float32) + act_two)
        .astype(jnp.bfloat16)
        .reshape(sessions, length, width)
    )
    grad_top = grad_out.reshape(item_count, width).astype(jnp.float32)
    scale = 1.0 / math.sqrt(item_count * groups * shards)
    grad_hidden, second_weights, second_gains = layer_backward(
        grad_top, weight_two, gain_two, saved_two, 2, sessions, length
    )
    grad_inner, first_weights, first_gains = layer_backward(
        grad_hidden.reshape(item_count, width), weight_one, gain_one, saved_one, 1, sessions, length
    )
    grad_embed = (grad_top + grad_inner.reshape(item_count, width)).astype(jnp.bfloat16)
    repeated = jnp.repeat(grad_embed, 3, axis=0)
    arrived = to_owners(repeated, slot_place, shards, slot_count, width)
    dense_grad = (
        jnp.zeros((3 * rows_dev, width), jnp.float32)
        .at[jnp.maximum(asked_rows, 0).reshape(-1)]
        .add(arrived.reshape(-1, width).astype(jnp.float32))
    )
    table_grad = lax.psum_scatter(
        dense_grad.astype(jnp.bfloat16), "dp", scatter_dimension=1, tiled=True
    ).astype(jnp.float32)
    table_grad = table_grad.reshape(3, rows_dev, quarter)
    totals = lax.psum((first_weights, second_weights, first_gains, second_gains), ("dp", "table"))
    return (
        block_out,
        totals[0] * scale,
        totals[1] * scale,
        totals[2] * scale,
        totals[3] * scale,
        table_grad,
    )


VMEM = pl.BlockSpec(memory_space=pltpu.VMEM)


def columns_fit(items_shape, table_shape, groups, shards):
    sessions, length, _ = items_shape
    _, rows_dev, width = table_shape
    run = 2 * length
    return (
        2 * width == groups * LANES
        and groups > 1
        and (groups & (groups - 1)) == 0
        and sessions % 4 == 0
        and run % 16 == 0
        and run % ROWS == 0
        and (groups * sessions * length // 2) % (4 * UNROLL) == 0
        and rows_dev % 32 == 0
        and 4 * shards * rows_dev * LANES * 4 <= 40 * MIB
        and table_shape[0] == 3
        and shards == 8
    )


def low_lanes(rows):
    return lax.broadcasted_iota(jnp.int32, (rows, LANES), 1) < LANES // 2


def swap_halves(values):
    return pltpu.roll(values, LANES // 2, 1)


def own_columns(at, table):
    tables, rows_dev, _ = table.shape
    half = rows_dev // 2

    def kernel(at_ref, table_ref, first_ref, last_ref, all_ref):
        odd = at_ref[0] % 2 == 1
        low = low_lanes(half)
        for t in range(tables):
            top = table_ref[t, :half, :].astype(jnp.float32)
            bottom = table_ref[t, half:, :].astype(jnp.float32)
            in_low = jnp.where(odd, swap_halves(top), top)
            in_high = jnp.where(odd, bottom, swap_halves(bottom))
            values = jnp.where(low, in_low, in_high).astype(jnp.bfloat16)
            if t < tables - 1:
                first_ref[t] = values
            else:
                last_ref[0] = values
            all_ref[t] = values

    def whole(count):
        return pl.BlockSpec((count, half, LANES), lambda i, m: (0, 0, 0))

    return pl.pallas_call(
        kernel,
        grid_spec=pltpu.PrefetchScalarGridSpec(
            num_scalar_prefetch=1,
            grid=(1,),
            in_specs=[pl.BlockSpec((tables, rows_dev, LANES), lambda i, m: (0, 0, m[0] // 2))],
            out_specs=[whole(tables - 1), whole(1), whole(tables)],
        ),
        out_shape=[
            jax.ShapeDtypeStruct((count, half, LANES), jnp.bfloat16)
            for count in (tables - 1, 1, tables)
        ],
        compiler_params=pltpu.CompilerParams(vmem_limit_bytes=24 * MIB),
        name="own_columns",
    )(at, table)


def look_up(codes, slots, total, last):
    count = codes[0].shape[0]
    half = slots[0][0].shape[1]

    def kernel(low_ref, high_ref, *refs):
        slot_refs, refs = refs[: len(slots)], refs[len(slots) :]
        total_ref = None if total is None else refs[0]
        out_ref, rows, found = refs[-3:]
        for s, slot_ref in enumerate(slot_refs):
            values = slot_ref[0].astype(jnp.float32)
            rows[pl.ds(2 * s * half, half), :] = values
            rows[pl.ds((2 * s + 1) * half, half), :] = swap_halves(values)
        low = low_lanes(1)

        def some(step, carry):
            for j in range(16):
                i = step * 16 + j
                for_low = rows[pl.ds(low_ref[i], 1), :]
                for_high = rows[pl.ds(high_ref[i], 1), :]
                found[pl.ds(i, 1), :] = jnp.where(low, for_low, for_high)
            return carry

        lax.fori_loop(0, count // 16, some, 0)
        result = found[...]
        if total_ref is not None:
            result = result + total_ref[...]
        out_ref[...] = result.astype(out_ref.dtype)

    def part(at):
        return pl.BlockSpec((1, half, LANES), lambda i, *codes: (at, 0, 0))

    operands = [slot[0] for slot in slots] + ([] if total is None else [total])
    whole = pl.BlockSpec((count, LANES), lambda i, *codes: (0, 0))
    return pl.pallas_call(
        kernel,
        grid_spec=pltpu.PrefetchScalarGridSpec(
            num_scalar_prefetch=2,
            grid=(1,),
            in_specs=[part(slot[1]) for slot in slots] + ([] if total is None else [whole]),
            out_specs=whole,
            scratch_shapes=[
                pltpu.VMEM((2 * len(slots) * half, LANES), jnp.float32),
                pltpu.VMEM((count, LANES), jnp.float32),
            ],
        ),
        out_shape=jax.ShapeDtypeStruct((count, LANES), jnp.bfloat16 if last else jnp.float32),
        compiler_params=pltpu.CompilerParams(vmem_limit_bytes=32 * MIB),
        cost_estimate=pl.CostEstimate(
            flops=0, bytes_accessed=8 * 3 * count * LANES * 4, transcendentals=0
        ),
        name="look_up",
    )(*codes, *operands)


def add_rows(codes, blocks, shards, half, chains):
    tables = len(codes)
    count = codes[0][0].shape[0]
    per = blocks[0].shape[0]
    planes = shards // 2

    def kernel(*refs):
        code_refs, refs = refs[: 2 * tables], refs[2 * tables :]
        block_refs, refs = refs[: len(blocks)], refs[len(blocks) :]
        out_refs, values, refs = refs[: 2 * tables], refs[2 * tables], refs[2 * tables + 1 :]
        sums = [refs[t * chains : (t + 1) * chains] for t in range(tables)]
        for k, block_ref in enumerate(block_refs):
            values[pl.ds(k * per, per), :] = block_ref[...].astype(jnp.float32)
        for part in refs:
            part[...] = jnp.zeros_like(part)
        low = low_lanes(1)
        high = jnp.logical_not(low)

        def some(step, carry):
            for j in range(UNROLL):
                ready = []
                for c in range(chains):
                    i = c * (count // chains) + step * UNROLL + j
                    value = values[pl.ds(i, 1), :]
                    for t in range(tables):
                        part = sums[t][c]
                        to_low, to_high = pl.ds(code_refs[2 * t][i], 1), pl.ds(code_refs[2 * t + 1][i], 1)
                        ready.append(
                            (part, to_low, part[to_low, :] + value, to_high, part[to_high, :] + value)
                        )
                for part, to_low, in_low, to_high, in_high in ready:
                    pltpu.store(part.at[to_low, :], in_low, mask=low)
                    pltpu.store(part.at[to_high, :], in_high, mask=high)
            return carry

        lax.fori_loop(0, count // (chains * UNROLL), some, 0)
        for t in range(tables):
            for s in range(shards):
                straight = sum(part[pl.ds(2 * s * half, half), :] for part in sums[t])
                crossed = sum(part[pl.ds((2 * s + 1) * half, half), :] for part in sums[t])
                result = (straight + swap_halves(crossed)).astype(jnp.bfloat16)
                out_refs[2 * t + s // planes][s % planes] = result

    results = pl.pallas_call(
        kernel,
        grid_spec=pltpu.PrefetchScalarGridSpec(
            num_scalar_prefetch=2 * tables,
            grid=(),
            in_specs=[VMEM] * len(blocks),
            out_specs=[VMEM] * (2 * tables),
            scratch_shapes=[pltpu.VMEM((count, LANES), jnp.float32)]
            + [pltpu.VMEM((2 * shards * half, LANES), jnp.float32)] * (tables * chains),
        ),
        out_shape=[jax.ShapeDtypeStruct((planes, half, LANES), jnp.bfloat16)] * (2 * tables),
        compiler_params=pltpu.CompilerParams(vmem_limit_bytes=56 * MIB),
        cost_estimate=pl.CostEstimate(
            flops=0, bytes_accessed=tables * 40 * MIB, transcendentals=0
        ),
        name="add_rows",
    )(*[part for pair in codes for part in pair], *blocks)
    return list(zip(results[::2], results[1::2]))


def finished(parts, tables, earlier):
    _, half, lanes = parts[0][0].shape
    count = len(parts)
    begin = 0 if earlier is None else tables - count

    def kernel(*refs):
        refs, out_ref = refs[:-1], refs[-1]
        for t in range(count):
            total = sum(ref[...].reshape(half, lanes).astype(jnp.float32) for ref in refs[4 * t : 4 * t + 4])
            turned = total.T
            out_ref[t, :, :half] = turned[: lanes // 2]
            out_ref[t, :, half:] = turned[lanes // 2 :]

    own = pl.BlockSpec((1, half, lanes), lambda i: (0, 0, 0))

    def row_block(n):
        return pl.BlockSpec((half, lanes), lambda i: (n, 0))

    operands, specs = [], []
    for near, got, down, last, n in parts:
        operands += [near, got, down, last]
        specs += [own, own, row_block(0), row_block(n)]
    if earlier is not None:
        operands.append(earlier)
        specs.append(pl.BlockSpec(memory_space=pl.ANY))
    return pl.pallas_call(
        kernel,
        grid=(1,),
        in_specs=specs,
        out_specs=pl.BlockSpec((count, lanes // 2, 2 * half), lambda i: (begin // count, 0, 0)),
        out_shape=jax.ShapeDtypeStruct((tables, lanes // 2, 2 * half), jnp.float32),
        input_output_aliases={} if earlier is None else {len(operands) - 1: 0},
        compiler_params=pltpu.CompilerParams(vmem_limit_bytes=32 * MIB),
        name="finished",
    )(*operands)


def weight_chunk(tall, groups):
    return -(-(2 * tall + 16) // (32 * groups)) * 16


def scaled_sums(at, near, far, tall, scale):
    groups, chunk, width = near.shape

    def kernel(at_ref, near_ref, far_ref, one_ref, two_ref, gain_one_ref, gain_two_ref, flat):
        me, core = at_ref[0], at_ref[1]
        for k in range(groups):
            for part_ref, side in ((near_ref, core), (far_ref, 1 - core)):
                begin = pl.multiple_of((side * groups + (me ^ k)) * chunk, 16)
                flat[pl.ds(begin, chunk), :] = part_ref[k].astype(jnp.float32) * scale
        one_ref[...] = flat[:tall, :]
        two_ref[...] = flat[tall : 2 * tall, :]
        gain_one_ref[...] = flat[2 * tall : 2 * tall + 1, :]
        gain_two_ref[...] = flat[2 * tall + 1 : 2 * tall + 2, :]

    return pl.pallas_call(
        kernel,
        grid_spec=pltpu.PrefetchScalarGridSpec(
            num_scalar_prefetch=1,
            grid=(),
            in_specs=[VMEM] * 2,
            out_specs=[VMEM] * 4,
            scratch_shapes=[pltpu.VMEM((2 * groups * chunk, width), jnp.float32)],
        ),
        out_shape=[jax.ShapeDtypeStruct((tall, width), jnp.float32)] * 2
        + [jax.ShapeDtypeStruct((1, width), jnp.float32)] * 2,
        compiler_params=pltpu.CompilerParams(vmem_limit_bytes=16 * MIB),
        name="scaled_sums",
    )(at, near, far)


def both_layers(me, blocks, weight_one, gain_one, weight_two, gain_two, grad_out, length):
    groups = len(blocks)
    items, width = grad_out.shape
    run = 2 * length
    steps = items // (2 * run)
    tall = weight_one.shape[0]
    chunk = weight_chunk(tall, groups)

    def kernel(me_ref, *refs):
        block_refs, refs = refs[:groups], refs[groups:]
        w_one_ref, g_one_ref, w_two_ref, g_two_ref, top_ref, out_ref, *refs = refs
        grad_refs, refs = refs[:groups], refs[groups:]
        kept_ref, given_ref, held, packed, sum_one, sum_two, sum_gains, flat, turned_one, turned_two = refs
        step = pl.program_id(0)
        me_at, core = me_ref[0], me_ref[1]
        low = low_lanes(run)
        place = lax.broadcasted_iota(jnp.int32, (run, width), 0)
        place = jnp.where(place >= length, place - length, place)

        @pl.when(step == 0)
        def _():
            sum_one[...] = jnp.zeros_like(sum_one)
            sum_two[...] = jnp.zeros_like(sum_two)
            sum_gains[...] = jnp.zeros_like(sum_gains)
            for weight_ref, turned_ref in ((w_one_ref, turned_one), (w_two_ref, turned_two)):
                for k in range(tall // width):
                    at = slice(k * width, (k + 1) * width)
                    turned_ref[at, :] = weight_ref[at, :].T

        def taps(values, gap):
            one = jnp.where(place >= gap, pltpu.roll(values, gap, 0), 0.0)
            two = jnp.where(place >= 2 * gap, pltpu.roll(values, 2 * gap, 0), 0.0)
            return jnp.concatenate([x.astype(jnp.bfloat16) for x in (values, one, two)], axis=1)

        def untaps(values, gap):
            one = jnp.where(place < length - gap, pltpu.roll(values, run - gap, 0), 0.0)
            two = jnp.where(place < length - 2 * gap, pltpu.roll(values, run - 2 * gap, 0), 0.0)
            return [x.astype(jnp.bfloat16) for x in (values, one, two)]

        def by_rows(work, *arrays):
            parts = [work(*(a[r : r + ROWS] for a in arrays)) for r in range(0, run, ROWS)]
            return [jnp.concatenate(values, axis=0) for values in zip(*parts)]

        def activate(before, gain):
            centred = before - jnp.mean(before, axis=-1, keepdims=True)
            inv_std = lax.rsqrt(jnp.mean(centred * centred, axis=-1, keepdims=True) + 1e-05)
            normal = centred * inv_std
            inputs = normal * gain
            square = inputs * inputs
            part = 0.5 + 0.5 * jnp.tanh(inputs * (GELU_C + GELU_C * GELU_K * square))
            slope = part + inputs * (part - part * part) * (
                2.0 * GELU_C + 6.0 * GELU_C * GELU_K * square
            )
            return normal, inv_std, inputs * part, slope

        def unwind(grad, normal, inv_std, slope, gain, row):
            scaled = grad * slope
            sum_gains[row] += jnp.sum((scaled * normal).reshape(-1, 8, width), axis=0)
            back = scaled * gain
            before = inv_std * (
                back
                - jnp.mean(back, axis=-1, keepdims=True)
                - normal * jnp.mean(back * normal, axis=-1, keepdims=True)
            )
            return before.astype(jnp.bfloat16).astype(jnp.float32)

        def products(before, values, turned_ref, gap, total):
            stacked = jnp.concatenate(untaps(before, gap), axis=1)
            total[...] += lax.dot_general(
                values.astype(jnp.bfloat16),
                stacked,
                (((0,), (0,)), ((), ())),
                preferred_element_type=jnp.float32,
            )
            return jnp.dot(stacked, turned_ref[...], preferred_element_type=jnp.float32)

        for k in range(groups):
            held[k] = block_refs[k][...].astype(jnp.float32)
        gain_one_at, gain_two_at = g_one_ref[...], g_two_ref[...]
        back_to = [None, None]

        def one_side(side):
            columns = []
            for q in range(0, groups, 2):
                left = held[q ^ me_at]
                right = held[(q + 1) ^ me_at]
                if side == 0:
                    columns.append(jnp.where(low, left, swap_halves(right)))
                else:
                    columns.append(jnp.where(low, swap_halves(left), right))
            embedded = jnp.concatenate(columns, axis=1)
            rows = pl.ds(side * run, run)
            top = top_ref[rows, :].astype(jnp.float32)
            stacked = taps(embedded, 1)
            yield
            before = jnp.dot(stacked, w_one_ref[...], preferred_element_type=jnp.float32)
            yield

            def first(before):
                normal, inv_std, output, slope = activate(before, gain_one_at)
                return normal, inv_std, output.astype(jnp.bfloat16).astype(jnp.float32), slope

            normal, inv_std, hidden, slope = by_rows(first, before)
            stacked = taps(hidden, 2)
            yield
            before = jnp.dot(stacked, w_two_ref[...], preferred_element_type=jnp.float32)
            yield

            def second(before, values, grad):
                normal, inv_std, output, slope = activate(before, gain_two_at)
                return values + output, unwind(grad, normal, inv_std, slope, gain_two_at, 1)

            output, before = by_rows(second, before, embedded, top)
            out_ref[rows, :] = output.astype(jnp.bfloat16)
            yield
            grad = products(before, hidden, turned_two, 2, sum_two)
            yield

            def third(grad, normal, inv_std, slope):
                return (unwind(grad, normal, inv_std, slope, gain_one_at, 0),)

            (before,) = by_rows(third, grad, normal, inv_std, slope)
            yield
            back_to[side] = top + products(before, embedded, turned_one, 1, sum_one)

        sides = [one_side(0), one_side(1)]
        next(sides[0])
        while sides:
            for one in sides[::-1]:
                if next(one, "done") == "done":
                    sides.remove(one)

        for q in range(groups):
            at = slice((q // 2) * LANES, (q // 2 + 1) * LANES)
            first, second = back_to[0][:, at], back_to[1][:, at]
            if q % 2 == 0:
                pair = jnp.where(low, first, swap_halves(second))
            else:
                pair = jnp.where(low, swap_halves(first), second)
            packed[q ^ me_at] = pair
        for k in range(groups):
            grad_refs[k][...] = packed[k].astype(jnp.bfloat16)

        @pl.when(step == steps - 1)
        def _():
            for n, total in enumerate((sum_one, sum_two)):
                for k in range(tall // width):
                    flat[n * tall + k * width : n * tall + (k + 1) * width, :] = total[
                        :, k * width : (k + 1) * width
                    ].astype(jnp.bfloat16)
            gains = [jnp.sum(sum_gains[n], axis=0, keepdims=True) for n in range(2)]
            flat[2 * tall : 2 * tall + 16, :] = jnp.concatenate(
                gains + [jnp.zeros((14, width), jnp.float32)], axis=0
            ).astype(jnp.bfloat16)
            if 2 * groups * chunk > 2 * tall + 16:
                flat[2 * tall + 16 :, :] = jnp.zeros(
                    (2 * groups * chunk - 2 * tall - 16, width), jnp.bfloat16
                )
            for k in range(groups):
                for part_ref, side in ((kept_ref, core), (given_ref, 1 - core)):
                    begin = pl.multiple_of((side * groups + (me_at ^ k)) * chunk, 16)
                    part_ref[k] = flat[pl.ds(begin, chunk), :]

    def whole(shape):
        return pl.BlockSpec(shape, lambda j, m: (0, 0))

    def by_step(rows, columns):
        return pl.BlockSpec((rows, columns), lambda j, m: (j, 0))

    return pl.pallas_call(
        kernel,
        grid_spec=pltpu.PrefetchScalarGridSpec(
            num_scalar_prefetch=1,
            grid=(steps,),
            in_specs=[by_step(run, LANES)] * groups
            + [whole((tall, width)), whole((1, width))] * 2
            + [by_step(2 * run, width)],
            out_specs=[by_step(2 * run, width)]
            + [by_step(run, LANES)] * groups
            + [pl.BlockSpec((groups, chunk, width), lambda j, m: (0, 0, 0))] * 2,
            scratch_shapes=[
                pltpu.VMEM((groups, run, LANES), jnp.float32),
                pltpu.VMEM((groups, run, LANES), jnp.float32),
                pltpu.VMEM((width, tall), jnp.float32),
                pltpu.VMEM((width, tall), jnp.float32),
                pltpu.VMEM((2, 8, width), jnp.float32),
                pltpu.VMEM((2 * groups * chunk, width), jnp.bfloat16),
                pltpu.VMEM((tall, width), jnp.bfloat16),
                pltpu.VMEM((tall, width), jnp.bfloat16),
            ],
        ),
        out_shape=[jax.ShapeDtypeStruct((items, width), jnp.bfloat16)]
        + [jax.ShapeDtypeStruct((items // 2, LANES), jnp.bfloat16)] * groups
        + [jax.ShapeDtypeStruct((groups, chunk, width), jnp.bfloat16)] * 2,
        compiler_params=pltpu.CompilerParams(vmem_limit_bytes=48 * MIB),
        name="both_layers",
    )(
        me,
        *blocks,
        weight_one,
        gain_one.reshape(1, width),
        weight_two,
        gain_two.reshape(1, width),
        grad_out,
    )


def together(*values):
    return lax.optimization_barrier(values)


def after(values, *first):
    return lax.optimization_barrier((values, *first))[0]


def column_plan(shard_of, offsets, table, weight_one, gain_one, weight_two, gain_two, grad_out):
    sessions, length, _ = shard_of.shape
    tables, rows_dev, width = table.shape
    items = sessions * length
    groups = lax.axis_size("dp")
    shards = lax.axis_size("table")
    planes = shards // 2
    half = rows_dev // 2
    run = 2 * length
    me = lax.axis_index("dp")
    plane, core = lax.axis_index("table") // 2, lax.axis_index("table") % 2
    at = jnp.stack([me, core]).astype(jnp.int32)

    def dp_flip(values, k):
        return lax.ppermute(values, "dp", [(i, i ^ k) for i in range(groups)])

    def table_shift(values, k):
        return lax.ppermute(values, "table", [(i, (i + k) % shards) for i in range(shards)])

    def up(values):
        return table_shift(values, 2)

    def down(values):
        return table_shift(values, -2)

    def plane_flip(values, k):
        return lax.ppermute(values, "table", [(i, i ^ (2 * k)) for i in range(shards)])

    def across(values):
        return lax.ppermute(values, "table", [(i, i ^ 1) for i in range(shards)])

    slot = (shard_of + core) % 2 * planes + (shard_of // 2 - plane + planes) % planes
    places = jnp.stack(
        [slot * rows_dev + offsets, slot * rows_dev + (offsets + half) % rows_dev], axis=0
    ).astype(jnp.int32)
    places = places.reshape(2, items // (2 * run), 2, run, tables)
    mine = jnp.stack([places[0, :, 0], places[1, :, 1]], axis=0)
    mine = jnp.transpose(mine, (3, 0, 1, 2)).reshape(tables, 2, items // 2)

    first, last, own = own_columns(at, table)
    mine = after(mine, own)
    all_codes = mine
    for k in range((groups - 1).bit_length()):
        all_codes = jnp.concatenate([all_codes, dp_flip(all_codes, 2**k)], axis=2)
    codes = [(all_codes[t, 0], all_codes[t, 1]) for t in range(tables)]

    def from_planes(own, first=None):
        near = [None] * planes
        rising = falling = own
        for k in range(1, planes // 2 + 1):
            if first is not None and k == planes // 2:
                rising = after(rising, first)
            near[planes - k] = rising = up(rising)
            if k <= (planes - 1) // 2:
                near[k] = falling = down(falling)
        return near[1:]

    near_first = from_planes(first)
    swapped = across(after(own, all_codes))
    far_first = [across(values) for values in near_first]
    last = after(last, swapped, far_first[0], far_first[-1])

    def slots(t, near, far, place):
        return [(own, t), *((v, place) for v in near), (swapped, t), *((v, place) for v in far)]

    total = look_up(codes[0], slots(0, near_first, far_first, 0), None, False)
    near_last = from_planes(last, total)
    for t in range(1, tables - 1):
        total = look_up(codes[t], slots(t, near_first, far_first, t), total, False)
    far_last = [across(after(values, total)) for values in near_last]
    total = look_up(codes[tables - 1], slots(tables - 1, near_last, far_last, 0), total, True)

    pieces = total.reshape(groups, items // 2, LANES)
    arrived = [pieces[0]] + [dp_flip(pieces[k], k) for k in range(1, groups)]
    done = both_layers(
        at, arrived, weight_one, gain_one, weight_two, gain_two, grad_out.reshape(items, width), length
    )
    block_out = done[0].reshape(sessions, length, width)
    sent, kept, given = done[1 : 1 + groups], done[1 + groups], done[2 + groups]
    blocks = [sent[0]] + [dp_flip(sent[k], k) for k in range(1, groups)]

    def add_up(parts):
        return sum(part.astype(jnp.float32) for part in parts)

    got = across(given)
    chunks = [kept[k].astype(jnp.float32) + got[k].astype(jnp.float32) for k in range(groups)]
    chunks = [chunks[0]] + [chunk.astype(jnp.bfloat16) for chunk in chunks[1:]]
    blocks = [after(block, *chunks) for block in blocks]
    chunks = [chunks[0]] + [dp_flip(chunk, k) for k, chunk in enumerate(chunks[1:], 1)]

    def side(near, got, r):
        return near[r].astype(jnp.float32) + got[r].astype(jnp.float32)

    def packed(*values):
        return jnp.concatenate([value.astype(jnp.bfloat16) for value in values], axis=0)

    (near_0, far_0), (near_1, far_1) = add_rows(codes[:2], blocks, shards, half, 2)
    far_0, *chunks = together(far_0, *chunks)
    chunk = add_up(chunks).astype(jnp.bfloat16)
    got_0 = across(far_0)
    got_1 = across(after(far_1, got_0))
    going = [
        packed(side(near_0, got_0, 2)),
        packed(side(near_0, got_0, 3)),
        packed(side(near_1, got_1, 2)),
        packed(side(near_1, got_1, 3)),
    ]
    came = [up(going[0]), down(going[1]), up(going[2]), down(going[3]), plane_flip(chunk, 1)]
    blocks = [after(block, *going, chunk) for block in blocks]
    ((near_2, far_2),) = add_rows(codes[2:], blocks, shards, half, 4)
    far_2, up_0, down_0, up_1, down_1, other = together(far_2, *came)
    got_2 = across(far_2)
    chunk = add_up([chunk, other]).astype(jnp.bfloat16)
    going = packed(
        side(near_0, got_0, 1) + up_0.astype(jnp.float32),
        side(near_1, got_1, 1) + up_1.astype(jnp.float32),
        side(near_2, got_2, 2),
    )
    last_01, down_2, other = together(
        up(going), down(packed(side(near_2, got_2, 3))), plane_flip(chunk, 2)
    )
    chunk = add_up([chunk, other]).astype(jnp.bfloat16)
    going = packed(side(near_2, got_2, 1) + last_01[2 * half :].astype(jnp.float32))
    last_2, *chunks = together(up(going), *(dp_flip(chunk, k) for k in range(1, groups)))
    near = jnp.stack([chunk, *chunks], axis=0)
    far = across(near)
    sums = scaled_sums(at, near, far, weight_one.shape[0], 1.0 / math.sqrt(items * groups * shards))

    grads = finished(
        [(near_0, got_0, down_0, last_01, 0), (near_1, got_1, down_1, last_01, 1)], tables, None
    )
    grads = finished([(near_2, got_2, down_2, last_2, 0)], tables, grads)
    table_grad = jnp.transpose(grads, (0, 2, 1))
    return (block_out, sums[0], sums[1], sums[2].reshape(width), sums[3].reshape(width), table_grad)


def solution(mesh):
    placed = (
        P(("dp", "table"), None, None),
        P(("dp", "table"), None, None),
        P(None, "table", None),
        P(),
        P(),
        P(),
        P(),
        P(("dp", "table"), None, None),
    )

    def on_device(shard_of, offsets, table, *rest):
        fits = columns_fit(shard_of.shape, table.shape, mesh.shape["dp"], mesh.shape["table"])
        plan = column_plan if fits else padded_plan
        return plan(shard_of, offsets, table, *rest)

    return jax.shard_map(
        on_device,
        mesh=mesh,
        in_specs=placed,
        out_specs=(P(("dp", "table"), None, None), P(), P(), P(), P(), P(None, "table", "dp")),
        check_vma=False,
    )
```

```python
import math

import jax
import jax.numpy as jnp
from jax import lax
from jax.experimental import pallas as pl
from jax.experimental.pallas import tpu as pltpu
from jax.sharding import PartitionSpec as P

GELU_C = 0.7978845608028654
GELU_K = 0.044715
LANES = 128
MIB = 2**20

CHAINS = 4
UNROLL = 16
ROWS = 40


def shifted(values, spacing):
    return jnp.pad(values, ((0, 0), (spacing, 0), (0, 0)))[:, : values.shape[1], :]


def unshifted(values, spacing):
    return jnp.pad(values, ((0, 0), (0, spacing), (0, 0)))[:, spacing:, :]


def stack_taps(values, spacing):
    return jnp.concatenate(
        [values, shifted(values, spacing), shifted(values, 2 * spacing)], axis=-1
    )


def gelu_parts(inputs):
    inner = GELU_C * (inputs + GELU_K * inputs * inputs * inputs)
    tangent = jnp.tanh(inner)
    output = 0.5 * inputs * (1.0 + tangent)
    slope = 0.5 * (1.0 + tangent) + 0.5 * inputs * (1.0 - tangent * tangent) * GELU_C * (
        1.0 + 3.0 * GELU_K * inputs * inputs
    )
    return (output, slope)


def layer_forward(values, weight, gain, spacing):
    sessions, length, width = values.shape
    stacked = stack_taps(values, spacing).reshape(sessions * length, 3 * width)
    before_norm = jnp.dot(stacked, weight, preferred_element_type=jnp.float32)
    centred = before_norm - jnp.mean(before_norm, axis=-1, keepdims=True)
    inv_std = lax.rsqrt(jnp.mean(centred * centred, axis=-1, keepdims=True) + 1e-05)
    normal = centred * inv_std
    output, slope = gelu_parts(normal * gain)
    return (output, (stacked, normal, inv_std, slope))


def layer_backward(grad_output, weight, gain, saved, spacing, sessions, length):
    stacked, normal, inv_std, slope = saved
    width = weight.shape[1]
    grad_scaled = grad_output * slope
    grad_gain = jnp.sum(grad_scaled * normal, axis=0)
    grad_normal = grad_scaled * gain
    grad_before = inv_std * (
        grad_normal
        - jnp.mean(grad_normal, axis=-1, keepdims=True)
        - normal * jnp.mean(grad_normal * normal, axis=-1, keepdims=True)
    )
    grad_before = grad_before.astype(jnp.bfloat16)
    grad_weight = lax.dot_general(
        stacked, grad_before, (((0,), (0,)), ((), ())), preferred_element_type=jnp.float32
    )
    grad_taps = lax.dot_general(
        grad_before, weight, (((1,), (1,)), ((), ())), preferred_element_type=jnp.float32
    ).reshape(sessions, length, 3 * width)
    grad_input = (
        grad_taps[..., :width]
        + unshifted(grad_taps[..., width : 2 * width], spacing)
        + unshifted(grad_taps[..., 2 * width :], 2 * spacing)
    )
    return (grad_input, grad_weight, grad_gain)


def to_owners(grad_rows, slot_place, shards, slot_count, width):
    outgoing = (
        jnp.zeros((shards * slot_count, width), jnp.bfloat16)
        .at[slot_place]
        .set(grad_rows)
        .reshape(shards, slot_count, width)
    )
    return lax.all_to_all(outgoing, "table", split_axis=0, concat_axis=0, tiled=True)


def padded_plan(shard_of, offsets, table, weight_one, gain_one, weight_two, gain_two, grad_out):
    sessions, length, _ = shard_of.shape
    width = table.shape[2]
    rows_dev = table.shape[1]
    item_count = sessions * length
    shards = lax.axis_size("table")
    groups = lax.axis_size("dp")
    quarter = width // groups
    slot_count = 8 * ((6 * item_count + 8 * shards - 1) // (8 * shards))
    target = shard_of.reshape(-1)
    table_pick = jnp.tile(jnp.arange(3, dtype=jnp.int32), item_count)
    row_codes = table_pick * rows_dev + offsets.reshape(-1)
    onehot = (jnp.arange(shards, dtype=jnp.int32)[:, None] == target[None, :]).astype(jnp.int32)
    before = jnp.cumsum(onehot, axis=1) - onehot
    slot_rank = jnp.sum(before * onehot, axis=0)
    slot_place = target * slot_count + slot_rank
    requests = (
        jnp.full((shards * slot_count,), -1, jnp.int32)
        .at[slot_place]
        .set(row_codes)
        .reshape(shards, slot_count)
    )
    table_flat = table.reshape(3 * rows_dev, width)
    asked_rows = lax.all_to_all(requests, "table", split_axis=0, concat_axis=0, tiled=True)
    found_rows = jnp.take(table_flat, jnp.maximum(asked_rows, 0), axis=0)
    found_rows = jnp.where((asked_rows >= 0)[..., None], found_rows, jnp.zeros((), jnp.bfloat16))
    sent_back = lax.all_to_all(found_rows, "table", split_axis=0, concat_axis=0, tiled=True)
    picked = jnp.take(sent_back.reshape(shards * slot_count, width), slot_place, axis=0).reshape(
        item_count, 3, width
    )
    embedded = (
        jnp.sum(picked.astype(jnp.float32), axis=1)
        .astype(jnp.bfloat16)
        .reshape(sessions, length, width)
    )
    act_one, saved_one = layer_forward(embedded, weight_one, gain_one, 1)
    hidden = act_one.astype(jnp.bfloat16).reshape(sessions, length, width)
    act_two, saved_two = layer_forward(hidden, weight_two, gain_two, 2)
    block_out = (
        (embedded.reshape(item_count, width).astype(jnp.float32) + act_two)
        .astype(jnp.bfloat16)
        .reshape(sessions, length, width)
    )
    grad_top = grad_out.reshape(item_count, width).astype(jnp.float32)
    scale = 1.0 / math.sqrt(item_count * groups * shards)
    grad_hidden, second_weights, second_gains = layer_backward(
        grad_top, weight_two, gain_two, saved_two, 2, sessions, length
    )
    grad_inner, first_weights, first_gains = layer_backward(
        grad_hidden.reshape(item_count, width), weight_one, gain_one, saved_one, 1, sessions, length
    )
    grad_embed = (grad_top + grad_inner.reshape(item_count, width)).astype(jnp.bfloat16)
    repeated = jnp.repeat(grad_embed, 3, axis=0)
    arrived = to_owners(repeated, slot_place, shards, slot_count, width)
    dense_grad = (
        jnp.zeros((3 * rows_dev, width), jnp.float32)
        .at[jnp.maximum(asked_rows, 0).reshape(-1)]
        .add(arrived.reshape(-1, width).astype(jnp.float32))
    )
    table_grad = lax.psum_scatter(
        dense_grad.astype(jnp.bfloat16), "dp", scatter_dimension=1, tiled=True
    ).astype(jnp.float32)
    table_grad = table_grad.reshape(3, rows_dev, quarter)
    totals = lax.psum((first_weights, second_weights, first_gains, second_gains), ("dp", "table"))
    return (
        block_out,
        totals[0] * scale,
        totals[1] * scale,
        totals[2] * scale,
        totals[3] * scale,
        table_grad,
    )


VMEM = pl.BlockSpec(memory_space=pltpu.VMEM)


def columns_fit(items_shape, table_shape, groups, shards):
    sessions, length, _ = items_shape
    _, rows_dev, width = table_shape
    run = 2 * length
    return (
        2 * width == groups * LANES
        and groups > 1
        and (groups & (groups - 1)) == 0
        and sessions % 4 == 0
        and run % 16 == 0
        and run % ROWS == 0
        and (groups * sessions * length // 2) % (4 * UNROLL) == 0
        and rows_dev % 32 == 0
        and 4 * shards * rows_dev * LANES * 4 <= 40 * MIB
        and table_shape[0] == 3
        and shards == 8
    )


def low_lanes(rows):
    return lax.broadcasted_iota(jnp.int32, (rows, LANES), 1) < LANES // 2


def swap_halves(values):
    return pltpu.roll(values, LANES // 2, 1)


def own_columns(at, table):
    tables, rows_dev, _ = table.shape
    half = rows_dev // 2

    def kernel(at_ref, table_ref, first_ref, last_ref, all_ref):
        odd = at_ref[0] % 2 == 1
        low = low_lanes(half)
        for t in range(tables):
            top = table_ref[t, :half, :].astype(jnp.float32)
            bottom = table_ref[t, half:, :].astype(jnp.float32)
            in_low = jnp.where(odd, swap_halves(top), top)
            in_high = jnp.where(odd, bottom, swap_halves(bottom))
            values = jnp.where(low, in_low, in_high).astype(jnp.bfloat16)
            if t < tables - 1:
                first_ref[t] = values
            else:
                last_ref[0] = values
            all_ref[t] = values

    def whole(count):
        return pl.BlockSpec((count, half, LANES), lambda i, m: (0, 0, 0))

    return pl.pallas_call(
        kernel,
        grid_spec=pltpu.PrefetchScalarGridSpec(
            num_scalar_prefetch=1,
            grid=(1,),
            in_specs=[pl.BlockSpec((tables, rows_dev, LANES), lambda i, m: (0, 0, m[0] // 2))],
            out_specs=[whole(tables - 1), whole(1), whole(tables)],
        ),
        out_shape=[
            jax.ShapeDtypeStruct((count, half, LANES), jnp.bfloat16)
            for count in (tables - 1, 1, tables)
        ],
        compiler_params=pltpu.CompilerParams(vmem_limit_bytes=24 * MIB),
        name="own_columns",
    )(at, table)


def look_up(codes, slots, total, last):
    count = codes[0].shape[0]
    half = slots[0][0].shape[1]

    def kernel(low_ref, high_ref, *refs):
        slot_refs, refs = refs[: len(slots)], refs[len(slots) :]
        total_ref = None if total is None else refs[0]
        out_ref, rows, found = refs[-3:]
        for s, slot_ref in enumerate(slot_refs):
            values = slot_ref[0].astype(jnp.float32)
            rows[pl.ds(2 * s * half, half), :] = values
            rows[pl.ds((2 * s + 1) * half, half), :] = swap_halves(values)
        low = low_lanes(1)

        def some(step, carry):
            for j in range(16):
                i = step * 16 + j
                for_low = rows[pl.ds(low_ref[i], 1), :]
                for_high = rows[pl.ds(high_ref[i], 1), :]
                found[pl.ds(i, 1), :] = jnp.where(low, for_low, for_high)
            return carry

        lax.fori_loop(0, count // 16, some, 0)
        result = found[...]
        if total_ref is not None:
            result = result + total_ref[...]
        out_ref[...] = result.astype(out_ref.dtype)

    def part(at):
        return pl.BlockSpec((1, half, LANES), lambda i, *codes: (at, 0, 0))

    operands = [slot[0] for slot in slots] + ([] if total is None else [total])
    whole = pl.BlockSpec((count, LANES), lambda i, *codes: (0, 0))
    return pl.pallas_call(
        kernel,
        grid_spec=pltpu.PrefetchScalarGridSpec(
            num_scalar_prefetch=2,
            grid=(1,),
            in_specs=[part(slot[1]) for slot in slots] + ([] if total is None else [whole]),
            out_specs=whole,
            scratch_shapes=[
                pltpu.VMEM((2 * len(slots) * half, LANES), jnp.float32),
                pltpu.VMEM((count, LANES), jnp.float32),
            ],
        ),
        out_shape=jax.ShapeDtypeStruct((count, LANES), jnp.bfloat16 if last else jnp.float32),
        compiler_params=pltpu.CompilerParams(vmem_limit_bytes=20 * MIB),
        cost_estimate=pl.CostEstimate(
            flops=0, bytes_accessed=8 * 3 * count * LANES * 4, transcendentals=0
        ),
        name="look_up",
    )(*codes, *operands)


def add_rows(codes, blocks, shards, half, chains):
    tables = len(codes)
    count = codes[0][0].shape[0]
    per = blocks[0].shape[0]
    planes = shards // 2

    def kernel(*refs):
        code_refs, refs = refs[: 2 * tables], refs[2 * tables :]
        block_refs, refs = refs[: len(blocks)], refs[len(blocks) :]
        out_refs, values, refs = refs[: 2 * tables], refs[2 * tables], refs[2 * tables + 1 :]
        sums = [refs[t * chains : (t + 1) * chains] for t in range(tables)]
        for k, block_ref in enumerate(block_refs):
            values[pl.ds(k * per, per), :] = block_ref[...].astype(jnp.float32)
        for part in refs:
            part[...] = jnp.zeros_like(part)
        low = low_lanes(1)
        high = jnp.logical_not(low)

        def some(step, carry):
            for j in range(UNROLL):
                ready = []
                for c in range(chains):
                    i = c * (count // chains) + step * UNROLL + j
                    value = values[pl.ds(i, 1), :]
                    for t in range(tables):
                        part = sums[t][c]
                        to_low, to_high = pl.ds(code_refs[2 * t][i], 1), pl.ds(code_refs[2 * t + 1][i], 1)
                        ready.append(
                            (part, to_low, part[to_low, :] + value, to_high, part[to_high, :] + value)
                        )
                for part, to_low, in_low, to_high, in_high in ready:
                    pltpu.store(part.at[to_low, :], in_low, mask=low)
                    pltpu.store(part.at[to_high, :], in_high, mask=high)
            return carry

        lax.fori_loop(0, count // (chains * UNROLL), some, 0)
        for t in range(tables):
            for s in range(shards):
                straight = sum(part[pl.ds(2 * s * half, half), :] for part in sums[t])
                crossed = sum(part[pl.ds((2 * s + 1) * half, half), :] for part in sums[t])
                result = (straight + swap_halves(crossed)).astype(jnp.bfloat16)
                out_refs[2 * t + s // planes][s % planes] = result

    results = pl.pallas_call(
        kernel,
        grid_spec=pltpu.PrefetchScalarGridSpec(
            num_scalar_prefetch=2 * tables,
            grid=(),
            in_specs=[VMEM] * len(blocks),
            out_specs=[VMEM] * (2 * tables),
            scratch_shapes=[pltpu.VMEM((count, LANES), jnp.float32)]
            + [pltpu.VMEM((2 * shards * half, LANES), jnp.float32)] * (tables * chains),
        ),
        out_shape=[jax.ShapeDtypeStruct((planes, half, LANES), jnp.bfloat16)] * (2 * tables),
        compiler_params=pltpu.CompilerParams(vmem_limit_bytes=42 * MIB),
        cost_estimate=pl.CostEstimate(
            flops=0, bytes_accessed=tables * 40 * MIB, transcendentals=0
        ),
        name="add_rows",
    )(*[part for pair in codes for part in pair], *blocks)
    return list(zip(results[::2], results[1::2]))


def finished(parts, begin, tables, earlier):
    _, half, lanes = parts[0][0].shape
    count = len(parts)

    def kernel(*refs):
        refs, out_ref = refs[:-1], refs[-1]
        for t in range(count):
            total = sum(ref[...].reshape(half, lanes).astype(jnp.float32) for ref in refs[4 * t : 4 * t + 4])
            turned = total.T
            out_ref[t, :, :half] = turned[: lanes // 2]
            out_ref[t, :, half:] = turned[lanes // 2 :]

    own = pl.BlockSpec((1, half, lanes), lambda i: (0, 0, 0))

    def row_block(n):
        return pl.BlockSpec((half, lanes), lambda i: (n, 0))

    operands, specs = [], []
    for near, got, down, d, last, n in parts:
        operands += [near, got, down, last]
        specs += [own, own, row_block(d), row_block(n)]
    if earlier is not None:
        operands.append(earlier)
        specs.append(pl.BlockSpec(memory_space=pl.ANY))
    return pl.pallas_call(
        kernel,
        grid=(1,),
        in_specs=specs,
        out_specs=pl.BlockSpec((count, lanes // 2, 2 * half), lambda i: (begin // count, 0, 0)),
        out_shape=jax.ShapeDtypeStruct((tables, lanes // 2, 2 * half), jnp.float32),
        input_output_aliases={} if earlier is None else {len(operands) - 1: 0},
        compiler_params=pltpu.CompilerParams(vmem_limit_bytes=32 * MIB),
        name="finished",
    )(*operands)


def weight_chunk(tall, groups):
    return -(-(2 * tall + 16) // (32 * groups)) * 16


def scaled_sums(at, near, far, tall, scale):
    groups, chunk, width = near.shape

    def kernel(at_ref, near_ref, far_ref, one_ref, two_ref, gain_one_ref, gain_two_ref, flat):
        me, core = at_ref[0], at_ref[1]
        for k in range(groups):
            for part_ref, side in ((near_ref, core), (far_ref, 1 - core)):
                begin = pl.multiple_of((side * groups + (me ^ k)) * chunk, 16)
                flat[pl.ds(begin, chunk), :] = part_ref[k].astype(jnp.float32) * scale
        one_ref[...] = flat[:tall, :]
        two_ref[...] = flat[tall : 2 * tall, :]
        gain_one_ref[...] = flat[2 * tall : 2 * tall + 1, :]
        gain_two_ref[...] = flat[2 * tall + 1 : 2 * tall + 2, :]

    return pl.pallas_call(
        kernel,
        grid_spec=pltpu.PrefetchScalarGridSpec(
            num_scalar_prefetch=1,
            grid=(),
            in_specs=[VMEM] * 2,
            out_specs=[VMEM] * 4,
            scratch_shapes=[pltpu.VMEM((2 * groups * chunk, width), jnp.float32)],
        ),
        out_shape=[jax.ShapeDtypeStruct((tall, width), jnp.float32)] * 2
        + [jax.ShapeDtypeStruct((1, width), jnp.float32)] * 2,
        compiler_params=pltpu.CompilerParams(vmem_limit_bytes=16 * MIB),
        name="scaled_sums",
    )(at, near, far)


def both_layers(me, blocks, weight_one, gain_one, weight_two, gain_two, grad_out, length):
    groups = len(blocks)
    items, width = grad_out.shape
    run = 2 * length
    steps = items // (2 * run)
    tall = weight_one.shape[0]
    chunk = weight_chunk(tall, groups)

    def kernel(me_ref, *refs):
        block_refs, refs = refs[:groups], refs[groups:]
        w_one_ref, g_one_ref, w_two_ref, g_two_ref, top_ref, out_ref, *refs = refs
        grad_refs, refs = refs[:groups], refs[groups:]
        kept_ref, given_ref, held, packed, sum_one, sum_two, sum_gains, flat, turned_one, turned_two = refs
        step = pl.program_id(0)
        me_at, core = me_ref[0], me_ref[1]
        low = low_lanes(run)
        place = lax.broadcasted_iota(jnp.int32, (run, width), 0)
        place = jnp.where(place >= length, place - length, place)

        @pl.when(step == 0)
        def _():
            sum_one[...] = jnp.zeros_like(sum_one)
            sum_two[...] = jnp.zeros_like(sum_two)
            sum_gains[...] = jnp.zeros_like(sum_gains)
            for weight_ref, turned_ref in ((w_one_ref, turned_one), (w_two_ref, turned_two)):
                for k in range(tall // width):
                    at = slice(k * width, (k + 1) * width)
                    turned_ref[at, :] = weight_ref[at, :].T

        def taps(values, gap):
            one = jnp.where(place >= gap, pltpu.roll(values, gap, 0), 0.0)
            two = jnp.where(place >= 2 * gap, pltpu.roll(values, 2 * gap, 0), 0.0)
            return jnp.concatenate([x.astype(jnp.bfloat16) for x in (values, one, two)], axis=1)

        def untaps(values, gap):
            one = jnp.where(place < length - gap, pltpu.roll(values, run - gap, 0), 0.0)
            two = jnp.where(place < length - 2 * gap, pltpu.roll(values, run - 2 * gap, 0), 0.0)
            return [x.astype(jnp.bfloat16) for x in (values, one, two)]

        def by_rows(work, *arrays):
            parts = [work(*(a[r : r + ROWS] for a in arrays)) for r in range(0, run, ROWS)]
            return [jnp.concatenate(values, axis=0) for values in zip(*parts)]

        def activate(before, gain):
            centred = before - jnp.mean(before, axis=-1, keepdims=True)
            inv_std = lax.rsqrt(jnp.mean(centred * centred, axis=-1, keepdims=True) + 1e-05)
            normal = centred * inv_std
            inputs = normal * gain
            square = inputs * inputs
            part = 0.5 + 0.5 * jnp.tanh(inputs * (GELU_C + GELU_C * GELU_K * square))
            slope = part + inputs * (part - part * part) * (
                2.0 * GELU_C + 6.0 * GELU_C * GELU_K * square
            )
            return normal, inv_std, inputs * part, slope

        def unwind(grad, normal, inv_std, slope, gain, row):
            scaled = grad * slope
            sum_gains[row] += jnp.sum((scaled * normal).reshape(-1, 8, width), axis=0)
            back = scaled * gain
            before = inv_std * (
                back
                - jnp.mean(back, axis=-1, keepdims=True)
                - normal * jnp.mean(back * normal, axis=-1, keepdims=True)
            )
            return before.astype(jnp.bfloat16).astype(jnp.float32)

        def products(before, values, turned_ref, gap, total):
            stacked = jnp.concatenate(untaps(before, gap), axis=1)
            total[...] += lax.dot_general(
                values.astype(jnp.bfloat16),
                stacked,
                (((0,), (0,)), ((), ())),
                preferred_element_type=jnp.float32,
            )
            return jnp.dot(stacked, turned_ref[...], preferred_element_type=jnp.float32)

        for k in range(groups):
            held[k] = block_refs[k][...].astype(jnp.float32)
        gain_one_at, gain_two_at = g_one_ref[...], g_two_ref[...]
        back_to = [None, None]

        def one_side(side):
            columns = []
            for q in range(0, groups, 2):
                left = held[q ^ me_at]
                right = held[(q + 1) ^ me_at]
                if side == 0:
                    columns.append(jnp.where(low, left, swap_halves(right)))
                else:
                    columns.append(jnp.where(low, swap_halves(left), right))
            embedded = jnp.concatenate(columns, axis=1)
            rows = pl.ds(side * run, run)
            top = top_ref[rows, :].astype(jnp.float32)
            stacked = taps(embedded, 1)
            yield
            before = jnp.dot(stacked, w_one_ref[...], preferred_element_type=jnp.float32)
            yield

            def first(before):
                normal, inv_std, output, slope = activate(before, gain_one_at)
                return normal, inv_std, output.astype(jnp.bfloat16).astype(jnp.float32), slope

            normal, inv_std, hidden, slope = by_rows(first, before)
            stacked = taps(hidden, 2)
            yield
            before = jnp.dot(stacked, w_two_ref[...], preferred_element_type=jnp.float32)
            yield

            def second(before, values, grad):
                normal, inv_std, output, slope = activate(before, gain_two_at)
                return values + output, unwind(grad, normal, inv_std, slope, gain_two_at, 1)

            output, before = by_rows(second, before, embedded, top)
            out_ref[rows, :] = output.astype(jnp.bfloat16)
            yield
            grad = products(before, hidden, turned_two, 2, sum_two)
            yield

            def third(grad, normal, inv_std, slope):
                return (unwind(grad, normal, inv_std, slope, gain_one_at, 0),)

            (before,) = by_rows(third, grad, normal, inv_std, slope)
            yield
            back_to[side] = top + products(before, embedded, turned_one, 1, sum_one)

        sides = [one_side(0), one_side(1)]
        next(sides[0])
        while sides:
            for one in sides[::-1]:
                if next(one, "done") == "done":
                    sides.remove(one)

        for q in range(groups):
            at = slice((q // 2) * LANES, (q // 2 + 1) * LANES)
            first, second = back_to[0][:, at], back_to[1][:, at]
            if q % 2 == 0:
                pair = jnp.where(low, first, swap_halves(second))
            else:
                pair = jnp.where(low, swap_halves(first), second)
            packed[q ^ me_at] = pair
        for k in range(groups):
            grad_refs[k][...] = packed[k].astype(jnp.bfloat16)

        @pl.when(step == steps - 1)
        def _():
            for n, total in enumerate((sum_one, sum_two)):
                for k in range(tall // width):
                    flat[n * tall + k * width : n * tall + (k + 1) * width, :] = total[
                        :, k * width : (k + 1) * width
                    ].astype(jnp.bfloat16)
            gains = [jnp.sum(sum_gains[n], axis=0, keepdims=True) for n in range(2)]
            flat[2 * tall : 2 * tall + 16, :] = jnp.concatenate(
                gains + [jnp.zeros((14, width), jnp.float32)], axis=0
            ).astype(jnp.bfloat16)
            if 2 * groups * chunk > 2 * tall + 16:
                flat[2 * tall + 16 :, :] = jnp.zeros(
                    (2 * groups * chunk - 2 * tall - 16, width), jnp.bfloat16
                )
            for k in range(groups):
                for part_ref, side in ((kept_ref, core), (given_ref, 1 - core)):
                    begin = pl.multiple_of((side * groups + (me_at ^ k)) * chunk, 16)
                    part_ref[k] = flat[pl.ds(begin, chunk), :]

    def whole(shape):
        return pl.BlockSpec(shape, lambda j, m: (0, 0))

    def by_step(rows, columns):
        return pl.BlockSpec((rows, columns), lambda j, m: (j, 0))

    return pl.pallas_call(
        kernel,
        grid_spec=pltpu.PrefetchScalarGridSpec(
            num_scalar_prefetch=1,
            grid=(steps,),
            in_specs=[by_step(run, LANES)] * groups
            + [whole((tall, width)), whole((1, width))] * 2
            + [by_step(2 * run, width)],
            out_specs=[by_step(2 * run, width)]
            + [by_step(run, LANES)] * groups
            + [pl.BlockSpec((groups, chunk, width), lambda j, m: (0, 0, 0))] * 2,
            scratch_shapes=[
                pltpu.VMEM((groups, run, LANES), jnp.float32),
                pltpu.VMEM((groups, run, LANES), jnp.float32),
                pltpu.VMEM((width, tall), jnp.float32),
                pltpu.VMEM((width, tall), jnp.float32),
                pltpu.VMEM((2, 8, width), jnp.float32),
                pltpu.VMEM((2 * groups * chunk, width), jnp.bfloat16),
                pltpu.VMEM((tall, width), jnp.bfloat16),
                pltpu.VMEM((tall, width), jnp.bfloat16),
            ],
        ),
        out_shape=[jax.ShapeDtypeStruct((items, width), jnp.bfloat16)]
        + [jax.ShapeDtypeStruct((items // 2, LANES), jnp.bfloat16)] * groups
        + [jax.ShapeDtypeStruct((groups, chunk, width), jnp.bfloat16)] * 2,
        compiler_params=pltpu.CompilerParams(vmem_limit_bytes=32 * MIB),
        name="both_layers",
    )(
        me,
        *blocks,
        weight_one,
        gain_one.reshape(1, width),
        weight_two,
        gain_two.reshape(1, width),
        grad_out,
    )


def together(*values):
    return lax.optimization_barrier(values)


def after(values, *first):
    return lax.optimization_barrier((values, *first))[0]


def column_plan(shard_of, offsets, table, weight_one, gain_one, weight_two, gain_two, grad_out):
    sessions, length, _ = shard_of.shape
    tables, rows_dev, width = table.shape
    items = sessions * length
    groups = lax.axis_size("dp")
    shards = lax.axis_size("table")
    planes = shards // 2
    half = rows_dev // 2
    run = 2 * length
    me = lax.axis_index("dp")
    plane, core = lax.axis_index("table") // 2, lax.axis_index("table") % 2
    at = jnp.stack([me, core]).astype(jnp.int32)

    def dp_flip(values, k):
        return lax.ppermute(values, "dp", [(i, i ^ k) for i in range(groups)])

    def table_shift(values, k):
        return lax.ppermute(values, "table", [(i, (i + k) % shards) for i in range(shards)])

    def up(values):
        return table_shift(values, 2)

    def down(values):
        return table_shift(values, -2)

    def across(values):
        return lax.ppermute(values, "table", [(i, i ^ 1) for i in range(shards)])

    slot = (shard_of + core) % 2 * planes + (shard_of // 2 - plane + planes) % planes
    places = jnp.stack(
        [slot * rows_dev + offsets, slot * rows_dev + (offsets + half) % rows_dev], axis=0
    ).astype(jnp.int32)
    places = places.reshape(2, items // (2 * run), 2, run, tables)
    mine = jnp.stack([places[0, :, 0], places[1, :, 1]], axis=0)
    mine = jnp.transpose(mine, (3, 0, 1, 2)).reshape(tables, 2, items // 2)

    first, last, own = own_columns(at, table)
    mine = after(mine, own)
    all_codes = mine
    for k in range((groups - 1).bit_length()):
        all_codes = jnp.concatenate([all_codes, dp_flip(all_codes, 2**k)], axis=2)
    codes = [(all_codes[t, 0], all_codes[t, 1]) for t in range(tables)]

    def from_planes(own, first=None):
        near = [None] * planes
        rising = falling = own
        for k in range(1, planes // 2 + 1):
            if first is not None and k == planes // 2:
                rising = after(rising, first)
            near[planes - k] = rising = up(rising)
            if k <= (planes - 1) // 2:
                near[k] = falling = down(falling)
        return near[1:]

    near_first = from_planes(first)
    swapped = across(after(own, all_codes))
    far_first = [across(values) for values in near_first]
    last = after(last, swapped, far_first[0], far_first[-1])

    def slots(t, near, far, place):
        return [(own, t), *((v, place) for v in near), (swapped, t), *((v, place) for v in far)]

    total = look_up(codes[0], slots(0, near_first, far_first, 0), None, False)
    near_last = from_planes(last, total)
    for t in range(1, tables - 1):
        total = look_up(codes[t], slots(t, near_first, far_first, t), total, False)
    far_last = [across(after(values, total)) for values in near_last]
    total = look_up(codes[tables - 1], slots(tables - 1, near_last, far_last, 0), total, True)

    pieces = total.reshape(groups, items // 2, LANES)
    arrived = [pieces[0]] + [dp_flip(pieces[k], k) for k in range(1, groups)]
    done = both_layers(
        at, arrived, weight_one, gain_one, weight_two, gain_two, grad_out.reshape(items, width), length
    )
    block_out = done[0].reshape(sessions, length, width)
    sent, kept, given = done[1 : 1 + groups], done[1 + groups], done[2 + groups]
    blocks = [sent[0]] + [dp_flip(sent[k], k) for k in range(1, groups)]

    def add_up(parts):
        return sum(part.astype(jnp.float32) for part in parts)

    got = across(given)
    chunks = [kept[k].astype(jnp.float32) + got[k].astype(jnp.float32) for k in range(groups)]
    chunks = [chunks[0]] + [chunk.astype(jnp.bfloat16) for chunk in chunks[1:]]
    blocks = [after(block, *chunks) for block in blocks]
    chunks = [chunks[0]] + [dp_flip(chunk, k) for k, chunk in enumerate(chunks[1:], 1)]

    def side(near, got, r):
        return near[r].astype(jnp.float32) + got[r].astype(jnp.float32)

    def packed(*values):
        return jnp.concatenate([value.astype(jnp.bfloat16) for value in values], axis=0)

    ((near_2, far_2),) = add_rows(codes[2:], blocks, shards, half, 4)
    far_2, *chunks[:-1] = together(far_2, *chunks[:-1])
    chunk = add_up(chunks).astype(jnp.bfloat16)
    got_2 = across(far_2)
    going = [packed(side(near_2, got_2, 2)), packed(side(near_2, got_2, 3)), chunk]
    came = [up(going[0]), down(going[1]), *(table_shift(chunk, k) for k in (shards // 2, 2, -2))]
    blocks = [after(block, *going) for block in blocks]
    (near_0, far_0), (near_1, far_1) = add_rows(codes[:2], blocks, shards, half, 2)
    far_0, up_2, down_2, *chunks = together(far_0, *came)
    got_0 = across(far_0)
    got_1 = across(after(far_1, got_0))
    chunk = (add_up([chunk, chunks[0]]) + add_up(chunks[1:])).astype(jnp.bfloat16)
    going = packed(
        side(near_2, got_2, 1) + up_2.astype(jnp.float32), side(near_0, got_0, 2), side(near_1, got_1, 2)
    )
    up_01, down_01, *chunks = together(
        up(going),
        down(packed(side(near_0, got_0, 3), side(near_1, got_1, 3))),
        *(dp_flip(chunk, k) for k in range(1, groups)),
    )
    near = jnp.stack([chunk, *chunks], axis=0)
    going = packed(
        side(near_0, got_0, 1) + up_01[half : 2 * half].astype(jnp.float32),
        side(near_1, got_1, 1) + up_01[2 * half :].astype(jnp.float32),
    )
    last_01, far = up(going), across(near)
    sums = scaled_sums(at, near, far, weight_one.shape[0], 1.0 / math.sqrt(items * groups * shards))

    near_2 = after(near_2, *sums)
    grads = finished([(near_2, got_2, down_2, 0, up_01, 0)], 2, tables, None)
    last_01, grads = together(last_01, grads)
    grads = finished(
        [(near_0, got_0, down_01, 0, last_01, 0), (near_1, got_1, down_01, 1, last_01, 1)], 0, tables, grads
    )
    table_grad = jnp.transpose(grads, (0, 2, 1))
    return (block_out, sums[0], sums[1], sums[2].reshape(width), sums[3].reshape(width), table_grad)


def solution(mesh):
    placed = (
        P(("dp", "table"), None, None),
        P(("dp", "table"), None, None),
        P(None, "table", None),
        P(),
        P(),
        P(),
        P(),
        P(("dp", "table"), None, None),
    )

    def on_device(shard_of, offsets, table, *rest):
        fits = columns_fit(shard_of.shape, table.shape, mesh.shape["dp"], mesh.shape["table"])
        plan = column_plan if fits else padded_plan
        return plan(shard_of, offsets, table, *rest)

    return jax.shard_map(
        on_device,
        mesh=mesh,
        in_specs=placed,
        out_specs=(P(("dp", "table"), None, None), P(), P(), P(), P(), P(None, "table", "dp")),
        check_vma=False,
    )
```

```python
import math

import jax
import jax.numpy as jnp
from jax import lax
from jax.experimental import pallas as pl
from jax.experimental.pallas import tpu as pltpu
from jax.sharding import PartitionSpec as P

GELU_C = 0.7978845608028654
GELU_K = 0.044715
LANES = 128
MIB = 2**20

UNROLL = 16
ROWS = 40


def shifted(values, spacing):
    return jnp.pad(values, ((0, 0), (spacing, 0), (0, 0)))[:, : values.shape[1], :]


def unshifted(values, spacing):
    return jnp.pad(values, ((0, 0), (0, spacing), (0, 0)))[:, spacing:, :]


def stack_taps(values, spacing):
    return jnp.concatenate(
        [values, shifted(values, spacing), shifted(values, 2 * spacing)], axis=-1
    )


def gelu_parts(inputs):
    inner = GELU_C * (inputs + GELU_K * inputs * inputs * inputs)
    tangent = jnp.tanh(inner)
    output = 0.5 * inputs * (1.0 + tangent)
    slope = 0.5 * (1.0 + tangent) + 0.5 * inputs * (1.0 - tangent * tangent) * GELU_C * (
        1.0 + 3.0 * GELU_K * inputs * inputs
    )
    return (output, slope)


def layer_forward(values, weight, gain, spacing):
    sessions, length, width = values.shape
    stacked = stack_taps(values, spacing).reshape(sessions * length, 3 * width)
    before_norm = jnp.dot(stacked, weight, preferred_element_type=jnp.float32)
    centred = before_norm - jnp.mean(before_norm, axis=-1, keepdims=True)
    inv_std = lax.rsqrt(jnp.mean(centred * centred, axis=-1, keepdims=True) + 1e-05)
    normal = centred * inv_std
    output, slope = gelu_parts(normal * gain)
    return (output, (stacked, normal, inv_std, slope))


def layer_backward(grad_output, weight, gain, saved, spacing, sessions, length):
    stacked, normal, inv_std, slope = saved
    width = weight.shape[1]
    grad_scaled = grad_output * slope
    grad_gain = jnp.sum(grad_scaled * normal, axis=0)
    grad_normal = grad_scaled * gain
    grad_before = inv_std * (
        grad_normal
        - jnp.mean(grad_normal, axis=-1, keepdims=True)
        - normal * jnp.mean(grad_normal * normal, axis=-1, keepdims=True)
    )
    grad_before = grad_before.astype(jnp.bfloat16)
    grad_weight = lax.dot_general(
        stacked, grad_before, (((0,), (0,)), ((), ())), preferred_element_type=jnp.float32
    )
    grad_taps = lax.dot_general(
        grad_before, weight, (((1,), (1,)), ((), ())), preferred_element_type=jnp.float32
    ).reshape(sessions, length, 3 * width)
    grad_input = (
        grad_taps[..., :width]
        + unshifted(grad_taps[..., width : 2 * width], spacing)
        + unshifted(grad_taps[..., 2 * width :], 2 * spacing)
    )
    return (grad_input, grad_weight, grad_gain)


def to_owners(grad_rows, slot_place, shards, slot_count, width):
    outgoing = (
        jnp.zeros((shards * slot_count, width), jnp.bfloat16)
        .at[slot_place]
        .set(grad_rows)
        .reshape(shards, slot_count, width)
    )
    return lax.all_to_all(outgoing, "table", split_axis=0, concat_axis=0, tiled=True)


def padded_plan(shard_of, offsets, table, weight_one, gain_one, weight_two, gain_two, grad_out):
    sessions, length, _ = shard_of.shape
    width = table.shape[2]
    rows_dev = table.shape[1]
    item_count = sessions * length
    shards = lax.axis_size("table")
    groups = lax.axis_size("dp")
    quarter = width // groups
    slot_count = 8 * ((6 * item_count + 8 * shards - 1) // (8 * shards))
    target = shard_of.reshape(-1)
    table_pick = jnp.tile(jnp.arange(3, dtype=jnp.int32), item_count)
    row_codes = table_pick * rows_dev + offsets.reshape(-1)
    onehot = (jnp.arange(shards, dtype=jnp.int32)[:, None] == target[None, :]).astype(jnp.int32)
    before = jnp.cumsum(onehot, axis=1) - onehot
    slot_rank = jnp.sum(before * onehot, axis=0)
    slot_place = target * slot_count + slot_rank
    requests = (
        jnp.full((shards * slot_count,), -1, jnp.int32)
        .at[slot_place]
        .set(row_codes)
        .reshape(shards, slot_count)
    )
    table_flat = table.reshape(3 * rows_dev, width)
    asked_rows = lax.all_to_all(requests, "table", split_axis=0, concat_axis=0, tiled=True)
    found_rows = jnp.take(table_flat, jnp.maximum(asked_rows, 0), axis=0)
    found_rows = jnp.where((asked_rows >= 0)[..., None], found_rows, jnp.zeros((), jnp.bfloat16))
    sent_back = lax.all_to_all(found_rows, "table", split_axis=0, concat_axis=0, tiled=True)
    picked = jnp.take(sent_back.reshape(shards * slot_count, width), slot_place, axis=0).reshape(
        item_count, 3, width
    )
    embedded = (
        jnp.sum(picked.astype(jnp.float32), axis=1)
        .astype(jnp.bfloat16)
        .reshape(sessions, length, width)
    )
    act_one, saved_one = layer_forward(embedded, weight_one, gain_one, 1)
    hidden = act_one.astype(jnp.bfloat16).reshape(sessions, length, width)
    act_two, saved_two = layer_forward(hidden, weight_two, gain_two, 2)
    block_out = (
        (embedded.reshape(item_count, width).astype(jnp.float32) + act_two)
        .astype(jnp.bfloat16)
        .reshape(sessions, length, width)
    )
    grad_top = grad_out.reshape(item_count, width).astype(jnp.float32)
    scale = 1.0 / math.sqrt(item_count * groups * shards)
    grad_hidden, second_weights, second_gains = layer_backward(
        grad_top, weight_two, gain_two, saved_two, 2, sessions, length
    )
    grad_inner, first_weights, first_gains = layer_backward(
        grad_hidden.reshape(item_count, width), weight_one, gain_one, saved_one, 1, sessions, length
    )
    grad_embed = (grad_top + grad_inner.reshape(item_count, width)).astype(jnp.bfloat16)
    repeated = jnp.repeat(grad_embed, 3, axis=0)
    arrived = to_owners(repeated, slot_place, shards, slot_count, width)
    dense_grad = (
        jnp.zeros((3 * rows_dev, width), jnp.float32)
        .at[jnp.maximum(asked_rows, 0).reshape(-1)]
        .add(arrived.reshape(-1, width).astype(jnp.float32))
    )
    table_grad = lax.psum_scatter(
        dense_grad.astype(jnp.bfloat16), "dp", scatter_dimension=1, tiled=True
    ).astype(jnp.float32)
    table_grad = table_grad.reshape(3, rows_dev, quarter)
    totals = lax.psum((first_weights, second_weights, first_gains, second_gains), ("dp", "table"))
    return (
        block_out,
        totals[0] * scale,
        totals[1] * scale,
        totals[2] * scale,
        totals[3] * scale,
        table_grad,
    )


VMEM = pl.BlockSpec(memory_space=pltpu.VMEM)


def columns_fit(items_shape, table_shape, groups, shards):
    sessions, length, _ = items_shape
    _, rows_dev, width = table_shape
    run = 2 * length
    return (
        2 * width == groups * LANES
        and groups > 1
        and (groups & (groups - 1)) == 0
        and sessions % 4 == 0
        and sessions <= 16
        and run % 16 == 0
        and run % ROWS == 0
        and (groups * sessions * length // 2) % (4 * UNROLL) == 0
        and rows_dev % 32 == 0
        and 4 * shards * rows_dev * LANES * 4 <= 40 * MIB
        and table_shape[0] == 3
        and shards == 8
    )


def low_lanes(rows):
    return lax.broadcasted_iota(jnp.int32, (rows, LANES), 1) < LANES // 2


def swap_halves(values):
    return pltpu.roll(values, LANES // 2, 1)


def own_columns(at, table):
    tables, rows_dev, _ = table.shape
    half = rows_dev // 2

    def kernel(at_ref, table_ref, first_ref, last_ref, all_ref):
        odd = at_ref[0] % 2 == 1
        low = low_lanes(half)
        for t in range(tables):
            top = table_ref[t, :half, :].astype(jnp.float32)
            bottom = table_ref[t, half:, :].astype(jnp.float32)
            in_low = jnp.where(odd, swap_halves(top), top)
            in_high = jnp.where(odd, bottom, swap_halves(bottom))
            values = jnp.where(low, in_low, in_high).astype(jnp.bfloat16)
            if t < tables - 1:
                first_ref[t] = values
            else:
                last_ref[0] = values
            all_ref[t] = values

    def whole(count):
        return pl.BlockSpec((count, half, LANES), lambda i, m: (0, 0, 0))

    return pl.pallas_call(
        kernel,
        grid_spec=pltpu.PrefetchScalarGridSpec(
            num_scalar_prefetch=1,
            grid=(1,),
            in_specs=[pl.BlockSpec((tables, rows_dev, LANES), lambda i, m: (0, 0, m[0] // 2))],
            out_specs=[whole(tables - 1), whole(1), whole(tables)],
        ),
        out_shape=[
            jax.ShapeDtypeStruct((count, half, LANES), jnp.bfloat16)
            for count in (tables - 1, 1, tables)
        ],
        compiler_params=pltpu.CompilerParams(vmem_limit_bytes=24 * MIB),
        name="own_columns",
    )(at, table)


def look_up(codes, slots, total, last):
    count = codes[0].shape[0]
    half = slots[0][0].shape[1]

    def kernel(low_ref, high_ref, *refs):
        slot_refs, refs = refs[: len(slots)], refs[len(slots) :]
        total_ref = None if total is None else refs[0]
        out_ref, rows, found = refs[-3:]
        for s, slot_ref in enumerate(slot_refs):
            values = slot_ref[0].astype(jnp.float32)
            rows[pl.ds(2 * s * half, half), :] = values
            rows[pl.ds((2 * s + 1) * half, half), :] = swap_halves(values)
        low = low_lanes(1)

        def some(step, carry):
            for j in range(2 * UNROLL):
                i = step * 2 * UNROLL + j
                for_low = rows[pl.ds(low_ref[i], 1), :]
                for_high = rows[pl.ds(high_ref[i], 1), :]
                found[pl.ds(i, 1), :] = jnp.where(low, for_low, for_high)
            return carry

        lax.fori_loop(0, count // (2 * UNROLL), some, 0)
        result = found[...]
        if total_ref is not None:
            result = result + total_ref[...]
        out_ref[...] = result.astype(out_ref.dtype)

    def part(at):
        return pl.BlockSpec((1, half, LANES), lambda i, *codes: (at, 0, 0))

    operands = [slot[0] for slot in slots] + ([] if total is None else [total])
    whole = pl.BlockSpec((count, LANES), lambda i, *codes: (0, 0))
    return pl.pallas_call(
        kernel,
        grid_spec=pltpu.PrefetchScalarGridSpec(
            num_scalar_prefetch=2,
            grid=(1,),
            in_specs=[part(slot[1]) for slot in slots] + ([] if total is None else [whole]),
            out_specs=whole,
            scratch_shapes=[
                pltpu.VMEM((2 * len(slots) * half, LANES), jnp.float32),
                pltpu.VMEM((count, LANES), jnp.float32),
            ],
        ),
        out_shape=jax.ShapeDtypeStruct((count, LANES), jnp.bfloat16 if last else jnp.float32),
        compiler_params=pltpu.CompilerParams(vmem_limit_bytes=20 * MIB),
        cost_estimate=pl.CostEstimate(
            flops=0, bytes_accessed=8 * 3 * count * LANES * 4, transcendentals=0
        ),
        name="look_up",
    )(*codes, *operands)


def add_rows(codes, blocks, shards, half, chains):
    tables = len(codes)
    count = codes[0][0].shape[0]
    per = blocks[0].shape[0]
    planes = shards // 2

    def kernel(*refs):
        code_refs, refs = refs[: 2 * tables], refs[2 * tables :]
        block_refs, refs = refs[: len(blocks)], refs[len(blocks) :]
        out_refs, values, refs = refs[: 2 * tables], refs[2 * tables], refs[2 * tables + 1 :]
        sums = [refs[t * chains : (t + 1) * chains] for t in range(tables)]
        for k, block_ref in enumerate(block_refs):
            values[pl.ds(k * per, per), :] = block_ref[...].astype(jnp.float32)
        for part in refs:
            part[...] = jnp.zeros_like(part)
        low = low_lanes(1)
        high = jnp.logical_not(low)

        def some(step, carry):
            for j in range(UNROLL):
                ready = []
                for c in range(chains):
                    i = c * (count // chains) + step * UNROLL + j
                    value = values[pl.ds(i, 1), :]
                    for t in range(tables):
                        part = sums[t][c]
                        to_low, to_high = pl.ds(code_refs[2 * t][i], 1), pl.ds(code_refs[2 * t + 1][i], 1)
                        ready.append(
                            (part, to_low, part[to_low, :] + value, to_high, part[to_high, :] + value)
                        )
                for part, to_low, in_low, to_high, in_high in ready:
                    pltpu.store(part.at[to_low, :], in_low, mask=low)
                    pltpu.store(part.at[to_high, :], in_high, mask=high)
            return carry

        lax.fori_loop(0, count // (chains * UNROLL), some, 0)
        for t in range(tables):
            for s in range(shards):
                straight = sum(part[pl.ds(2 * s * half, half), :] for part in sums[t])
                crossed = sum(part[pl.ds((2 * s + 1) * half, half), :] for part in sums[t])
                result = (straight + swap_halves(crossed)).astype(jnp.bfloat16)
                out_refs[2 * t + s // planes][s % planes] = result

    results = pl.pallas_call(
        kernel,
        grid_spec=pltpu.PrefetchScalarGridSpec(
            num_scalar_prefetch=2 * tables,
            grid=(),
            in_specs=[VMEM] * len(blocks),
            out_specs=[VMEM] * (2 * tables),
            scratch_shapes=[pltpu.VMEM((count, LANES), jnp.float32)]
            + [pltpu.VMEM((2 * shards * half, LANES), jnp.float32)] * (tables * chains),
        ),
        out_shape=[jax.ShapeDtypeStruct((planes, half, LANES), jnp.bfloat16)] * (2 * tables),
        compiler_params=pltpu.CompilerParams(vmem_limit_bytes=42 * MIB),
        cost_estimate=pl.CostEstimate(
            flops=0, bytes_accessed=tables * 40 * MIB, transcendentals=0
        ),
        name="add_rows",
    )(*[part for pair in codes for part in pair], *blocks)
    return list(zip(results[::2], results[1::2]))


def finished(parts, begin, tables, earlier):
    _, half, lanes = parts[0][0].shape
    count = len(parts)

    def kernel(*refs):
        refs, out_ref = refs[:-1], refs[-1]
        for t in range(count):
            total = sum(ref[...].reshape(half, lanes).astype(jnp.float32) for ref in refs[4 * t : 4 * t + 4])
            turned = total.T
            out_ref[t, :, :half] = turned[: lanes // 2]
            out_ref[t, :, half:] = turned[lanes // 2 :]

    own = pl.BlockSpec((1, half, lanes), lambda i: (0, 0, 0))

    def row_block(n):
        return pl.BlockSpec((half, lanes), lambda i: (n, 0))

    operands, specs = [], []
    for near, got, down, d, last, n in parts:
        operands += [near, got, down, last]
        specs += [own, own, row_block(d), row_block(n)]
    if earlier is not None:
        operands.append(earlier)
        specs.append(pl.BlockSpec(memory_space=pl.ANY))
    return pl.pallas_call(
        kernel,
        grid=(1,),
        in_specs=specs,
        out_specs=pl.BlockSpec((count, lanes // 2, 2 * half), lambda i: (begin // count, 0, 0)),
        out_shape=jax.ShapeDtypeStruct((tables, lanes // 2, 2 * half), jnp.float32),
        input_output_aliases={} if earlier is None else {len(operands) - 1: 0},
        compiler_params=pltpu.CompilerParams(vmem_limit_bytes=32 * MIB),
        name="finished",
    )(*operands)


def weight_chunk(tall, groups):
    return -(-(2 * tall + 16) // (32 * groups)) * 16


def scaled_sums(at, near, far, tall, width, scale):
    groups = near.shape[0]
    chunk = near.shape[1] * LANES // width

    def kernel(at_ref, near_ref, far_ref, one_ref, two_ref, gain_one_ref, gain_two_ref, flat):
        me, core = at_ref[0], at_ref[1]
        for k in range(groups):
            for part_ref, side in ((near_ref, core), (far_ref, 1 - core)):
                begin = pl.multiple_of((side * groups + (me ^ k)) * chunk, 16)
                for n in range(width // LANES):
                    values = part_ref[k, n * chunk : (n + 1) * chunk, :].astype(jnp.float32)
                    flat[pl.ds(begin, chunk), n * LANES : (n + 1) * LANES] = values * scale
        one_ref[...] = flat[:tall, :]
        two_ref[...] = flat[tall : 2 * tall, :]
        gain_one_ref[...] = flat[2 * tall : 2 * tall + 1, :]
        gain_two_ref[...] = flat[2 * tall + 1 : 2 * tall + 2, :]

    return pl.pallas_call(
        kernel,
        grid_spec=pltpu.PrefetchScalarGridSpec(
            num_scalar_prefetch=1,
            grid=(),
            in_specs=[VMEM] * 2,
            out_specs=[VMEM] * 4,
            scratch_shapes=[pltpu.VMEM((2 * groups * chunk, width), jnp.float32)],
        ),
        out_shape=[jax.ShapeDtypeStruct((tall, width), jnp.float32)] * 2
        + [jax.ShapeDtypeStruct((1, width), jnp.float32)] * 2,
        compiler_params=pltpu.CompilerParams(vmem_limit_bytes=16 * MIB),
        name="scaled_sums",
    )(at, near, far)


def both_layers(me, blocks, weight_one, gain_one, weight_two, gain_two, grad_out, length):
    groups = len(blocks)
    items, width = grad_out.shape
    run = 2 * length
    steps = items // (2 * run)
    tall = weight_one.shape[0]
    chunk = weight_chunk(tall, groups)

    def kernel(me_ref, *refs):
        block_refs, refs = refs[:groups], refs[groups:]
        w_one_ref, g_one_ref, w_two_ref, g_two_ref, top_ref, out_ref, *refs = refs
        grad_refs, refs = refs[:groups], refs[groups:]
        kept_ref, given_ref, held, packed, sum_one, sum_two, sum_gains, flat, turned_one, turned_two = refs
        me_at, core = me_ref[0], me_ref[1]
        low = low_lanes(run)
        place = lax.broadcasted_iota(jnp.int32, (run, width), 0)
        place = jnp.where(place >= length, place - length, place)

        sum_one[...] = jnp.zeros_like(sum_one)
        sum_two[...] = jnp.zeros_like(sum_two)
        sum_gains[...] = jnp.zeros_like(sum_gains)
        for weight_ref, turned_ref in ((w_one_ref, turned_one), (w_two_ref, turned_two)):
            for k in range(tall // width):
                at = slice(k * width, (k + 1) * width)
                turned_ref[at, :] = weight_ref[at, :].T

        def taps(values, gap):
            one = jnp.where(place >= gap, pltpu.roll(values, gap, 0), 0.0)
            two = jnp.where(place >= 2 * gap, pltpu.roll(values, 2 * gap, 0), 0.0)
            return jnp.concatenate([x.astype(jnp.bfloat16) for x in (values, one, two)], axis=1)

        def untaps(values, gap):
            one = jnp.where(place < length - gap, pltpu.roll(values, run - gap, 0), 0.0)
            two = jnp.where(place < length - 2 * gap, pltpu.roll(values, run - 2 * gap, 0), 0.0)
            return [x.astype(jnp.bfloat16) for x in (values, one, two)]

        def by_rows(work, *arrays):
            parts = [work(*(a[r : r + ROWS] for a in arrays)) for r in range(0, run, ROWS)]
            return [jnp.concatenate(values, axis=0) for values in zip(*parts)]

        def activate(before, gain):
            centred = before - jnp.mean(before, axis=-1, keepdims=True)
            inv_std = lax.rsqrt(jnp.mean(centred * centred, axis=-1, keepdims=True) + 1e-05)
            normal = centred * inv_std
            inputs = normal * gain
            square = inputs * inputs
            part = 0.5 + 0.5 * jnp.tanh(inputs * (GELU_C + GELU_C * GELU_K * square))
            slope = part + inputs * (part - part * part) * (
                2.0 * GELU_C + 6.0 * GELU_C * GELU_K * square
            )
            return normal, inv_std, inputs * part, slope

        def unwind(grad, normal, inv_std, slope, gain, row):
            scaled = grad * slope
            sum_gains[row] += jnp.sum((scaled * normal).reshape(-1, 8, width), axis=0)
            back = scaled * gain
            before = inv_std * (
                back
                - jnp.mean(back, axis=-1, keepdims=True)
                - normal * jnp.mean(back * normal, axis=-1, keepdims=True)
            )
            return before.astype(jnp.bfloat16).astype(jnp.float32)

        def products(before, values, turned_ref, gap, total):
            stacked = jnp.concatenate(untaps(before, gap), axis=1)
            total[...] += lax.dot_general(
                values.astype(jnp.bfloat16),
                stacked,
                (((0,), (0,)), ((), ())),
                preferred_element_type=jnp.float32,
            )
            return jnp.dot(stacked, turned_ref[...], preferred_element_type=jnp.float32)

        for k in range(groups):
            held[k] = block_refs[k][...].astype(jnp.float32)
        gain_one_at, gain_two_at = g_one_ref[...], g_two_ref[...]
        back_to = [None] * (2 * steps)

        def one_part(n):
            side, packed_rows = n % 2, pl.ds(n // 2 * run, run)
            columns = []
            for q in range(0, groups, 2):
                left = held[q ^ me_at, packed_rows, :]
                right = held[(q + 1) ^ me_at, packed_rows, :]
                if side == 0:
                    columns.append(jnp.where(low, left, swap_halves(right)))
                else:
                    columns.append(jnp.where(low, swap_halves(left), right))
            embedded = jnp.concatenate(columns, axis=1)
            rows = pl.ds(n * run, run)
            top = top_ref[rows, :].astype(jnp.float32)
            stacked = taps(embedded, 1)
            yield
            before = jnp.dot(stacked, w_one_ref[...], preferred_element_type=jnp.float32)
            yield

            def first(before):
                normal, inv_std, output, slope = activate(before, gain_one_at)
                return normal, inv_std, output.astype(jnp.bfloat16).astype(jnp.float32), slope

            normal, inv_std, hidden, slope = by_rows(first, before)
            stacked = taps(hidden, 2)
            yield
            before = jnp.dot(stacked, w_two_ref[...], preferred_element_type=jnp.float32)
            yield

            def second(before, values, grad):
                normal, inv_std, output, slope = activate(before, gain_two_at)
                return values + output, unwind(grad, normal, inv_std, slope, gain_two_at, 1)

            output, before = by_rows(second, before, embedded, top)
            out_ref[rows, :] = output.astype(jnp.bfloat16)
            yield
            grad = products(before, hidden, turned_two, 2, sum_two)
            yield

            def third(grad, normal, inv_std, slope):
                return (unwind(grad, normal, inv_std, slope, gain_one_at, 0),)

            (before,) = by_rows(third, grad, normal, inv_std, slope)
            yield
            back_to[n] = top + products(before, embedded, turned_one, 1, sum_one)
            if side == 0:
                return
            for q in range(groups):
                at = slice((q // 2) * LANES, (q // 2 + 1) * LANES)
                first, second = back_to[n - 1][:, at], back_to[n][:, at]
                if q % 2 == 0:
                    pair = jnp.where(low, first, swap_halves(second))
                else:
                    pair = jnp.where(low, swap_halves(first), second)
                packed[q ^ me_at, packed_rows, :] = pair

        waiting = [one_part(n) for n in range(2 * steps)]
        active = [waiting.pop(0)]
        next(active[0])
        while active:
            if len(active) < 2 and waiting:
                active.append(waiting.pop(0))
            for one in active[::-1]:
                if next(one, "done") == "done":
                    active.remove(one)
        for k in range(groups):
            grad_refs[k][...] = packed[k].astype(jnp.bfloat16)

        for n, total in enumerate((sum_one, sum_two)):
            for k in range(tall // width):
                flat[n * tall + k * width : n * tall + (k + 1) * width, :] = total[
                    :, k * width : (k + 1) * width
                ].astype(jnp.bfloat16)
        gains = [jnp.sum(sum_gains[n], axis=0, keepdims=True) for n in range(2)]
        flat[2 * tall : 2 * tall + 16, :] = jnp.concatenate(
            gains + [jnp.zeros((14, width), jnp.float32)], axis=0
        ).astype(jnp.bfloat16)
        if 2 * groups * chunk > 2 * tall + 16:
            flat[2 * tall + 16 :, :] = jnp.zeros(
                (2 * groups * chunk - 2 * tall - 16, width), jnp.bfloat16
            )
        for k in range(groups):
            for part_ref, side in ((kept_ref, core), (given_ref, 1 - core)):
                begin = pl.multiple_of((side * groups + (me_at ^ k)) * chunk, 16)
                part_ref[k] = flat[pl.ds(begin, chunk), :]

    def whole(shape):
        return pl.BlockSpec(shape, lambda j, m: (0, 0))

    return pl.pallas_call(
        kernel,
        grid_spec=pltpu.PrefetchScalarGridSpec(
            num_scalar_prefetch=1,
            grid=(1,),
            in_specs=[whole((items // 2, LANES))] * groups
            + [whole((tall, width)), whole((1, width))] * 2
            + [whole((items, width))],
            out_specs=[whole((items, width))]
            + [whole((items // 2, LANES))] * groups
            + [pl.BlockSpec((groups, chunk, width), lambda j, m: (0, 0, 0))] * 2,
            scratch_shapes=[
                pltpu.VMEM((groups, items // 2, LANES), jnp.float32),
                pltpu.VMEM((groups, items // 2, LANES), jnp.float32),
                pltpu.VMEM((width, tall), jnp.float32),
                pltpu.VMEM((width, tall), jnp.float32),
                pltpu.VMEM((2, 8, width), jnp.float32),
                pltpu.VMEM((2 * groups * chunk, width), jnp.bfloat16),
                pltpu.VMEM((tall, width), jnp.bfloat16),
                pltpu.VMEM((tall, width), jnp.bfloat16),
            ],
        ),
        out_shape=[jax.ShapeDtypeStruct((items, width), jnp.bfloat16)]
        + [jax.ShapeDtypeStruct((items // 2, LANES), jnp.bfloat16)] * groups
        + [jax.ShapeDtypeStruct((groups, chunk, width), jnp.bfloat16)] * 2,
        compiler_params=pltpu.CompilerParams(vmem_limit_bytes=32 * MIB),
        name="both_layers",
    )(
        me,
        *blocks,
        weight_one,
        gain_one.reshape(1, width),
        weight_two,
        gain_two.reshape(1, width),
        grad_out,
    )


def together(*values):
    return lax.optimization_barrier(values)


def after(values, *first):
    return lax.optimization_barrier((values, *first))[0]


def column_plan(shard_of, offsets, table, weight_one, gain_one, weight_two, gain_two, grad_out):
    sessions, length, _ = shard_of.shape
    tables, rows_dev, width = table.shape
    items = sessions * length
    groups = lax.axis_size("dp")
    shards = lax.axis_size("table")
    planes = shards // 2
    half = rows_dev // 2
    run = 2 * length
    me = lax.axis_index("dp")
    plane, core = lax.axis_index("table") // 2, lax.axis_index("table") % 2
    at = jnp.stack([me, core]).astype(jnp.int32)

    def dp_flip(values, k):
        return lax.ppermute(values, "dp", [(i, i ^ k) for i in range(groups)])

    def table_shift(values, k):
        return lax.ppermute(values, "table", [(i, (i + k) % shards) for i in range(shards)])

    def up(values):
        return table_shift(values, 2)

    def down(values):
        return table_shift(values, -2)

    def across(values):
        return lax.ppermute(values, "table", [(i, i ^ 1) for i in range(shards)])

    slot = (shard_of + core) % 2 * planes + (shard_of // 2 - plane + planes) % planes
    places = jnp.stack(
        [slot * rows_dev + offsets, slot * rows_dev + (offsets + half) % rows_dev], axis=0
    ).astype(jnp.int32)
    places = places.reshape(2, items // (2 * run), 2, run, tables)
    mine = jnp.stack([places[0, :, 0], places[1, :, 1]], axis=0)
    mine = jnp.transpose(mine, (3, 0, 1, 2)).reshape(tables, 2, items // 2)

    first, last, own = own_columns(at, table)
    all_codes = mine
    for k in range((groups - 1).bit_length()):
        all_codes = jnp.concatenate([all_codes, dp_flip(all_codes, 2**k)], axis=2)
    codes = [(all_codes[t, 0], all_codes[t, 1]) for t in range(tables)]

    def from_planes(own, first=None):
        near = [None] * planes
        rising = falling = own
        for k in range(1, planes // 2 + 1):
            if first is not None and k == planes // 2:
                rising = after(rising, first)
            near[planes - k] = rising = up(rising)
            if k <= (planes - 1) // 2:
                near[k] = falling = down(falling)
        return near[1:]

    near_first = from_planes(first)
    swapped = across(after(own, all_codes))
    far_first = [across(values) for values in near_first]
    last = after(last, swapped, far_first[0], far_first[-1])

    def slots(t, near, far, place):
        return [(own, t), *((v, place) for v in near), (swapped, t), *((v, place) for v in far)]

    total = look_up(codes[0], slots(0, near_first, far_first, 0), None, False)
    near_last = from_planes(last, total)
    for t in range(1, tables - 1):
        total = look_up(codes[t], slots(t, near_first, far_first, t), total, False)
    far_last = [across(after(values, total)) for values in near_last]
    total = look_up(codes[tables - 1], slots(tables - 1, near_last, far_last, 0), total, True)

    pieces = total.reshape(groups, items // 2, LANES)
    arrived = [pieces[0]] + [dp_flip(pieces[k], k) for k in range(1, groups)]
    done = both_layers(
        at, arrived, weight_one, gain_one, weight_two, gain_two, grad_out.reshape(items, width), length
    )
    block_out = done[0].reshape(sessions, length, width)
    sent, kept, given = done[1 : 1 + groups], done[1 + groups], done[2 + groups]
    blocks = [sent[0]] + [dp_flip(sent[k], k) for k in range(1, groups)]

    def add_up(parts):
        return sum(part.astype(jnp.float32) for part in parts)

    got = across(given)
    chunks = [kept[k].astype(jnp.float32) + got[k].astype(jnp.float32) for k in range(groups)]
    chunks = [chunks[0]] + [chunk.astype(jnp.bfloat16) for chunk in chunks[1:]]
    blocks = [after(block, *chunks) for block in blocks]
    chunks = [chunks[0]] + [dp_flip(chunk, k) for k, chunk in enumerate(chunks[1:], 1)]

    def side(near, got, r):
        return near[r].astype(jnp.float32) + got[r].astype(jnp.float32)

    def packed(*values):
        return jnp.concatenate([value.astype(jnp.bfloat16) for value in values], axis=0)

    ((near_2, far_2),) = add_rows(codes[2:], blocks, shards, half, 4)
    far_2, *chunks = together(far_2, *chunks)
    chunk = add_up(chunks)
    chunk = packed(*(chunk[:, n : n + LANES] for n in range(0, width, LANES)))
    got_2 = across(far_2)
    going = [packed(side(near_2, got_2, 2), chunk), packed(side(near_2, got_2, 3), chunk)]
    came = [up(going[0]), down(going[1])]
    blocks = [after(block, *going) for block in blocks]
    (near_0, far_0), (near_1, far_1) = add_rows(codes[:2], blocks, shards, half, 2)
    far_0, far_1, up_2, down_2 = together(far_0, far_1, *came)
    opposite = up(up_2[half:])
    got_0 = across(far_0)
    got_1 = across(far_1)
    chunk = (add_up([chunk, opposite]) + add_up([up_2[half:], down_2[half:]])).astype(jnp.bfloat16)
    going = packed(
        side(near_2, got_2, 1) + up_2[:half].astype(jnp.float32), side(near_0, got_0, 2), side(near_1, got_1, 2)
    )
    up_01, down_01, *chunks = together(
        up(after(going, chunk)),
        down(packed(side(near_0, got_0, 3), side(near_1, got_1, 3))),
        *(dp_flip(chunk, k) for k in range(1, groups)),
    )
    near = jnp.stack([chunk, *chunks], axis=0)
    going = packed(
        side(near_0, got_0, 1) + up_01[half : 2 * half].astype(jnp.float32),
        side(near_1, got_1, 1) + up_01[2 * half :].astype(jnp.float32),
    )
    last_01, far = up(going), across(near)
    sums = scaled_sums(at, near, far, weight_one.shape[0], width, 1.0 / math.sqrt(items * groups * shards))

    near_2 = after(near_2, *sums)
    grads = finished([(near_2, got_2, down_2, 0, up_01, 0)], 2, tables, None)
    last_01, grads = together(last_01, grads)
    grads = finished(
        [(near_0, got_0, down_01, 0, last_01, 0), (near_1, got_1, down_01, 1, last_01, 1)], 0, tables, grads
    )
    table_grad = jnp.transpose(grads, (0, 2, 1))
    return (block_out, sums[0], sums[1], sums[2].reshape(width), sums[3].reshape(width), table_grad)


def solution(mesh):
    placed = (
        P(("dp", "table"), None, None),
        P(("dp", "table"), None, None),
        P(None, "table", None),
        P(),
        P(),
        P(),
        P(),
        P(("dp", "table"), None, None),
    )

    def on_device(shard_of, offsets, table, *rest):
        fits = columns_fit(shard_of.shape, table.shape, mesh.shape["dp"], mesh.shape["table"])
        plan = column_plan if fits else padded_plan
        return plan(shard_of, offsets, table, *rest)

    return jax.shard_map(
        on_device,
        mesh=mesh,
        in_specs=placed,
        out_specs=(P(("dp", "table"), None, None), P(), P(), P(), P(), P(None, "table", "dp")),
        check_vma=False,
    )
```

```python
import math

import jax
import jax.numpy as jnp
from jax import lax
from jax.experimental import pallas as pl
from jax.experimental.pallas import tpu as pltpu
from jax.sharding import PartitionSpec as P

GELU_C = 0.7978845608028654
GELU_K = 0.044715
LANES = 128
MIB = 2**20

UNROLL = 16


def shifted(values, spacing):
    return jnp.pad(values, ((0, 0), (spacing, 0), (0, 0)))[:, : values.shape[1], :]


def unshifted(values, spacing):
    return jnp.pad(values, ((0, 0), (0, spacing), (0, 0)))[:, spacing:, :]


def stack_taps(values, spacing):
    return jnp.concatenate(
        [values, shifted(values, spacing), shifted(values, 2 * spacing)], axis=-1
    )


def gelu_parts(inputs):
    inner = GELU_C * (inputs + GELU_K * inputs * inputs * inputs)
    tangent = jnp.tanh(inner)
    output = 0.5 * inputs * (1.0 + tangent)
    slope = 0.5 * (1.0 + tangent) + 0.5 * inputs * (1.0 - tangent * tangent) * GELU_C * (
        1.0 + 3.0 * GELU_K * inputs * inputs
    )
    return (output, slope)


def layer_forward(values, weight, gain, spacing):
    sessions, length, width = values.shape
    stacked = stack_taps(values, spacing).reshape(sessions * length, 3 * width)
    before_norm = jnp.dot(stacked, weight, preferred_element_type=jnp.float32)
    centred = before_norm - jnp.mean(before_norm, axis=-1, keepdims=True)
    inv_std = lax.rsqrt(jnp.mean(centred * centred, axis=-1, keepdims=True) + 1e-05)
    normal = centred * inv_std
    output, slope = gelu_parts(normal * gain)
    return (output, (stacked, normal, inv_std, slope))


def layer_backward(grad_output, weight, gain, saved, spacing, sessions, length):
    stacked, normal, inv_std, slope = saved
    width = weight.shape[1]
    grad_scaled = grad_output * slope
    grad_gain = jnp.sum(grad_scaled * normal, axis=0)
    grad_normal = grad_scaled * gain
    grad_before = inv_std * (
        grad_normal
        - jnp.mean(grad_normal, axis=-1, keepdims=True)
        - normal * jnp.mean(grad_normal * normal, axis=-1, keepdims=True)
    )
    grad_before = grad_before.astype(jnp.bfloat16)
    grad_weight = lax.dot_general(
        stacked, grad_before, (((0,), (0,)), ((), ())), preferred_element_type=jnp.float32
    )
    grad_taps = lax.dot_general(
        grad_before, weight, (((1,), (1,)), ((), ())), preferred_element_type=jnp.float32
    ).reshape(sessions, length, 3 * width)
    grad_input = (
        grad_taps[..., :width]
        + unshifted(grad_taps[..., width : 2 * width], spacing)
        + unshifted(grad_taps[..., 2 * width :], 2 * spacing)
    )
    return (grad_input, grad_weight, grad_gain)


def to_owners(grad_rows, slot_place, shards, slot_count, width):
    outgoing = (
        jnp.zeros((shards * slot_count, width), jnp.bfloat16)
        .at[slot_place]
        .set(grad_rows)
        .reshape(shards, slot_count, width)
    )
    return lax.all_to_all(outgoing, "table", split_axis=0, concat_axis=0, tiled=True)


def padded_plan(shard_of, offsets, table, weight_one, gain_one, weight_two, gain_two, grad_out):
    sessions, length, _ = shard_of.shape
    width = table.shape[2]
    rows_dev = table.shape[1]
    item_count = sessions * length
    shards = lax.axis_size("table")
    groups = lax.axis_size("dp")
    quarter = width // groups
    slot_count = 8 * ((6 * item_count + 8 * shards - 1) // (8 * shards))
    target = shard_of.reshape(-1)
    table_pick = jnp.tile(jnp.arange(3, dtype=jnp.int32), item_count)
    row_codes = table_pick * rows_dev + offsets.reshape(-1)
    onehot = (jnp.arange(shards, dtype=jnp.int32)[:, None] == target[None, :]).astype(jnp.int32)
    before = jnp.cumsum(onehot, axis=1) - onehot
    slot_rank = jnp.sum(before * onehot, axis=0)
    slot_place = target * slot_count + slot_rank
    requests = (
        jnp.full((shards * slot_count,), -1, jnp.int32)
        .at[slot_place]
        .set(row_codes)
        .reshape(shards, slot_count)
    )
    table_flat = table.reshape(3 * rows_dev, width)
    asked_rows = lax.all_to_all(requests, "table", split_axis=0, concat_axis=0, tiled=True)
    found_rows = jnp.take(table_flat, jnp.maximum(asked_rows, 0), axis=0)
    found_rows = jnp.where((asked_rows >= 0)[..., None], found_rows, jnp.zeros((), jnp.bfloat16))
    sent_back = lax.all_to_all(found_rows, "table", split_axis=0, concat_axis=0, tiled=True)
    picked = jnp.take(sent_back.reshape(shards * slot_count, width), slot_place, axis=0).reshape(
        item_count, 3, width
    )
    embedded = (
        jnp.sum(picked.astype(jnp.float32), axis=1)
        .astype(jnp.bfloat16)
        .reshape(sessions, length, width)
    )
    act_one, saved_one = layer_forward(embedded, weight_one, gain_one, 1)
    hidden = act_one.astype(jnp.bfloat16).reshape(sessions, length, width)
    act_two, saved_two = layer_forward(hidden, weight_two, gain_two, 2)
    block_out = (
        (embedded.reshape(item_count, width).astype(jnp.float32) + act_two)
        .astype(jnp.bfloat16)
        .reshape(sessions, length, width)
    )
    grad_top = grad_out.reshape(item_count, width).astype(jnp.float32)
    scale = 1.0 / math.sqrt(item_count * groups * shards)
    grad_hidden, second_weights, second_gains = layer_backward(
        grad_top, weight_two, gain_two, saved_two, 2, sessions, length
    )
    grad_inner, first_weights, first_gains = layer_backward(
        grad_hidden.reshape(item_count, width), weight_one, gain_one, saved_one, 1, sessions, length
    )
    grad_embed = (grad_top + grad_inner.reshape(item_count, width)).astype(jnp.bfloat16)
    repeated = jnp.repeat(grad_embed, 3, axis=0)
    arrived = to_owners(repeated, slot_place, shards, slot_count, width)
    dense_grad = (
        jnp.zeros((3 * rows_dev, width), jnp.float32)
        .at[jnp.maximum(asked_rows, 0).reshape(-1)]
        .add(arrived.reshape(-1, width).astype(jnp.float32))
    )
    table_grad = lax.psum_scatter(
        dense_grad.astype(jnp.bfloat16), "dp", scatter_dimension=1, tiled=True
    ).astype(jnp.float32)
    table_grad = table_grad.reshape(3, rows_dev, quarter)
    totals = lax.psum((first_weights, second_weights, first_gains, second_gains), ("dp", "table"))
    return (
        block_out,
        totals[0] * scale,
        totals[1] * scale,
        totals[2] * scale,
        totals[3] * scale,
        table_grad,
    )


VMEM = pl.BlockSpec(memory_space=pltpu.VMEM)


def columns_fit(items_shape, table_shape, groups, shards):
    sessions, length, _ = items_shape
    _, rows_dev, width = table_shape
    run = 2 * length
    return (
        2 * width == groups * LANES
        and groups > 1
        and (groups & (groups - 1)) == 0
        and sessions % 4 == 0
        and sessions <= 16
        and run % 16 == 0
        and (groups * sessions * length // 2) % (4 * UNROLL) == 0
        and rows_dev % 32 == 0
        and 4 * shards * rows_dev * LANES * 4 <= 40 * MIB
        and table_shape[0] == 3
        and shards == 8
    )


def low_lanes(rows):
    return lax.broadcasted_iota(jnp.int32, (rows, LANES), 1) < LANES // 2


def swap_halves(values):
    return pltpu.roll(values, LANES // 2, 1)


def own_columns(at, table):
    tables, rows_dev, _ = table.shape
    half = rows_dev // 2

    def kernel(at_ref, table_ref, first_ref, last_ref, all_ref):
        odd = at_ref[0] % 2 == 1
        low = low_lanes(half)
        for t in range(tables):
            top = table_ref[t, :half, :].astype(jnp.float32)
            bottom = table_ref[t, half:, :].astype(jnp.float32)
            in_low = jnp.where(odd, swap_halves(top), top)
            in_high = jnp.where(odd, bottom, swap_halves(bottom))
            values = jnp.where(low, in_low, in_high).astype(jnp.bfloat16)
            if t < tables - 1:
                first_ref[t] = values
            else:
                last_ref[0] = values
            all_ref[t] = values

    def whole(count):
        return pl.BlockSpec((count, half, LANES), lambda i, m: (0, 0, 0))

    return pl.pallas_call(
        kernel,
        grid_spec=pltpu.PrefetchScalarGridSpec(
            num_scalar_prefetch=1,
            grid=(1,),
            in_specs=[pl.BlockSpec((tables, rows_dev, LANES), lambda i, m: (0, 0, m[0] // 2))],
            out_specs=[whole(tables - 1), whole(1), whole(tables)],
        ),
        out_shape=[
            jax.ShapeDtypeStruct((count, half, LANES), jnp.bfloat16)
            for count in (tables - 1, 1, tables)
        ],
        compiler_params=pltpu.CompilerParams(vmem_limit_bytes=24 * MIB),
        name="own_columns",
    )(at, table)


def look_up(codes, slots, total, last):
    count = codes[0].shape[0]
    half = slots[0][0].shape[1]

    def kernel(low_ref, high_ref, *refs):
        slot_refs, refs = refs[: len(slots)], refs[len(slots) :]
        total_ref = None if total is None else refs[0]
        out_ref, rows, found = refs[-3:]
        for s, slot_ref in enumerate(slot_refs):
            values = slot_ref[0].astype(jnp.float32)
            rows[pl.ds(2 * s * half, half), :] = values
            rows[pl.ds((2 * s + 1) * half, half), :] = swap_halves(values)
        low = low_lanes(1)

        def some(step, carry):
            for j in range(2 * UNROLL):
                i = step * 2 * UNROLL + j
                for_low = rows[pl.ds(low_ref[i], 1), :]
                for_high = rows[pl.ds(high_ref[i], 1), :]
                found[pl.ds(i, 1), :] = jnp.where(low, for_low, for_high)
            return carry

        lax.fori_loop(0, count // (2 * UNROLL), some, 0)
        result = found[...]
        if total_ref is not None:
            result = result + total_ref[...]
        out_ref[...] = result.astype(out_ref.dtype)

    def part(at):
        return pl.BlockSpec((1, half, LANES), lambda i, *codes: (at, 0, 0))

    operands = [slot[0] for slot in slots] + ([] if total is None else [total])
    whole = pl.BlockSpec((count, LANES), lambda i, *codes: (0, 0))
    return pl.pallas_call(
        kernel,
        grid_spec=pltpu.PrefetchScalarGridSpec(
            num_scalar_prefetch=2,
            grid=(1,),
            in_specs=[part(slot[1]) for slot in slots] + ([] if total is None else [whole]),
            out_specs=whole,
            scratch_shapes=[
                pltpu.VMEM((2 * len(slots) * half, LANES), jnp.float32),
                pltpu.VMEM((count, LANES), jnp.float32),
            ],
        ),
        out_shape=jax.ShapeDtypeStruct((count, LANES), jnp.bfloat16 if last else jnp.float32),
        compiler_params=pltpu.CompilerParams(vmem_limit_bytes=20 * MIB),
        cost_estimate=pl.CostEstimate(
            flops=0, bytes_accessed=8 * 3 * count * LANES * 4, transcendentals=0
        ),
        name="look_up",
    )(*codes, *operands)


def add_rows(codes, blocks, shards, half, chains):
    tables = len(codes)
    count = codes[0][0].shape[0]
    per = blocks[0].shape[0]
    planes = shards // 2

    def kernel(*refs):
        code_refs, refs = refs[: 2 * tables], refs[2 * tables :]
        block_refs, refs = refs[: len(blocks)], refs[len(blocks) :]
        out_refs, values, refs = refs[: 2 * tables], refs[2 * tables], refs[2 * tables + 1 :]
        sums = [refs[t * chains : (t + 1) * chains] for t in range(tables)]
        for k, block_ref in enumerate(block_refs):
            values[pl.ds(k * per, per), :] = block_ref[...].astype(jnp.float32)
        for part in refs:
            part[...] = jnp.zeros_like(part)
        low = low_lanes(1)
        high = jnp.logical_not(low)

        def some(step, carry):
            for j in range(UNROLL):
                ready = []
                for c in range(chains):
                    i = c * (count // chains) + step * UNROLL + j
                    value = values[pl.ds(i, 1), :]
                    for t in range(tables):
                        part = sums[t][c]
                        to_low, to_high = pl.ds(code_refs[2 * t][i], 1), pl.ds(code_refs[2 * t + 1][i], 1)
                        ready.append(
                            (part, to_low, part[to_low, :] + value, to_high, part[to_high, :] + value)
                        )
                for part, to_low, in_low, to_high, in_high in ready:
                    pltpu.store(part.at[to_low, :], in_low, mask=low)
                    pltpu.store(part.at[to_high, :], in_high, mask=high)
            return carry

        lax.fori_loop(0, count // (chains * UNROLL), some, 0)
        for t in range(tables):
            for s in range(shards):
                straight = sum(part[pl.ds(2 * s * half, half), :] for part in sums[t])
                crossed = sum(part[pl.ds((2 * s + 1) * half, half), :] for part in sums[t])
                result = (straight + swap_halves(crossed)).astype(jnp.bfloat16)
                out_refs[2 * t + s // planes][s % planes] = result

    results = pl.pallas_call(
        kernel,
        grid_spec=pltpu.PrefetchScalarGridSpec(
            num_scalar_prefetch=2 * tables,
            grid=(),
            in_specs=[VMEM] * len(blocks),
            out_specs=[VMEM] * (2 * tables),
            scratch_shapes=[pltpu.VMEM((count, LANES), jnp.float32)]
            + [pltpu.VMEM((2 * shards * half, LANES), jnp.float32)] * (tables * chains),
        ),
        out_shape=[jax.ShapeDtypeStruct((planes, half, LANES), jnp.bfloat16)] * (2 * tables),
        compiler_params=pltpu.CompilerParams(vmem_limit_bytes=42 * MIB),
        cost_estimate=pl.CostEstimate(
            flops=0, bytes_accessed=tables * 40 * MIB, transcendentals=0
        ),
        name="add_rows",
    )(*[part for pair in codes for part in pair], *blocks)
    return list(zip(results[::2], results[1::2]))


def finished(parts, begin, tables, earlier):
    _, half, lanes = parts[0][0].shape
    count = len(parts)

    def kernel(*refs):
        refs, out_ref = refs[:-1], refs[-1]
        for t in range(count):
            total = sum(ref[...].reshape(half, lanes).astype(jnp.float32) for ref in refs[4 * t : 4 * t + 4])
            turned = total.T
            out_ref[t, :, :half] = turned[: lanes // 2]
            out_ref[t, :, half:] = turned[lanes // 2 :]

    own = pl.BlockSpec((1, half, lanes), lambda i: (0, 0, 0))

    def row_block(n):
        return pl.BlockSpec((half, lanes), lambda i: (n, 0))

    operands, specs = [], []
    for near, got, down, d, last, n in parts:
        operands += [near, got, down, last]
        specs += [own, own, row_block(d), row_block(n)]
    if earlier is not None:
        operands.append(earlier)
        specs.append(pl.BlockSpec(memory_space=pl.ANY))
    return pl.pallas_call(
        kernel,
        grid=(1,),
        in_specs=specs,
        out_specs=pl.BlockSpec((count, lanes // 2, 2 * half), lambda i: (begin // count, 0, 0)),
        out_shape=jax.ShapeDtypeStruct((tables, lanes // 2, 2 * half), jnp.float32),
        input_output_aliases={} if earlier is None else {len(operands) - 1: 0},
        compiler_params=pltpu.CompilerParams(vmem_limit_bytes=32 * MIB),
        name="finished",
    )(*operands)


def weight_chunk(tall, groups):
    return -(-(2 * tall + 16) // (32 * groups)) * 16


def scaled_sums(at, near, far, tall, width, scale):
    groups = near.shape[0]
    chunk = near.shape[1] * LANES // width

    def kernel(at_ref, near_ref, far_ref, one_ref, two_ref, gain_one_ref, gain_two_ref, flat):
        me, core = at_ref[0], at_ref[1]
        for k in range(groups):
            for part_ref, side in ((near_ref, core), (far_ref, 1 - core)):
                begin = pl.multiple_of((side * groups + (me ^ k)) * chunk, 16)
                for n in range(width // LANES):
                    values = part_ref[k, n * chunk : (n + 1) * chunk, :].astype(jnp.float32)
                    flat[pl.ds(begin, chunk), n * LANES : (n + 1) * LANES] = values * scale
        one_ref[...] = flat[:tall, :]
        two_ref[...] = flat[tall : 2 * tall, :]
        gain_one_ref[...] = flat[2 * tall : 2 * tall + 1, :]
        gain_two_ref[...] = flat[2 * tall + 1 : 2 * tall + 2, :]

    return pl.pallas_call(
        kernel,
        grid_spec=pltpu.PrefetchScalarGridSpec(
            num_scalar_prefetch=1,
            grid=(),
            in_specs=[VMEM] * 2,
            out_specs=[VMEM] * 4,
            scratch_shapes=[pltpu.VMEM((2 * groups * chunk, width), jnp.float32)],
        ),
        out_shape=[jax.ShapeDtypeStruct((tall, width), jnp.float32)] * 2
        + [jax.ShapeDtypeStruct((1, width), jnp.float32)] * 2,
        compiler_params=pltpu.CompilerParams(vmem_limit_bytes=16 * MIB),
        name="scaled_sums",
    )(at, near, far)


def both_layers(me, blocks, weight_one, gain_one, weight_two, gain_two, grad_out, length):
    groups = len(blocks)
    items, width = grad_out.shape
    run = 2 * length
    steps = items // (2 * run)
    tall = weight_one.shape[0]
    chunk = weight_chunk(tall, groups)

    def kernel(me_ref, *refs):
        block_refs, refs = refs[:groups], refs[groups:]
        w_one_ref, g_one_ref, w_two_ref, g_two_ref, top_ref, out_ref, *refs = refs
        grad_refs, refs = refs[:groups], refs[groups:]
        kept_ref, given_ref, held, packed, sum_one, sum_two, sum_gains, flat, turned_one, turned_two = refs
        me_at, core = me_ref[0], me_ref[1]
        low = low_lanes(run)
        place = lax.broadcasted_iota(jnp.int32, (run, width), 0)
        place = jnp.where(place >= length, place - length, place)

        sum_one[...] = jnp.zeros_like(sum_one)
        sum_two[...] = jnp.zeros_like(sum_two)
        sum_gains[...] = jnp.zeros_like(sum_gains)
        for weight_ref, turned_ref in ((w_one_ref, turned_one), (w_two_ref, turned_two)):
            for k in range(tall // width):
                at = slice(k * width, (k + 1) * width)
                turned_ref[at, :] = weight_ref[at, :].T

        def taps(values, gap):
            one = jnp.where(place >= gap, pltpu.roll(values, gap, 0), 0.0)
            two = jnp.where(place >= 2 * gap, pltpu.roll(values, 2 * gap, 0), 0.0)
            return jnp.concatenate([x.astype(jnp.bfloat16) for x in (values, one, two)], axis=1)

        def untaps(values, gap):
            one = jnp.where(place < length - gap, pltpu.roll(values, run - gap, 0), 0.0)
            two = jnp.where(place < length - 2 * gap, pltpu.roll(values, run - 2 * gap, 0), 0.0)
            return [x.astype(jnp.bfloat16) for x in (values, one, two)]

        def activate(before, gain):
            centred = before - jnp.mean(before, axis=-1, keepdims=True)
            inv_std = lax.rsqrt(jnp.mean(centred * centred, axis=-1, keepdims=True) + 1e-05)
            normal = centred * inv_std
            inputs = normal * gain
            square = inputs * inputs
            part = 0.5 + 0.5 * jnp.tanh(inputs * (GELU_C + GELU_C * GELU_K * square))
            slope = part + inputs * (part - part * part) * (
                2.0 * GELU_C + 6.0 * GELU_C * GELU_K * square
            )
            return normal, inv_std, inputs * part, slope

        def unwind(grad, normal, inv_std, slope, gain, row):
            scaled = grad * slope
            sum_gains[row] += jnp.sum((scaled * normal).reshape(-1, 8, width), axis=0)
            back = scaled * gain
            before = inv_std * (
                back
                - jnp.mean(back, axis=-1, keepdims=True)
                - normal * jnp.mean(back * normal, axis=-1, keepdims=True)
            )
            return before.astype(jnp.bfloat16).astype(jnp.float32)

        def products(before, values, turned_ref, gap, total):
            stacked = jnp.concatenate(untaps(before, gap), axis=1)
            total[...] += lax.dot_general(
                values.astype(jnp.bfloat16),
                stacked,
                (((0,), (0,)), ((), ())),
                preferred_element_type=jnp.float32,
            )
            return jnp.dot(stacked, turned_ref[...], preferred_element_type=jnp.float32)

        for k in range(groups):
            held[k] = block_refs[k][...].astype(jnp.float32)
        gain_one_at, gain_two_at = g_one_ref[...], g_two_ref[...]
        back_to = [None] * (2 * steps)

        def one_part(n):
            side, packed_rows = n % 2, pl.ds(n // 2 * run, run)
            columns = []
            for q in range(0, groups, 2):
                left = held[q ^ me_at, packed_rows, :]
                right = held[(q + 1) ^ me_at, packed_rows, :]
                if side == 0:
                    columns.append(jnp.where(low, left, swap_halves(right)))
                else:
                    columns.append(jnp.where(low, swap_halves(left), right))
            embedded = jnp.concatenate(columns, axis=1)
            rows = pl.ds(n * run, run)
            top = top_ref[rows, :].astype(jnp.float32)
            stacked = taps(embedded, 1)
            yield
            before = jnp.dot(stacked, w_one_ref[...], preferred_element_type=jnp.float32)
            yield

            def first(before):
                normal, inv_std, output, slope = activate(before, gain_one_at)
                return normal, inv_std, output.astype(jnp.bfloat16).astype(jnp.float32), slope

            normal, inv_std, hidden, slope = first(before)
            stacked = taps(hidden, 2)
            yield
            before = jnp.dot(stacked, w_two_ref[...], preferred_element_type=jnp.float32)
            yield

            def second(before, values, grad):
                normal, inv_std, output, slope = activate(before, gain_two_at)
                return values + output, unwind(grad, normal, inv_std, slope, gain_two_at, 1)

            output, before = second(before, embedded, top)
            out_ref[rows, :] = output.astype(jnp.bfloat16)
            yield
            grad = products(before, hidden, turned_two, 2, sum_two)
            yield

            before = unwind(grad, normal, inv_std, slope, gain_one_at, 0)
            yield
            back_to[n] = top + products(before, embedded, turned_one, 1, sum_one)
            if side == 0:
                return
            for q in range(groups):
                at = slice((q // 2) * LANES, (q // 2 + 1) * LANES)
                first, second = back_to[n - 1][:, at], back_to[n][:, at]
                if q % 2 == 0:
                    pair = jnp.where(low, first, swap_halves(second))
                else:
                    pair = jnp.where(low, swap_halves(first), second)
                packed[q ^ me_at, packed_rows, :] = pair

        waiting = [one_part(n) for n in range(2 * steps)]
        active = [waiting.pop(0)]
        next(active[0])
        while active:
            if len(active) < 2 and waiting:
                active.append(waiting.pop(0))
            for one in active[::-1]:
                if next(one, "done") == "done":
                    active.remove(one)
        for k in range(groups):
            grad_refs[k][...] = packed[k].astype(jnp.bfloat16)

        for n, total in enumerate((sum_one, sum_two)):
            for k in range(tall // width):
                flat[n * tall + k * width : n * tall + (k + 1) * width, :] = total[
                    :, k * width : (k + 1) * width
                ].astype(jnp.bfloat16)
        gains = [jnp.sum(sum_gains[n], axis=0, keepdims=True) for n in range(2)]
        flat[2 * tall : 2 * tall + 16, :] = jnp.concatenate(
            gains + [jnp.zeros((14, width), jnp.float32)], axis=0
        ).astype(jnp.bfloat16)
        if 2 * groups * chunk > 2 * tall + 16:
            flat[2 * tall + 16 :, :] = jnp.zeros(
                (2 * groups * chunk - 2 * tall - 16, width), jnp.bfloat16
            )
        for k in range(groups):
            for part_ref, side in ((kept_ref, core), (given_ref, 1 - core)):
                begin = pl.multiple_of((side * groups + (me_at ^ k)) * chunk, 16)
                part_ref[k] = flat[pl.ds(begin, chunk), :]

    def whole(shape):
        return pl.BlockSpec(shape, lambda j, m: (0, 0))

    return pl.pallas_call(
        kernel,
        grid_spec=pltpu.PrefetchScalarGridSpec(
            num_scalar_prefetch=1,
            grid=(1,),
            in_specs=[whole((items // 2, LANES))] * groups
            + [whole((tall, width)), whole((1, width))] * 2
            + [whole((items, width))],
            out_specs=[whole((items, width))]
            + [whole((items // 2, LANES))] * groups
            + [pl.BlockSpec((groups, chunk, width), lambda j, m: (0, 0, 0))] * 2,
            scratch_shapes=[
                pltpu.VMEM((groups, items // 2, LANES), jnp.float32),
                pltpu.VMEM((groups, items // 2, LANES), jnp.float32),
                pltpu.VMEM((width, tall), jnp.float32),
                pltpu.VMEM((width, tall), jnp.float32),
                pltpu.VMEM((2, 8, width), jnp.float32),
                pltpu.VMEM((2 * groups * chunk, width), jnp.bfloat16),
                pltpu.VMEM((tall, width), jnp.bfloat16),
                pltpu.VMEM((tall, width), jnp.bfloat16),
            ],
        ),
        out_shape=[jax.ShapeDtypeStruct((items, width), jnp.bfloat16)]
        + [jax.ShapeDtypeStruct((items // 2, LANES), jnp.bfloat16)] * groups
        + [jax.ShapeDtypeStruct((groups, chunk, width), jnp.bfloat16)] * 2,
        compiler_params=pltpu.CompilerParams(vmem_limit_bytes=32 * MIB),
        name="both_layers",
    )(
        me,
        *blocks,
        weight_one,
        gain_one.reshape(1, width),
        weight_two,
        gain_two.reshape(1, width),
        grad_out,
    )


def together(*values):
    return lax.optimization_barrier(values)


def after(values, *first):
    return lax.optimization_barrier((values, *first))[0]


def column_plan(shard_of, offsets, table, weight_one, gain_one, weight_two, gain_two, grad_out):
    sessions, length, _ = shard_of.shape
    tables, rows_dev, width = table.shape
    items = sessions * length
    groups = lax.axis_size("dp")
    shards = lax.axis_size("table")
    planes = shards // 2
    half = rows_dev // 2
    run = 2 * length
    me = lax.axis_index("dp")
    plane, core = lax.axis_index("table") // 2, lax.axis_index("table") % 2
    at = jnp.stack([me, core]).astype(jnp.int32)

    def dp_flip(values, k):
        return lax.ppermute(values, "dp", [(i, i ^ k) for i in range(groups)])

    def table_shift(values, k):
        return lax.ppermute(values, "table", [(i, (i + k) % shards) for i in range(shards)])

    def up(values):
        return table_shift(values, 2)

    def down(values):
        return table_shift(values, -2)

    def across(values):
        return lax.ppermute(values, "table", [(i, i ^ 1) for i in range(shards)])

    slot = (shard_of + core) % 2 * planes + (shard_of // 2 - plane + planes) % planes
    places = jnp.stack(
        [slot * rows_dev + offsets, slot * rows_dev + (offsets + half) % rows_dev], axis=0
    ).astype(jnp.int32)
    places = places.reshape(2, items // (2 * run), 2, run, tables)
    mine = jnp.stack([places[0, :, 0], places[1, :, 1]], axis=0)
    mine = jnp.transpose(mine, (3, 0, 1, 2)).reshape(tables, 2, items // 2)

    first, last, own = own_columns(at, table)
    all_codes = mine
    for k in range((groups - 1).bit_length()):
        all_codes = jnp.concatenate([all_codes, dp_flip(all_codes, 2**k)], axis=2)
    codes = [(all_codes[t, 0], all_codes[t, 1]) for t in range(tables)]

    def from_planes(own, first=None):
        near = [None] * planes
        rising = falling = own
        for k in range(1, planes // 2 + 1):
            if first is not None and k == planes // 2:
                rising = after(rising, first)
            near[planes - k] = rising = up(rising)
            if k <= (planes - 1) // 2:
                near[k] = falling = down(falling)
        return near[1:]

    near_first = from_planes(first)
    swapped = across(after(own, all_codes))
    far_first = [across(values) for values in near_first]
    last = after(last, swapped, far_first[0], far_first[-1])

    def slots(t, near, far, place):
        return [(own, t), *((v, place) for v in near), (swapped, t), *((v, place) for v in far)]

    total = look_up(codes[0], slots(0, near_first, far_first, 0), None, False)
    near_last = from_planes(last, total)
    for t in range(1, tables - 1):
        total = look_up(codes[t], slots(t, near_first, far_first, t), total, False)
    far_last = [across(after(values, total)) for values in near_last]
    total = look_up(codes[tables - 1], slots(tables - 1, near_last, far_last, 0), total, True)

    pieces = total.reshape(groups, items // 2, LANES)
    arrived = [pieces[0]] + [dp_flip(pieces[k], k) for k in range(1, groups)]
    done = both_layers(
        at, arrived, weight_one, gain_one, weight_two, gain_two, grad_out.reshape(items, width), length
    )
    block_out = done[0].reshape(sessions, length, width)
    sent, kept, given = done[1 : 1 + groups], done[1 + groups], done[2 + groups]
    blocks = [sent[0]] + [dp_flip(sent[k], k) for k in range(1, groups)]

    def add_up(parts):
        return sum(part.astype(jnp.float32) for part in parts)

    got = across(given)
    chunks = [kept[k].astype(jnp.float32) + got[k].astype(jnp.float32) for k in range(groups)]
    chunks = [chunks[0]] + [chunk.astype(jnp.bfloat16) for chunk in chunks[1:]]
    blocks = [after(block, *chunks) for block in blocks]
    chunks = [chunks[0]] + [dp_flip(chunk, k) for k, chunk in enumerate(chunks[1:], 1)]

    def side(near, got, r):
        return near[r].astype(jnp.float32) + got[r].astype(jnp.float32)

    def packed(*values):
        return jnp.concatenate([value.astype(jnp.bfloat16) for value in values], axis=0)

    ((near_2, far_2),) = add_rows(codes[2:], blocks, shards, half, 4)
    far_2, *chunks = together(far_2, *chunks)
    chunk = add_up(chunks)
    chunk = packed(*(chunk[:, n : n + LANES] for n in range(0, width, LANES)))
    got_2 = across(far_2)
    going = [packed(side(near_2, got_2, 2), chunk), packed(side(near_2, got_2, 3), chunk)]
    came = [up(going[0]), down(going[1])]
    blocks = [after(block, *going) for block in blocks]
    (near_0, far_0), (near_1, far_1) = add_rows(codes[:2], blocks, shards, half, 2)
    far_0, far_1, up_2, down_2 = together(far_0, far_1, *came)
    opposite = up(up_2[half:])
    got_0 = across(far_0)
    got_1 = across(far_1)
    chunk = (add_up([chunk, opposite]) + add_up([up_2[half:], down_2[half:]])).astype(jnp.bfloat16)
    going = packed(
        side(near_2, got_2, 1) + up_2[:half].astype(jnp.float32), side(near_0, got_0, 2), side(near_1, got_1, 2)
    )
    up_01, down_01, *chunks = together(
        up(after(going, chunk)),
        down(packed(side(near_0, got_0, 3), side(near_1, got_1, 3))),
        *(dp_flip(chunk, k) for k in range(1, groups)),
    )
    near = jnp.stack([chunk, *chunks], axis=0)
    going = packed(
        side(near_0, got_0, 1) + up_01[half : 2 * half].astype(jnp.float32),
        side(near_1, got_1, 1) + up_01[2 * half :].astype(jnp.float32),
    )
    last_01, far = up(going), across(near)
    sums = scaled_sums(at, near, far, weight_one.shape[0], width, 1.0 / math.sqrt(items * groups * shards))

    near_2 = after(near_2, *sums)
    grads = finished([(near_2, got_2, down_2, 0, up_01, 0)], 2, tables, None)
    last_01, grads = together(last_01, grads)
    grads = finished(
        [(near_0, got_0, down_01, 0, last_01, 0), (near_1, got_1, down_01, 1, last_01, 1)], 0, tables, grads
    )
    table_grad = jnp.transpose(grads, (0, 2, 1))
    return (block_out, sums[0], sums[1], sums[2].reshape(width), sums[3].reshape(width), table_grad)


def solution(mesh):
    placed = (
        P(("dp", "table"), None, None),
        P(("dp", "table"), None, None),
        P(None, "table", None),
        P(),
        P(),
        P(),
        P(),
        P(("dp", "table"), None, None),
    )

    def on_device(shard_of, offsets, table, *rest):
        fits = columns_fit(shard_of.shape, table.shape, mesh.shape["dp"], mesh.shape["table"])
        plan = column_plan if fits else padded_plan
        return plan(shard_of, offsets, table, *rest)

    return jax.shard_map(
        on_device,
        mesh=mesh,
        in_specs=placed,
        out_specs=(P(("dp", "table"), None, None), P(), P(), P(), P(), P(None, "table", "dp")),
        check_vma=False,
    )
```

```python
import math

import jax
import jax.numpy as jnp
from jax import lax
from jax.experimental import pallas as pl
from jax.experimental.pallas import tpu as pltpu
from jax.sharding import PartitionSpec as P

GELU_C = 0.7978845608028654
GELU_K = 0.044715
LANES = 128
MIB = 2**20

UNROLL = 25


def shifted(values, spacing):
    return jnp.pad(values, ((0, 0), (spacing, 0), (0, 0)))[:, : values.shape[1], :]


def unshifted(values, spacing):
    return jnp.pad(values, ((0, 0), (0, spacing), (0, 0)))[:, spacing:, :]


def stack_taps(values, spacing):
    return jnp.concatenate(
        [values, shifted(values, spacing), shifted(values, 2 * spacing)], axis=-1
    )


def gelu_parts(inputs):
    inner = GELU_C * (inputs + GELU_K * inputs * inputs * inputs)
    tangent = jnp.tanh(inner)
    output = 0.5 * inputs * (1.0 + tangent)
    slope = 0.5 * (1.0 + tangent) + 0.5 * inputs * (1.0 - tangent * tangent) * GELU_C * (
        1.0 + 3.0 * GELU_K * inputs * inputs
    )
    return (output, slope)


def layer_forward(values, weight, gain, spacing):
    sessions, length, width = values.shape
    stacked = stack_taps(values, spacing).reshape(sessions * length, 3 * width)
    before_norm = jnp.dot(stacked, weight, preferred_element_type=jnp.float32)
    centred = before_norm - jnp.mean(before_norm, axis=-1, keepdims=True)
    inv_std = lax.rsqrt(jnp.mean(centred * centred, axis=-1, keepdims=True) + 1e-05)
    normal = centred * inv_std
    output, slope = gelu_parts(normal * gain)
    return (output, (stacked, normal, inv_std, slope))


def layer_backward(grad_output, weight, gain, saved, spacing, sessions, length):
    stacked, normal, inv_std, slope = saved
    width = weight.shape[1]
    grad_scaled = grad_output * slope
    grad_gain = jnp.sum(grad_scaled * normal, axis=0)
    grad_normal = grad_scaled * gain
    grad_before = inv_std * (
        grad_normal
        - jnp.mean(grad_normal, axis=-1, keepdims=True)
        - normal * jnp.mean(grad_normal * normal, axis=-1, keepdims=True)
    )
    grad_before = grad_before.astype(jnp.bfloat16)
    grad_weight = lax.dot_general(
        stacked, grad_before, (((0,), (0,)), ((), ())), preferred_element_type=jnp.float32
    )
    grad_taps = lax.dot_general(
        grad_before, weight, (((1,), (1,)), ((), ())), preferred_element_type=jnp.float32
    ).reshape(sessions, length, 3 * width)
    grad_input = (
        grad_taps[..., :width]
        + unshifted(grad_taps[..., width : 2 * width], spacing)
        + unshifted(grad_taps[..., 2 * width :], 2 * spacing)
    )
    return (grad_input, grad_weight, grad_gain)


def to_owners(grad_rows, slot_place, shards, slot_count, width):
    outgoing = (
        jnp.zeros((shards * slot_count, width), jnp.bfloat16)
        .at[slot_place]
        .set(grad_rows)
        .reshape(shards, slot_count, width)
    )
    return lax.all_to_all(outgoing, "table", split_axis=0, concat_axis=0, tiled=True)


def padded_plan(shard_of, offsets, table, weight_one, gain_one, weight_two, gain_two, grad_out):
    sessions, length, _ = shard_of.shape
    width = table.shape[2]
    rows_dev = table.shape[1]
    item_count = sessions * length
    shards = lax.axis_size("table")
    groups = lax.axis_size("dp")
    quarter = width // groups
    slot_count = 8 * ((6 * item_count + 8 * shards - 1) // (8 * shards))
    target = shard_of.reshape(-1)
    table_pick = jnp.tile(jnp.arange(3, dtype=jnp.int32), item_count)
    row_codes = table_pick * rows_dev + offsets.reshape(-1)
    onehot = (jnp.arange(shards, dtype=jnp.int32)[:, None] == target[None, :]).astype(jnp.int32)
    before = jnp.cumsum(onehot, axis=1) - onehot
    slot_rank = jnp.sum(before * onehot, axis=0)
    slot_place = target * slot_count + slot_rank
    requests = (
        jnp.full((shards * slot_count,), -1, jnp.int32)
        .at[slot_place]
        .set(row_codes)
        .reshape(shards, slot_count)
    )
    table_flat = table.reshape(3 * rows_dev, width)
    asked_rows = lax.all_to_all(requests, "table", split_axis=0, concat_axis=0, tiled=True)
    found_rows = jnp.take(table_flat, jnp.maximum(asked_rows, 0), axis=0)
    found_rows = jnp.where((asked_rows >= 0)[..., None], found_rows, jnp.zeros((), jnp.bfloat16))
    sent_back = lax.all_to_all(found_rows, "table", split_axis=0, concat_axis=0, tiled=True)
    picked = jnp.take(sent_back.reshape(shards * slot_count, width), slot_place, axis=0).reshape(
        item_count, 3, width
    )
    embedded = (
        jnp.sum(picked.astype(jnp.float32), axis=1)
        .astype(jnp.bfloat16)
        .reshape(sessions, length, width)
    )
    act_one, saved_one = layer_forward(embedded, weight_one, gain_one, 1)
    hidden = act_one.astype(jnp.bfloat16).reshape(sessions, length, width)
    act_two, saved_two = layer_forward(hidden, weight_two, gain_two, 2)
    block_out = (
        (embedded.reshape(item_count, width).astype(jnp.float32) + act_two)
        .astype(jnp.bfloat16)
        .reshape(sessions, length, width)
    )
    grad_top = grad_out.reshape(item_count, width).astype(jnp.float32)
    scale = 1.0 / math.sqrt(item_count * groups * shards)
    grad_hidden, second_weights, second_gains = layer_backward(
        grad_top, weight_two, gain_two, saved_two, 2, sessions, length
    )
    grad_inner, first_weights, first_gains = layer_backward(
        grad_hidden.reshape(item_count, width), weight_one, gain_one, saved_one, 1, sessions, length
    )
    grad_embed = (grad_top + grad_inner.reshape(item_count, width)).astype(jnp.bfloat16)
    repeated = jnp.repeat(grad_embed, 3, axis=0)
    arrived = to_owners(repeated, slot_place, shards, slot_count, width)
    dense_grad = (
        jnp.zeros((3 * rows_dev, width), jnp.float32)
        .at[jnp.maximum(asked_rows, 0).reshape(-1)]
        .add(arrived.reshape(-1, width).astype(jnp.float32))
    )
    table_grad = lax.psum_scatter(
        dense_grad.astype(jnp.bfloat16), "dp", scatter_dimension=1, tiled=True
    ).astype(jnp.float32)
    table_grad = table_grad.reshape(3, rows_dev, quarter)
    totals = lax.psum((first_weights, second_weights, first_gains, second_gains), ("dp", "table"))
    return (
        block_out,
        totals[0] * scale,
        totals[1] * scale,
        totals[2] * scale,
        totals[3] * scale,
        table_grad,
    )


VMEM = pl.BlockSpec(memory_space=pltpu.VMEM)


def columns_fit(items_shape, table_shape, groups, shards):
    sessions, length, _ = items_shape
    _, rows_dev, width = table_shape
    run = 2 * length
    return (
        2 * width == groups * LANES
        and groups > 1
        and (groups & (groups - 1)) == 0
        and sessions % 4 == 0
        and sessions <= 16
        and run % 16 == 0
        and (groups * sessions * length // 2) % (4 * UNROLL) == 0
        and rows_dev % 32 == 0
        and 4 * shards * rows_dev * LANES * 4 <= 40 * MIB
        and table_shape[0] == 3
        and shards == 8
    )


def low_lanes(rows):
    return lax.broadcasted_iota(jnp.int32, (rows, LANES), 1) < LANES // 2


def swap_halves(values):
    return pltpu.roll(values, LANES // 2, 1)


def own_columns(at, table):
    tables, rows_dev, _ = table.shape
    half = rows_dev // 2

    def kernel(at_ref, table_ref, first_ref, last_ref, all_ref):
        odd = at_ref[0] % 2 == 1
        low = low_lanes(half)
        for t in range(tables):
            top = table_ref[t, :half, :].astype(jnp.float32)
            bottom = table_ref[t, half:, :].astype(jnp.float32)
            in_low = jnp.where(odd, swap_halves(top), top)
            in_high = jnp.where(odd, bottom, swap_halves(bottom))
            values = jnp.where(low, in_low, in_high).astype(jnp.bfloat16)
            if t < tables - 1:
                first_ref[t] = values
            else:
                last_ref[0] = values
            all_ref[t] = values

    def whole(count):
        return pl.BlockSpec((count, half, LANES), lambda i, m: (0, 0, 0))

    return pl.pallas_call(
        kernel,
        grid_spec=pltpu.PrefetchScalarGridSpec(
            num_scalar_prefetch=1,
            grid=(1,),
            in_specs=[pl.BlockSpec((tables, rows_dev, LANES), lambda i, m: (0, 0, m[0] // 2))],
            out_specs=[whole(tables - 1), whole(1), whole(tables)],
        ),
        out_shape=[
            jax.ShapeDtypeStruct((count, half, LANES), jnp.bfloat16)
            for count in (tables - 1, 1, tables)
        ],
        compiler_params=pltpu.CompilerParams(vmem_limit_bytes=24 * MIB),
        name="own_columns",
    )(at, table)


def look_up(codes, slots, total, last):
    count = codes[0].shape[0]
    half = slots[0][0].shape[1]

    def kernel(low_ref, high_ref, *refs):
        slot_refs, refs = refs[: len(slots)], refs[len(slots) :]
        total_ref = None if total is None else refs[0]
        out_ref, rows, found = refs[-3:]
        for s, slot_ref in enumerate(slot_refs):
            values = slot_ref[0].astype(jnp.float32)
            rows[pl.ds(2 * s * half, half), :] = values
            rows[pl.ds((2 * s + 1) * half, half), :] = swap_halves(values)
        low = low_lanes(1)

        def some(step, carry):
            for j in range(2 * UNROLL):
                i = step * 2 * UNROLL + j
                for_low = rows[pl.ds(low_ref[i], 1), :]
                for_high = rows[pl.ds(high_ref[i], 1), :]
                found[pl.ds(i, 1), :] = jnp.where(low, for_low, for_high)
            return carry

        lax.fori_loop(0, count // (2 * UNROLL), some, 0)
        result = found[...]
        if total_ref is not None:
            result = result + total_ref[...]
        out_ref[...] = result.astype(out_ref.dtype)

    def part(at):
        return pl.BlockSpec((1, half, LANES), lambda i, *codes: (at, 0, 0))

    operands = [slot[0] for slot in slots] + ([] if total is None else [total])
    whole = pl.BlockSpec((count, LANES), lambda i, *codes: (0, 0))
    return pl.pallas_call(
        kernel,
        grid_spec=pltpu.PrefetchScalarGridSpec(
            num_scalar_prefetch=2,
            grid=(1,),
            in_specs=[part(slot[1]) for slot in slots] + ([] if total is None else [whole]),
            out_specs=whole,
            scratch_shapes=[
                pltpu.VMEM((2 * len(slots) * half, LANES), jnp.float32),
                pltpu.VMEM((count, LANES), jnp.float32),
            ],
        ),
        out_shape=jax.ShapeDtypeStruct((count, LANES), jnp.bfloat16 if last else jnp.float32),
        compiler_params=pltpu.CompilerParams(vmem_limit_bytes=20 * MIB),
        cost_estimate=pl.CostEstimate(
            flops=0, bytes_accessed=8 * 3 * count * LANES * 4, transcendentals=0
        ),
        name="look_up",
    )(*codes, *operands)


def add_rows(codes, blocks, shards, half, chains):
    tables = len(codes)
    count = codes[0][0].shape[0]
    per = blocks[0].shape[0]
    planes = shards // 2

    def kernel(*refs):
        code_refs, refs = refs[: 2 * tables], refs[2 * tables :]
        block_refs, refs = refs[: len(blocks)], refs[len(blocks) :]
        out_refs, values, refs = refs[: 2 * tables], refs[2 * tables], refs[2 * tables + 1 :]
        sums = [refs[t * chains : (t + 1) * chains] for t in range(tables)]
        for k, block_ref in enumerate(block_refs):
            values[pl.ds(k * per, per), :] = block_ref[...].astype(jnp.float32)
        for part in refs:
            part[...] = jnp.zeros_like(part)
        low = low_lanes(1)
        high = jnp.logical_not(low)

        def some(step, carry):
            for j in range(UNROLL):
                ready = []
                for c in range(chains):
                    i = c * (count // chains) + step * UNROLL + j
                    value = values[pl.ds(i, 1), :]
                    for t in range(tables):
                        part = sums[t][c]
                        to_low, to_high = pl.ds(code_refs[2 * t][i], 1), pl.ds(code_refs[2 * t + 1][i], 1)
                        ready.append(
                            (part, to_low, part[to_low, :] + value, to_high, part[to_high, :] + value)
                        )
                for part, to_low, in_low, to_high, in_high in ready:
                    pltpu.store(part.at[to_low, :], in_low, mask=low)
                    pltpu.store(part.at[to_high, :], in_high, mask=high)
            return carry

        lax.fori_loop(0, count // (chains * UNROLL), some, 0)
        for t in range(tables):
            for s in range(shards):
                straight = sum(part[pl.ds(2 * s * half, half), :] for part in sums[t])
                crossed = sum(part[pl.ds((2 * s + 1) * half, half), :] for part in sums[t])
                result = (straight + swap_halves(crossed)).astype(jnp.bfloat16)
                out_refs[2 * t + s // planes][s % planes] = result

    results = pl.pallas_call(
        kernel,
        grid_spec=pltpu.PrefetchScalarGridSpec(
            num_scalar_prefetch=2 * tables,
            grid=(),
            in_specs=[VMEM] * len(blocks),
            out_specs=[VMEM] * (2 * tables),
            scratch_shapes=[pltpu.VMEM((count, LANES), jnp.float32)]
            + [pltpu.VMEM((2 * shards * half, LANES), jnp.float32)] * (tables * chains),
        ),
        out_shape=[jax.ShapeDtypeStruct((planes, half, LANES), jnp.bfloat16)] * (2 * tables),
        compiler_params=pltpu.CompilerParams(vmem_limit_bytes=42 * MIB),
        cost_estimate=pl.CostEstimate(
            flops=0, bytes_accessed=tables * 40 * MIB, transcendentals=0
        ),
        name="add_rows",
    )(*[part for pair in codes for part in pair], *blocks)
    return list(zip(results[::2], results[1::2]))


def finished(parts, begin, tables, earlier):
    _, half, lanes = parts[0][0].shape
    count = len(parts)

    def kernel(*refs):
        refs, out_ref = refs[:-1], refs[-1]
        for t in range(count):
            total = sum(ref[...].reshape(half, lanes).astype(jnp.float32) for ref in refs[4 * t : 4 * t + 4])
            turned = total.T
            out_ref[t, :, :half] = turned[: lanes // 2]
            out_ref[t, :, half:] = turned[lanes // 2 :]

    own = pl.BlockSpec((1, half, lanes), lambda i: (0, 0, 0))

    def row_block(n):
        return pl.BlockSpec((half, lanes), lambda i: (n, 0))

    operands, specs = [], []
    for near, got, down, d, last, n in parts:
        operands += [near, got, down, last]
        specs += [own, own, row_block(d), row_block(n)]
    if earlier is not None:
        operands.append(earlier)
        specs.append(pl.BlockSpec(memory_space=pl.ANY))
    return pl.pallas_call(
        kernel,
        grid=(1,),
        in_specs=specs,
        out_specs=pl.BlockSpec((count, lanes // 2, 2 * half), lambda i: (begin // count, 0, 0)),
        out_shape=jax.ShapeDtypeStruct((tables, lanes // 2, 2 * half), jnp.float32),
        input_output_aliases={} if earlier is None else {len(operands) - 1: 0},
        compiler_params=pltpu.CompilerParams(vmem_limit_bytes=32 * MIB),
        name="finished",
    )(*operands)


def weight_chunk(tall, groups):
    return -(-(2 * tall + 16) // (32 * groups)) * 16


def scaled_sums(at, near, far, tall, width, scale):
    groups = near.shape[0]
    chunk = near.shape[1] * LANES // width

    def kernel(at_ref, near_ref, far_ref, one_ref, two_ref, gain_one_ref, gain_two_ref, flat):
        me, core = at_ref[0], at_ref[1]
        for k in range(groups):
            for part_ref, side in ((near_ref, core), (far_ref, 1 - core)):
                begin = pl.multiple_of((side * groups + (me ^ k)) * chunk, 16)
                for n in range(width // LANES):
                    values = part_ref[k, n * chunk : (n + 1) * chunk, :].astype(jnp.float32)
                    flat[pl.ds(begin, chunk), n * LANES : (n + 1) * LANES] = values * scale
        one_ref[...] = flat[:tall, :]
        two_ref[...] = flat[tall : 2 * tall, :]
        gain_one_ref[...] = flat[2 * tall : 2 * tall + 1, :]
        gain_two_ref[...] = flat[2 * tall + 1 : 2 * tall + 2, :]

    return pl.pallas_call(
        kernel,
        grid_spec=pltpu.PrefetchScalarGridSpec(
            num_scalar_prefetch=1,
            grid=(),
            in_specs=[VMEM] * 2,
            out_specs=[VMEM] * 4,
            scratch_shapes=[pltpu.VMEM((2 * groups * chunk, width), jnp.float32)],
        ),
        out_shape=[jax.ShapeDtypeStruct((tall, width), jnp.float32)] * 2
        + [jax.ShapeDtypeStruct((1, width), jnp.float32)] * 2,
        compiler_params=pltpu.CompilerParams(vmem_limit_bytes=16 * MIB),
        name="scaled_sums",
    )(at, near, far)


def both_layers(me, blocks, weight_one, gain_one, weight_two, gain_two, grad_out, length):
    groups = len(blocks)
    items, width = grad_out.shape
    run = 2 * length
    steps = items // (2 * run)
    tall = weight_one.shape[0]
    chunk = weight_chunk(tall, groups)

    def kernel(me_ref, *refs):
        block_refs, refs = refs[:groups], refs[groups:]
        w_one_ref, g_one_ref, w_two_ref, g_two_ref, top_ref, out_ref, *refs = refs
        grad_refs, refs = refs[:groups], refs[groups:]
        kept_ref, given_ref, held, packed, sum_one, sum_two, sum_gains, flat, turned_one, turned_two = refs
        me_at, core = me_ref[0], me_ref[1]
        low = low_lanes(run)
        place = lax.broadcasted_iota(jnp.int32, (run, width), 0)
        place = jnp.where(place >= length, place - length, place)

        sum_one[...] = jnp.zeros_like(sum_one)
        sum_two[...] = jnp.zeros_like(sum_two)
        sum_gains[...] = jnp.zeros_like(sum_gains)
        for weight_ref, turned_ref in ((w_one_ref, turned_one), (w_two_ref, turned_two)):
            for k in range(tall // width):
                at = slice(k * width, (k + 1) * width)
                turned_ref[at, :] = weight_ref[at, :].T

        def taps(values, gap):
            one = jnp.where(place >= gap, pltpu.roll(values, gap, 0), 0.0)
            two = jnp.where(place >= 2 * gap, pltpu.roll(values, 2 * gap, 0), 0.0)
            return jnp.concatenate([x.astype(jnp.bfloat16) for x in (values, one, two)], axis=1)

        def untaps(values, gap):
            one = jnp.where(place < length - gap, pltpu.roll(values, run - gap, 0), 0.0)
            two = jnp.where(place < length - 2 * gap, pltpu.roll(values, run - 2 * gap, 0), 0.0)
            return [x.astype(jnp.bfloat16) for x in (values, one, two)]

        def activate(before, gain):
            centred = before - jnp.mean(before, axis=-1, keepdims=True)
            inv_std = lax.rsqrt(jnp.mean(centred * centred, axis=-1, keepdims=True) + 1e-05)
            normal = centred * inv_std
            inputs = normal * gain
            square = inputs * inputs
            part = 0.5 + 0.5 * jnp.tanh(inputs * (GELU_C + GELU_C * GELU_K * square))
            slope = part + inputs * (part - part * part) * (
                2.0 * GELU_C + 6.0 * GELU_C * GELU_K * square
            )
            return normal, inv_std, inputs * part, slope

        def unwind(grad, normal, inv_std, slope, gain, row):
            scaled = grad * slope
            sum_gains[row] += jnp.sum((scaled * normal).reshape(-1, 8, width), axis=0)
            back = scaled * gain
            before = inv_std * (
                back
                - jnp.mean(back, axis=-1, keepdims=True)
                - normal * jnp.mean(back * normal, axis=-1, keepdims=True)
            )
            return before.astype(jnp.bfloat16).astype(jnp.float32)

        def products(before, values, turned_ref, gap, total):
            stacked = jnp.concatenate(untaps(before, gap), axis=1)
            total[...] += lax.dot_general(
                values.astype(jnp.bfloat16),
                stacked,
                (((0,), (0,)), ((), ())),
                preferred_element_type=jnp.float32,
            )
            return jnp.dot(stacked, turned_ref[...], preferred_element_type=jnp.float32)

        for k in range(groups):
            held[k] = block_refs[k][...].astype(jnp.float32)
        gain_one_at, gain_two_at = g_one_ref[...], g_two_ref[...]
        back_to = [None] * (2 * steps)

        def one_part(n):
            side, packed_rows = n % 2, pl.ds(n // 2 * run, run)
            columns = []
            for q in range(0, groups, 2):
                left = held[q ^ me_at, packed_rows, :]
                right = held[(q + 1) ^ me_at, packed_rows, :]
                if side == 0:
                    columns.append(jnp.where(low, left, swap_halves(right)))
                else:
                    columns.append(jnp.where(low, swap_halves(left), right))
            embedded = jnp.concatenate(columns, axis=1)
            rows = pl.ds(n * run, run)
            top = top_ref[rows, :].astype(jnp.float32)
            stacked = taps(embedded, 1)
            yield
            before = jnp.dot(stacked, w_one_ref[...], preferred_element_type=jnp.float32)
            yield

            def first(before):
                normal, inv_std, output, slope = activate(before, gain_one_at)
                return normal, inv_std, output.astype(jnp.bfloat16).astype(jnp.float32), slope

            normal, inv_std, hidden, slope = first(before)
            stacked = taps(hidden, 2)
            yield
            before = jnp.dot(stacked, w_two_ref[...], preferred_element_type=jnp.float32)
            yield

            def second(before, values, grad):
                normal, inv_std, output, slope = activate(before, gain_two_at)
                return values + output, unwind(grad, normal, inv_std, slope, gain_two_at, 1)

            output, before = second(before, embedded, top)
            out_ref[rows, :] = output.astype(jnp.bfloat16)
            yield
            grad = products(before, hidden, turned_two, 2, sum_two)
            yield

            before = unwind(grad, normal, inv_std, slope, gain_one_at, 0)
            yield
            back_to[n] = top + products(before, embedded, turned_one, 1, sum_one)
            if side == 0:
                return
            for q in range(groups):
                at = slice((q // 2) * LANES, (q // 2 + 1) * LANES)
                first, second = back_to[n - 1][:, at], back_to[n][:, at]
                if q % 2 == 0:
                    pair = jnp.where(low, first, swap_halves(second))
                else:
                    pair = jnp.where(low, swap_halves(first), second)
                packed[q ^ me_at, packed_rows, :] = pair

        waiting = [one_part(n) for n in range(2 * steps)]
        active = [waiting.pop(0)]
        next(active[0])
        while active:
            if len(active) < 2 and waiting:
                active.append(waiting.pop(0))
            for one in list(active):
                if next(one, "done") == "done":
                    active.remove(one)
        for k in range(groups):
            grad_refs[k][...] = packed[k].astype(jnp.bfloat16)

        for n, total in enumerate((sum_one, sum_two)):
            for k in range(tall // width):
                flat[n * tall + k * width : n * tall + (k + 1) * width, :] = total[
                    :, k * width : (k + 1) * width
                ].astype(jnp.bfloat16)
        gains = [jnp.sum(sum_gains[n], axis=0, keepdims=True) for n in range(2)]
        flat[2 * tall : 2 * tall + 16, :] = jnp.concatenate(
            gains + [jnp.zeros((14, width), jnp.float32)], axis=0
        ).astype(jnp.bfloat16)
        if 2 * groups * chunk > 2 * tall + 16:
            flat[2 * tall + 16 :, :] = jnp.zeros(
                (2 * groups * chunk - 2 * tall - 16, width), jnp.bfloat16
            )
        for k in range(groups):
            for part_ref, side in ((kept_ref, core), (given_ref, 1 - core)):
                begin = pl.multiple_of((side * groups + (me_at ^ k)) * chunk, 16)
                part_ref[k] = flat[pl.ds(begin, chunk), :]

    def whole(shape):
        return pl.BlockSpec(shape, lambda j, m: (0, 0))

    return pl.pallas_call(
        kernel,
        grid_spec=pltpu.PrefetchScalarGridSpec(
            num_scalar_prefetch=1,
            grid=(1,),
            in_specs=[whole((items // 2, LANES))] * groups
            + [whole((tall, width)), whole((1, width))] * 2
            + [whole((items, width))],
            out_specs=[whole((items, width))]
            + [whole((items // 2, LANES))] * groups
            + [pl.BlockSpec((groups, chunk, width), lambda j, m: (0, 0, 0))] * 2,
            scratch_shapes=[
                pltpu.VMEM((groups, items // 2, LANES), jnp.float32),
                pltpu.VMEM((groups, items // 2, LANES), jnp.float32),
                pltpu.VMEM((width, tall), jnp.float32),
                pltpu.VMEM((width, tall), jnp.float32),
                pltpu.VMEM((2, 8, width), jnp.float32),
                pltpu.VMEM((2 * groups * chunk, width), jnp.bfloat16),
                pltpu.VMEM((tall, width), jnp.bfloat16),
                pltpu.VMEM((tall, width), jnp.bfloat16),
            ],
        ),
        out_shape=[jax.ShapeDtypeStruct((items, width), jnp.bfloat16)]
        + [jax.ShapeDtypeStruct((items // 2, LANES), jnp.bfloat16)] * groups
        + [jax.ShapeDtypeStruct((groups, chunk, width), jnp.bfloat16)] * 2,
        compiler_params=pltpu.CompilerParams(vmem_limit_bytes=32 * MIB),
        name="both_layers",
    )(
        me,
        *blocks,
        weight_one,
        gain_one.reshape(1, width),
        weight_two,
        gain_two.reshape(1, width),
        grad_out,
    )


def together(*values):
    return lax.optimization_barrier(values)


def after(values, *first):
    return lax.optimization_barrier((values, *first))[0]


def column_plan(shard_of, offsets, table, weight_one, gain_one, weight_two, gain_two, grad_out):
    sessions, length, _ = shard_of.shape
    tables, rows_dev, width = table.shape
    items = sessions * length
    groups = lax.axis_size("dp")
    shards = lax.axis_size("table")
    planes = shards // 2
    half = rows_dev // 2
    run = 2 * length
    me = lax.axis_index("dp")
    plane, core = lax.axis_index("table") // 2, lax.axis_index("table") % 2
    at = jnp.stack([me, core]).astype(jnp.int32)

    def dp_flip(values, k):
        return lax.ppermute(values, "dp", [(i, i ^ k) for i in range(groups)])

    def table_shift(values, k):
        return lax.ppermute(values, "table", [(i, (i + k) % shards) for i in range(shards)])

    def up(values):
        return table_shift(values, 2)

    def down(values):
        return table_shift(values, -2)

    def across(values):
        return lax.ppermute(values, "table", [(i, i ^ 1) for i in range(shards)])

    slot = (shard_of + core) % 2 * planes + (shard_of // 2 - plane + planes) % planes
    places = jnp.stack(
        [slot * rows_dev + offsets, slot * rows_dev + (offsets + half) % rows_dev], axis=0
    ).astype(jnp.int32)
    places = places.reshape(2, items // (2 * run), 2, run, tables)
    mine = jnp.stack([places[0, :, 0], places[1, :, 1]], axis=0)
    mine = jnp.transpose(mine, (3, 0, 1, 2)).reshape(tables, 2, items // 2)

    first, last, own = own_columns(at, table)
    all_codes = mine
    for k in range((groups - 1).bit_length()):
        all_codes = jnp.concatenate([all_codes, dp_flip(all_codes, 2**k)], axis=2)
    codes = [(all_codes[t, 0], all_codes[t, 1]) for t in range(tables)]

    def from_planes(own, first=None):
        near = [None] * planes
        rising = falling = own
        for k in range(1, planes // 2 + 1):
            if first is not None and k == planes // 2:
                rising = after(rising, first)
            near[planes - k] = rising = up(rising)
            if k <= (planes - 1) // 2:
                near[k] = falling = down(falling)
        return near[1:]

    near_first = from_planes(first)
    swapped = across(after(own, all_codes))
    far_first = [across(values) for values in near_first]
    last = after(last, swapped, far_first[0], far_first[-1])

    def slots(t, near, far, place):
        return [(own, t), *((v, place) for v in near), (swapped, t), *((v, place) for v in far)]

    total = look_up(codes[0], slots(0, near_first, far_first, 0), None, False)
    near_last = from_planes(last, total)
    for t in range(1, tables - 1):
        total = look_up(codes[t], slots(t, near_first, far_first, t), total, False)
    far_last = [across(after(values, total)) for values in near_last]
    total = look_up(codes[tables - 1], slots(tables - 1, near_last, far_last, 0), total, True)

    pieces = total.reshape(groups, items // 2, LANES)
    arrived = [pieces[0]] + [dp_flip(pieces[k], k) for k in range(1, groups)]
    done = both_layers(
        at, arrived, weight_one, gain_one, weight_two, gain_two, grad_out.reshape(items, width), length
    )
    block_out = done[0].reshape(sessions, length, width)
    sent, kept, given = done[1 : 1 + groups], done[1 + groups], done[2 + groups]
    blocks = [sent[0]] + [dp_flip(sent[k], k) for k in range(1, groups)]

    def add_up(parts):
        return sum(part.astype(jnp.float32) for part in parts)

    got = across(given)
    chunks = [kept[k].astype(jnp.float32) + got[k].astype(jnp.float32) for k in range(groups)]
    chunks = [chunks[0]] + [chunk.astype(jnp.bfloat16) for chunk in chunks[1:]]
    blocks = [after(block, *chunks) for block in blocks]
    chunks = [chunks[0]] + [dp_flip(chunk, k) for k, chunk in enumerate(chunks[1:], 1)]

    def side(near, got, r):
        return near[r].astype(jnp.float32) + got[r].astype(jnp.float32)

    def packed(*values):
        return jnp.concatenate([value.astype(jnp.bfloat16) for value in values], axis=0)

    ((near_2, far_2),) = add_rows(codes[2:], blocks, shards, half, 4)
    far_2, *chunks = together(far_2, *chunks)
    chunk = add_up(chunks)
    chunk = packed(*(chunk[:, n : n + LANES] for n in range(0, width, LANES)))
    got_2 = across(far_2)
    going = [packed(side(near_2, got_2, 2), chunk), packed(side(near_2, got_2, 3), chunk)]
    came = [up(going[0]), down(going[1])]
    blocks = [after(block, *going) for block in blocks]
    (near_0, far_0), (near_1, far_1) = add_rows(codes[:2], blocks, shards, half, 2)
    far_0, far_1, up_2, down_2 = together(far_0, far_1, *came)
    opposite = up(up_2[half:])
    got_0 = across(far_0)
    got_1 = across(far_1)
    chunk = (add_up([chunk, opposite]) + add_up([up_2[half:], down_2[half:]])).astype(jnp.bfloat16)
    going = packed(
        side(near_2, got_2, 1) + up_2[:half].astype(jnp.float32), side(near_0, got_0, 2), side(near_1, got_1, 2)
    )
    up_01, down_01, *chunks = together(
        up(after(going, chunk)),
        down(packed(side(near_0, got_0, 3), side(near_1, got_1, 3))),
        *(dp_flip(chunk, k) for k in range(1, groups)),
    )
    near = jnp.stack([chunk, *chunks], axis=0)
    going = packed(
        side(near_0, got_0, 1) + up_01[half : 2 * half].astype(jnp.float32),
        side(near_1, got_1, 1) + up_01[2 * half :].astype(jnp.float32),
    )
    last_01, far = up(going), across(near)
    sums = scaled_sums(at, near, far, weight_one.shape[0], width, 1.0 / math.sqrt(items * groups * shards))

    near_2 = after(near_2, *sums)
    grads = finished([(near_2, got_2, down_2, 0, up_01, 0)], 2, tables, None)
    last_01, grads = together(last_01, grads)
    grads = finished(
        [(near_0, got_0, down_01, 0, last_01, 0), (near_1, got_1, down_01, 1, last_01, 1)], 0, tables, grads
    )
    table_grad = jnp.transpose(grads, (0, 2, 1))
    return (block_out, sums[0], sums[1], sums[2].reshape(width), sums[3].reshape(width), table_grad)


def solution(mesh):
    placed = (
        P(("dp", "table"), None, None),
        P(("dp", "table"), None, None),
        P(None, "table", None),
        P(),
        P(),
        P(),
        P(),
        P(("dp", "table"), None, None),
    )

    def on_device(shard_of, offsets, table, *rest):
        fits = columns_fit(shard_of.shape, table.shape, mesh.shape["dp"], mesh.shape["table"])
        plan = column_plan if fits else padded_plan
        return plan(shard_of, offsets, table, *rest)

    return jax.shard_map(
        on_device,
        mesh=mesh,
        in_specs=placed,
        out_specs=(P(("dp", "table"), None, None), P(), P(), P(), P(), P(None, "table", "dp")),
        check_vma=False,
    )
```
